128 devices in a mesh: wide: 16 (over y, x), narrow: 8 (over z, core).
Axes of the slice: x: 4, y: 4, z: 4, core: 2. Of those that a mesh axis runs over, the one named last changes fastest.
Arguments:
- initial: float32 [2, 512, 256, 128], P(None, 'wide', 'narrow'), may hold values from 0.5 to 2
- images: float32 [2, 4, 48, 48, 128], P(None, None, 'wide', 'narrow'), may hold values from 20 to 200
- blocks: bfloat16 [4, 8, 128, 128], replicated, may hold values from 0 to 0.03125
- lib_index: int32 [4, 512, 256], P(None, 'wide', 'narrow'), may hold values from 0 to 7
- tile_map: int32 [4, 512, 256], P(None, 'wide', 'narrow'), may hold values from 0 to 305
- win_x: int32 [16, 8, 4], P('wide', 'narrow'), may hold values from 0 to 31
- win_y: int32 [16, 8, 4], P('wide', 'narrow'), may hold values from 0 to 31
- win_z: int32 [16, 8, 4], P('wide', 'narrow'), may hold values from 0 to 64
Outputs:
- volume: float32 [2, 512, 256, 128], P(None, 'wide', 'narrow')
- correlation: float32 [16, 8, 4, 4096], P('wide', 'narrow')
The draws below stay inside these ranges and needn't reach their ends.
All inputs are finite; a program needn't handle non-finite values.
Results may differ from the reference program's by a relative error of at most 0.00062.
Values may be sent and summed in bfloat16 or wider, within the bound.
A program may use at most 128 MiB of HBM per device.

```python
import math
import jax
import jax.numpy as jnp
from jax import lax

CAMS = 4
NLIB = 8
PT = 128
DEPTH = 128
BX = 32
BY = 32
WIN = 64
DISP = 16
SWEEPS = 2
TPR = 3
TPC = 6
WIN_DEV = 4
REACH = 8
BRICKS_X = 16
BRICKS_Y = 8
NX = 512
NY = 256
TROWS = 48
TCOLS = 48
N_WIDE = 16
N_NARROW = 8


def draw_blocks(key, part):
    shape = (CAMS, NLIB, PT, DEPTH)
    uniform_part = jax.random.uniform(key, shape, jnp.float32)
    camera_ids = lax.broadcasted_iota(jnp.int32, shape, 0)
    member_ids = lax.broadcasted_iota(jnp.int32, shape, 1)
    pixel_ids = lax.broadcasted_iota(jnp.int32, shape, 2)
    voxel_ids = lax.broadcasted_iota(jnp.int32, shape, 3)
    offset = voxel_ids * PT // DEPTH + member_ids * (PT // NLIB) + camera_ids * (PT // (2 * CAMS))
    band = (pixel_ids - offset) % PT < PT // 2
    return jnp.where(band, uniform_part * (4.0 / PT), 0.0).astype(jnp.bfloat16)


def place_ends(result, rng, least, largest):
    longest = result.shape.index(max(result.shape))
    spots = []
    for shift in (0, 1):
        where = [jax.random.randint(jax.random.fold_in(rng, axis), (), 0, length) for axis, length in enumerate(result.shape)]
        where[longest] = (where[longest] + shift) % result.shape[longest]
        spots.append(tuple(where))
    return result.at[spots[0]].set(least).at[spots[1]].set(largest)


def steps_of(stream_key, extent, split, low, largest):
    level = 1.0
    for dim, parts in split:
        draws = jax.random.uniform(jax.random.fold_in(jax.random.fold_in(stream_key, 6), dim), (parts,), jnp.float32, low / len(split), largest / len(split))
        level = level * jnp.repeat(jnp.exp(draws), extent[dim] // parts).reshape((-1,) + (1,) * (len(extent) - 1 - dim))
    return level


def setup_inputs(seed: int = 0) -> dict:
    key_of = jax.random.split(jax.random.key(seed), 9)
    initial = jnp.clip(jnp.exp(math.log(2.0) - 1.3862944 * jax.random.uniform(key_of[0], (2, NX, NY, DEPTH), jnp.float32) ** steps_of(key_of[0], (2, NX, NY, DEPTH), ((1, 16), (2, 8)), -0.2, 0.2)), 0.5, 2.0)
    images = jnp.clip(jnp.exp(math.log(200.0) - 2.3025851 * jax.random.uniform(key_of[1], (2, CAMS, TROWS, TCOLS, PT), jnp.float32) ** steps_of(key_of[1], (2, CAMS, TROWS, TCOLS, PT), ((2, 16), (3, 8)), -0.2, 0.2)), 20.0, 200.0)
    blocks = draw_blocks(jax.random.fold_in(key_of[8], 71), 0)
    lib_index = place_ends(jax.random.randint(key_of[3], (CAMS, NX, NY), 0, NLIB), jax.random.fold_in(key_of[3], 1), 0, NLIB - 1).astype(jnp.int32)
    tile_map = place_ends(jax.random.randint(key_of[4], (CAMS, NX, NY), 0, (2 * REACH + 1) * TPR * TPC), jax.random.fold_in(key_of[4], 1), 0, ((2 * REACH + 1) * TPR * TPC) - 1).astype(jnp.int32)
    win_x = place_ends(jax.random.randint(key_of[5], (BRICKS_X, BRICKS_Y, WIN_DEV), 0, BX), jax.random.fold_in(key_of[5], 1), 0, BX - 1).astype(jnp.int32)
    win_y = place_ends(jax.random.randint(key_of[6], (BRICKS_X, BRICKS_Y, WIN_DEV), 0, BY), jax.random.fold_in(key_of[6], 1), 0, BY - 1).astype(jnp.int32)
    win_z = place_ends(jax.random.randint(key_of[7], (BRICKS_X, BRICKS_Y, WIN_DEV), 0, DEPTH - WIN + 1), jax.random.fold_in(key_of[7], 1), 0, DEPTH - WIN).astype(jnp.int32)
    return {"initial": initial, "images": images, "blocks": blocks, "lib_index": lib_index, "tile_map": tile_map, "win_x": win_x, "win_y": win_y, "win_z": win_z}


def column_tiles(rel):
    tile_count = TPR * TPC
    brick_row = (jnp.arange(NX, dtype=jnp.int32) // BX)[:, None]
    brick_col = (jnp.arange(NY, dtype=jnp.int32) // BY)[None, :]
    strip = brick_row - REACH + rel // tile_count
    within = rel % tile_count
    flat = (strip * TPR + within // TPC) * TCOLS + brick_col * TPC + within % TPC
    valid = (strip >= 0) & (strip < N_WIDE)
    return jnp.where(valid, flat, TROWS * TCOLS).astype(jnp.int32)

def reference(initial, images, blocks, lib_index, tile_map, win_x, win_y, win_z):
    volume = initial.astype(jnp.float32)
    tiles_total = TROWS * TCOLS
    logs = jnp.log(images + 1.0).reshape(2, CAMS, tiles_total, PT)
    for sweep_index in range(SWEEPS):
        for camera in range(CAMS):
            target = column_tiles(tile_map[camera]).reshape(-1)
            chosen = lib_index[camera]
            rounded = lax.optimization_barrier(volume.astype(jnp.bfloat16)).astype(jnp.float32)
            column_proj = jnp.zeros((2, NX, NY, PT), jnp.float32)
            for member in range(NLIB):
                weights = blocks[camera, member].astype(jnp.float32)
                product = jnp.einsum('exyk,pk->exyp', rounded, weights)
                column_proj = column_proj + jnp.where((chosen == member)[None, :, :, None], product, 0.0)
            flat_proj = column_proj.reshape(2, NX * NY, PT).transpose(1, 0, 2)
            summed = jax.ops.segment_sum(flat_proj, target, num_segments=tiles_total + 1)
            projection = summed[:tiles_total].transpose(1, 0, 2)
            log_ratio = (logs[:, camera] - jnp.log(projection + 1.0)).astype(jnp.bfloat16)
            padded_ratio = jnp.concatenate([log_ratio, jnp.zeros((2, 1, PT), jnp.bfloat16)], axis=1)
            spread = padded_ratio[:, target].reshape(2, NX, NY, PT).astype(jnp.float32)
            back_sum = jnp.zeros((2, NX, NY, DEPTH), jnp.float32)
            for member in range(NLIB):
                weights = blocks[camera, member].astype(jnp.float32)
                product = jnp.einsum('exyp,pk->exyk', spread, weights)
                back_sum = back_sum + jnp.where((chosen == member)[None, :, :, None], product, 0.0)
            volume = volume * jnp.exp(back_sum)
    half = WIN // 2
    padded = jnp.pad(volume, ((0, 0), (half, half), (half, half), (0, 0)))
    brick_x = (jnp.arange(N_WIDE, dtype=jnp.int32) * BX)[:, None, None]
    brick_y = (jnp.arange(N_NARROW, dtype=jnp.int32) * BY)[None, :, None]
    start_x = (win_x + brick_x).reshape(-1)
    start_y = (win_y + brick_y).reshape(-1)
    start_z = win_z.reshape(-1)
    starts = jnp.stack([start_x, start_y, start_z], axis=1).astype(jnp.int32)
    shifts = (jnp.arange(DISP, dtype=jnp.int32) - DISP // 2) % WIN

    def one_window(start):
        window = lax.dynamic_slice(padded, (jnp.int32(0), start[0], start[1], start[2]), (2, WIN, WIN, WIN))
        centred = window - lax.optimization_barrier(jnp.mean(window, axis=(1, 2, 3), keepdims=True))
        rms = jnp.sqrt(lax.optimization_barrier(jnp.mean(centred * centred, axis=(1, 2, 3))) + 1e-06)
        spectra = jnp.fft.fftn(centred, axes=(1, 2, 3))
        cross = jnp.conj(spectra[0]) * spectra[1]
        circular = jnp.real(jnp.fft.ifftn(cross))
        picked = circular[shifts][:, shifts][:, :, shifts]
        return (picked / (rms[0] * rms[1] * WIN ** 1.5)).reshape(-1)
    correlation = lax.map(one_window, starts).reshape(N_WIDE, N_NARROW, WIN_DEV, DISP * DISP * DISP)
    return (volume, correlation.astype(jnp.float32))
```

```python
import functools
import math

import jax
import jax.numpy as jnp
from jax import lax
from jax.experimental import pallas as pl
from jax.experimental.pallas import tpu as pltpu
from jax.sharding import PartitionSpec as P

MESH = pl.DeviceIdType.MESH
PROJ_ROWS = 24
RATIO_ROWS = 32
CHUNK = 256
WIN = 64
DISP = 16
SWEEPS = 2


def padded_2(block, sides, width):
    for axis, dim in sides:
        count = lax.axis_size(axis)
        forward = [(i, i + 1) for i in range(count - 1)]
        backward = [(target, source) for source, target in forward]
        low = lax.ppermute(
            lax.slice_in_dim(block, block.shape[dim] - width, None, axis=dim), axis, forward
        )
        high = lax.ppermute(lax.slice_in_dim(block, 0, width, axis=dim), axis, backward)
        block = jnp.concatenate([low, block, high], axis=dim)
    return block


def dft_tables():
    indices = jnp.arange(WIN, dtype=jnp.int32)
    full_angle = (
        2.0 * math.pi / WIN * (indices[:, None] * indices[None, :] % WIN).astype(jnp.float32)
    )
    shifts = (jnp.arange(DISP, dtype=jnp.int32) - DISP // 2) % WIN
    part_angle = (
        2.0 * math.pi / WIN * (indices[:, None] * shifts[None, :] % WIN).astype(jnp.float32)
    )
    return (jnp.cos(full_angle), jnp.sin(full_angle), jnp.cos(part_angle), jnp.sin(part_angle))


def turn_axis(real_part, imag_part, cosine, sine_table, form, sign):
    highest = lax.Precision.HIGHEST
    real_cos = jnp.einsum(form, real_part, cosine, precision=highest)
    real_sin = jnp.einsum(form, real_part, sine_table, precision=highest)
    imag_cos = jnp.einsum(form, imag_part, cosine, precision=highest)
    imag_sin = jnp.einsum(form, imag_part, sine_table, precision=highest)
    return (real_cos - sign * imag_sin, imag_cos + sign * real_sin)


def window_correlation(extended, start, tables):
    cosine, sine_table, cos_part, sin_part = tables
    highest = lax.Precision.HIGHEST
    window = lax.dynamic_slice(
        extended, (jnp.int32(0), start[0], start[1], start[2]), (2, WIN, WIN, WIN)
    )
    centred = window - jnp.mean(window, axis=(1, 2, 3), keepdims=True)
    rms = jnp.sqrt(jnp.mean(centred * centred, axis=(1, 2, 3)) + 1e-06)
    stacked = jnp.concatenate([cosine, -sine_table], axis=1)
    first = jnp.einsum("exyz,zk->exyk", centred, stacked, precision=highest)
    real_part = first[..., :WIN]
    imag_part = first[..., WIN:]
    real_part, imag_part = turn_axis(
        real_part, imag_part, cosine, sine_table, "exyk,yq->exqk", -1.0
    )
    real_part, imag_part = turn_axis(
        real_part, imag_part, cosine, sine_table, "exqk,xr->erqk", -1.0
    )
    cross_real = real_part[0] * real_part[1] + imag_part[0] * imag_part[1]
    cross_imag = real_part[0] * imag_part[1] - imag_part[0] * real_part[1]
    cross_real, cross_imag = turn_axis(
        cross_real, cross_imag, cos_part, sin_part, "abk,kd->abd", 1.0
    )
    cross_real, cross_imag = turn_axis(
        cross_real, cross_imag, cos_part, sin_part, "abd,bq->aqd", 1.0
    )
    final = jnp.einsum("aqd,ar->rqd", cross_real, cos_part, precision=highest)
    final = final - jnp.einsum("aqd,ar->rqd", cross_imag, sin_part, precision=highest)
    scale = 1.0 / (WIN**3 * WIN**1.5)
    return (final * scale / (rms[0] * rms[1])).reshape(-1)


def sweeps_kernel(
    init_ref, img_ref, fwd_ref, bwd_ref, lib_ref, gather_ref, spread_ref,
    vol_ref,
    cols_ref, part_ref, recv_ref, ratio_ref,
    part_send, part_recv, ratio_send, ratio_recv,
):
    count = lax.axis_size("wide")
    me = lax.axis_index("wide")
    cams, members = fwd_ref.shape[0], fwd_ref.shape[1] // 128
    columns = init_ref.shape[1]

    barrier = pltpu.get_barrier_semaphore()

    def greet(d, _):
        pl.semaphore_signal(
            barrier, inc=1, device_id={"wide": lax.rem(me + d, count)}, device_id_type=MESH
        )
        return 0

    lax.fori_loop(1, count, greet, 0)

    def masked(values, lib):
        return jnp.concatenate(
            [jnp.where(lib == m, values, jnp.zeros_like(values)) for m in range(members)], axis=1
        )

    def project_rows(e, cam, rows, vol):
        lhs = masked(vol.astype(jnp.bfloat16), lib_ref[cam, rows, :])
        proj = jnp.dot(lhs, fwd_ref[cam], preferred_element_type=jnp.float32)
        high = proj.astype(jnp.bfloat16)
        low = (proj - high.astype(jnp.float32)).astype(jnp.bfloat16)
        cols_ref[e, rows, 0:128] = high
        cols_ref[e, rows, 128:256] = low

    def part_copy(e, d):
        target = lax.rem(me + d, count)
        return pltpu.make_async_remote_copy(
            src_ref=part_ref.at[e, target],
            dst_ref=recv_ref.at[e, me],
            send_sem=part_send.at[e, d],
            recv_sem=part_recv.at[e, me],
            device_id={"wide": target},
            device_id_type=MESH,
        )

    def part_arrival(e, d):
        source = lax.rem(me + d, count)
        return pltpu.make_async_remote_copy(
            src_ref=part_ref.at[e, source],
            dst_ref=recv_ref.at[e, source],
            send_sem=part_send.at[e, d],
            recv_sem=part_recv.at[e, source],
            device_id={"wide": source},
            device_id_type=MESH,
        )

    def strip(e, owner):
        return ratio_ref.at[e, pl.ds(pl.multiple_of(owner * RATIO_ROWS, RATIO_ROWS), RATIO_ROWS)]

    def ratio_copy(e, d):
        target = lax.rem(me + d, count)
        return pltpu.make_async_remote_copy(
            src_ref=strip(e, me),
            dst_ref=strip(e, me),
            send_sem=ratio_send.at[e, d],
            recv_sem=ratio_recv.at[e, me],
            device_id={"wide": target},
            device_id_type=MESH,
        )

    def ratio_arrival(e, d):
        source = lax.rem(me + d, count)
        return pltpu.make_async_remote_copy(
            src_ref=strip(e, me),
            dst_ref=strip(e, source),
            send_sem=ratio_send.at[e, d],
            recv_sem=ratio_recv.at[e, source],
            device_id={"wide": source},
            device_id_type=MESH,
        )

    def each(action):
        def step(d, _):
            action(d)
            return 0

        lax.fori_loop(1, count, step, 0)

    def send_parts(e, cam):
        both = jnp.dot(gather_ref[cam], cols_ref[e], preferred_element_type=jnp.float32)
        total = both[:, 0:128] + both[:, 128:256]
        part_ref[e] = total.reshape(part_ref.shape[1:])
        each(lambda d: part_copy(e, d).start())

    def send_ratio(e, cam):
        def take(d, total):
            part_arrival(e, d).wait_recv()
            return total + recv_ref[e, lax.rem(me + d, count)]

        total = lax.fori_loop(1, count, take, part_ref[e, me])
        ratio = jnp.log(img_ref[e, cam] + 1.0) - jnp.log(total + 1.0)
        ratio = jnp.concatenate(
            [ratio, jnp.zeros((RATIO_ROWS - PROJ_ROWS, 128), jnp.float32)], axis=0
        )
        ratio_ref[e, pl.ds(pl.multiple_of(me * RATIO_ROWS, RATIO_ROWS), RATIO_ROWS), :] = (
            ratio.astype(jnp.bfloat16)
        )
        each(lambda d: ratio_copy(e, d).start())

    def collect_ratio(e):
        each(lambda d: ratio_arrival(e, d).wait_recv())
        each(lambda d: part_copy(e, d).wait_send())
        each(lambda d: ratio_copy(e, d).wait_send())

    def updated_rows(e, cam, rows):
        near = jnp.dot(spread_ref[cam, rows, :], ratio_ref[e], preferred_element_type=jnp.float32)
        lhs = masked(near.astype(jnp.bfloat16), lib_ref[cam, rows, :])
        back = jnp.dot(lhs, bwd_ref[cam], preferred_element_type=jnp.float32)
        return vol_ref[e, rows, :] * jnp.exp(back)

    def chunks(action):
        def step(i, _):
            action(pl.ds(pl.multiple_of(i * CHUNK, CHUNK), CHUNK))
            return 0

        lax.fori_loop(0, columns // CHUNK, step, 0, unroll=2)

    for e in range(2):
        def first(rows):
            vol = init_ref[e, rows, :]
            vol_ref[e, rows, :] = vol
            project_rows(e, 0, rows, vol)

        chunks(first)
        if e == 0:
            pl.semaphore_wait(barrier, count - 1)
        send_parts(e, 0)

    def round_step(r, _):
        cam = lax.rem(r, cams)
        following = lax.rem(r + 1, cams)
        for e in range(2):
            send_ratio(e, cam)
        for e in range(2):
            collect_ratio(e)

            def both(rows):
                vol = updated_rows(e, cam, rows)
                vol_ref[e, rows, :] = vol
                project_rows(e, following, rows, vol)

            chunks(both)
            send_parts(e, following)
        return 0

    last = SWEEPS * cams - 1
    lax.fori_loop(0, last, round_step, 0)
    for e in range(2):
        send_ratio(e, cams - 1)
    for e in range(2):
        collect_ratio(e)

        def final(rows):
            vol_ref[e, rows, :] = updated_rows(e, cams - 1, rows)

        chunks(final)


def reconstruct(initial, images, blocks, lib_index, tile_map):
    count = lax.axis_size("wide")
    own = lax.axis_index("wide")
    cams, members = blocks.shape[0], blocks.shape[1]
    columns = initial.shape[1] * initial.shape[2]
    tiles = images.shape[2] * images.shape[3]
    ids = tile_map.reshape(cams, columns)
    strips = own - count // 2 + ids // tiles
    inside = (strips >= 0) & (strips < count)
    gather_ids = jnp.where(inside, strips * PROJ_ROWS + ids % tiles, -1)
    spread_ids = jnp.where(inside, strips * RATIO_ROWS + ids % tiles, -1)
    gather = gather_ids[:, None, :] == lax.broadcasted_iota(
        jnp.int32, (cams, count * PROJ_ROWS, columns), 1
    )
    spread = spread_ids[:, :, None] == lax.broadcasted_iota(
        jnp.int32, (cams, columns, count * RATIO_ROWS), 2
    )
    lib = jnp.broadcast_to(lib_index.reshape(cams, columns, 1), (cams, columns, 128))
    backward = blocks.reshape(cams, members * 128, 128)
    forward = blocks.transpose(0, 1, 3, 2).reshape(cams, members * 128, 128)
    pictures = jnp.pad(
        images.reshape(2, cams, tiles, 128), ((0, 0), (0, 0), (0, PROJ_ROWS - tiles), (0, 0))
    )
    vmem = pl.BlockSpec(memory_space=pltpu.VMEM)
    return pl.pallas_call(
        sweeps_kernel,
        out_shape=jax.ShapeDtypeStruct((2, columns, 128), jnp.float32),
        in_specs=[vmem] * 7,
        out_specs=vmem,
        scratch_shapes=[
            pltpu.VMEM((2, columns, 256), jnp.bfloat16),
            pltpu.VMEM((2, count, PROJ_ROWS, 128), jnp.float32),
            pltpu.VMEM((2, count, PROJ_ROWS, 128), jnp.float32),
            pltpu.VMEM((2, count * RATIO_ROWS, 128), jnp.bfloat16),
            pltpu.SemaphoreType.DMA((2, count)),
            pltpu.SemaphoreType.DMA((2, count)),
            pltpu.SemaphoreType.DMA((2, count)),
            pltpu.SemaphoreType.DMA((2, count)),
        ],
        compiler_params=pltpu.CompilerParams(
            collective_id=0, has_side_effects=True, vmem_limit_bytes=48 * 1024 * 1024
        ),
        name="sweeps",
    )(
        initial.reshape(2, columns, 128),
        pictures,
        forward,
        backward,
        lib.astype(jnp.bfloat16),
        gather.astype(jnp.bfloat16),
        spread.astype(jnp.bfloat16),
    ).reshape(initial.shape)


def body(initial, images, blocks, lib_index, tile_map, win_x, win_y, win_z):
    volume = reconstruct(initial, images, blocks, lib_index, tile_map)
    extended = padded_2(volume, (("wide", 1), ("narrow", 2)), WIN // 2)
    tables = dft_tables()
    starts = jnp.stack([win_x.reshape(-1), win_y.reshape(-1), win_z.reshape(-1)], axis=1)

    def per_window(start):
        return window_correlation(extended, start, tables)

    results = lax.map(per_window, starts)
    correlation = results.reshape(1, 1, starts.shape[0], DISP * DISP * DISP)
    return (volume, correlation)


def solution(mesh):
    placed = (
        P(None, "wide", "narrow", None),
        P(None, None, "wide", "narrow", None),
        P(),
        P(None, "wide", "narrow"),
        P(None, "wide", "narrow"),
        P("wide", "narrow", None),
        P("wide", "narrow", None),
        P("wide", "narrow", None),
    )
    return jax.shard_map(
        body,
        mesh=mesh,
        in_specs=placed,
        out_specs=(P(None, "wide", "narrow", None), P("wide", "narrow", None, None)),
        check_vma=False,
    )
```

```python
import jax
import jax.numpy as jnp
import ml_dtypes
import numpy as np
from jax import lax
from jax.experimental import pallas as pl
from jax.experimental.pallas import tpu as pltpu
from jax.sharding import PartitionSpec as P

MESH = pl.DeviceIdType.MESH
PROJ_ROWS = 24
RATIO_ROWS = 32
CHUNK = 256
WIN = 64
DISP = 16
SWEEPS = 2
SPAN = 80
KEPT = 40


def padded_2(block, sides, width):
    for axis, dim in sides:
        count = lax.axis_size(axis)
        forward = [(i, i + 1) for i in range(count - 1)]
        backward = [(target, source) for source, target in forward]
        low = lax.ppermute(
            lax.slice_in_dim(block, block.shape[dim] - width, None, axis=dim), axis, forward
        )
        high = lax.ppermute(lax.slice_in_dim(block, 0, width, axis=dim), axis, backward)
        block = jnp.concatenate([low, block, high], axis=dim)
    return block


def sweeps_kernel(
    init_ref, img_ref, fwd_ref, bwd_ref, lib_ref, gather_ref, spread_ref,
    vol_ref,
    cols_ref, part_ref, recv_ref, ratio_ref,
    part_send, part_recv, ratio_send, ratio_recv,
):
    count = lax.axis_size("wide")
    me = lax.axis_index("wide")
    cams, members = fwd_ref.shape[0], fwd_ref.shape[1] // 128
    columns = init_ref.shape[1]

    barrier = pltpu.get_barrier_semaphore()

    def greet(d, _):
        pl.semaphore_signal(
            barrier, inc=1, device_id={"wide": lax.rem(me + d, count)}, device_id_type=MESH
        )
        return 0

    lax.fori_loop(1, count, greet, 0)

    def masked(values, lib):
        return jnp.concatenate(
            [jnp.where(lib == m, values, jnp.zeros_like(values)) for m in range(members)], axis=1
        )

    def project_rows(e, cam, rows, vol):
        lhs = masked(vol.astype(jnp.bfloat16), lib_ref[cam, rows, :])
        proj = jnp.dot(lhs, fwd_ref[cam], preferred_element_type=jnp.float32)
        high = proj.astype(jnp.bfloat16)
        low = (proj - high.astype(jnp.float32)).astype(jnp.bfloat16)
        cols_ref[e, rows, 0:128] = high
        cols_ref[e, rows, 128:256] = low

    def part_copy(e, d):
        target = lax.rem(me + d, count)
        return pltpu.make_async_remote_copy(
            src_ref=part_ref.at[e, target],
            dst_ref=recv_ref.at[e, me],
            send_sem=part_send.at[e, d],
            recv_sem=part_recv.at[e, me],
            device_id={"wide": target},
            device_id_type=MESH,
        )

    def part_arrival(e, d):
        source = lax.rem(me + d, count)
        return pltpu.make_async_remote_copy(
            src_ref=part_ref.at[e, source],
            dst_ref=recv_ref.at[e, source],
            send_sem=part_send.at[e, d],
            recv_sem=part_recv.at[e, source],
            device_id={"wide": source},
            device_id_type=MESH,
        )

    def strip(e, owner):
        return ratio_ref.at[e, pl.ds(pl.multiple_of(owner * RATIO_ROWS, RATIO_ROWS), RATIO_ROWS)]

    def ratio_copy(e, d):
        target = lax.rem(me + d, count)
        return pltpu.make_async_remote_copy(
            src_ref=strip(e, me),
            dst_ref=strip(e, me),
            send_sem=ratio_send.at[e, d],
            recv_sem=ratio_recv.at[e, me],
            device_id={"wide": target},
            device_id_type=MESH,
        )

    def ratio_arrival(e, d):
        source = lax.rem(me + d, count)
        return pltpu.make_async_remote_copy(
            src_ref=strip(e, me),
            dst_ref=strip(e, source),
            send_sem=ratio_send.at[e, d],
            recv_sem=ratio_recv.at[e, source],
            device_id={"wide": source},
            device_id_type=MESH,
        )

    def each(action):
        def step(d, _):
            action(d)
            return 0

        lax.fori_loop(1, count, step, 0)

    def send_parts(e, cam):
        both = jnp.dot(gather_ref[cam], cols_ref[e], preferred_element_type=jnp.float32)
        total = both[:, 0:128] + both[:, 128:256]
        part_ref[e] = total.reshape(part_ref.shape[1:])
        each(lambda d: part_copy(e, d).start())

    def send_ratio(e, cam):
        def take(d, total):
            part_arrival(e, d).wait_recv()
            return total + recv_ref[e, lax.rem(me + d, count)]

        total = lax.fori_loop(1, count, take, part_ref[e, me])
        ratio = jnp.log(img_ref[e, cam] + 1.0) - jnp.log(total + 1.0)
        ratio = jnp.concatenate(
            [ratio, jnp.zeros((RATIO_ROWS - PROJ_ROWS, 128), jnp.float32)], axis=0
        )
        ratio_ref[e, pl.ds(pl.multiple_of(me * RATIO_ROWS, RATIO_ROWS), RATIO_ROWS), :] = (
            ratio.astype(jnp.bfloat16)
        )
        each(lambda d: ratio_copy(e, d).start())

    def collect_ratio(e):
        each(lambda d: ratio_arrival(e, d).wait_recv())
        each(lambda d: part_copy(e, d).wait_send())
        each(lambda d: ratio_copy(e, d).wait_send())

    def updated_rows(e, cam, rows):
        near = jnp.dot(spread_ref[cam, rows, :], ratio_ref[e], preferred_element_type=jnp.float32)
        lhs = masked(near.astype(jnp.bfloat16), lib_ref[cam, rows, :])
        back = jnp.dot(lhs, bwd_ref[cam], preferred_element_type=jnp.float32)
        return vol_ref[e, rows, :] * jnp.exp(back)

    def chunks(action):
        def step(i, _):
            action(pl.ds(pl.multiple_of(i * CHUNK, CHUNK), CHUNK))
            return 0

        lax.fori_loop(0, columns // CHUNK, step, 0, unroll=2)

    for e in range(2):
        def first(rows):
            vol = init_ref[e, rows, :]
            vol_ref[e, rows, :] = vol
            project_rows(e, 0, rows, vol)

        chunks(first)
        if e == 0:
            pl.semaphore_wait(barrier, count - 1)
        send_parts(e, 0)

    def round_step(r, _):
        cam = lax.rem(r, cams)
        following = lax.rem(r + 1, cams)
        for e in range(2):
            send_ratio(e, cam)
        for e in range(2):
            collect_ratio(e)

            def both(rows):
                vol = updated_rows(e, cam, rows)
                vol_ref[e, rows, :] = vol
                project_rows(e, following, rows, vol)

            chunks(both)
            send_parts(e, following)
        return 0

    last = SWEEPS * cams - 1
    lax.fori_loop(0, last, round_step, 0)
    for e in range(2):
        send_ratio(e, cams - 1)
    for e in range(2):
        collect_ratio(e)

        def final(rows):
            vol_ref[e, rows, :] = updated_rows(e, cams - 1, rows)

        chunks(final)


def reconstruct(initial, images, blocks, lib_index, tile_map):
    count = lax.axis_size("wide")
    own = lax.axis_index("wide")
    cams, members = blocks.shape[0], blocks.shape[1]
    columns = initial.shape[1] * initial.shape[2]
    tiles = images.shape[2] * images.shape[3]
    ids = tile_map.reshape(cams, columns)
    strips = own - count // 2 + ids // tiles
    inside = (strips >= 0) & (strips < count)
    gather_ids = jnp.where(inside, strips * PROJ_ROWS + ids % tiles, -1)
    spread_ids = jnp.where(inside, strips * RATIO_ROWS + ids % tiles, -1)
    gather = gather_ids[:, None, :] == lax.broadcasted_iota(
        jnp.int32, (cams, count * PROJ_ROWS, columns), 1
    )
    spread = spread_ids[:, :, None] == lax.broadcasted_iota(
        jnp.int32, (cams, columns, count * RATIO_ROWS), 2
    )
    lib = jnp.broadcast_to(lib_index.reshape(cams, columns, 1), (cams, columns, 128))
    backward = blocks.reshape(cams, members * 128, 128)
    forward = blocks.transpose(0, 1, 3, 2).reshape(cams, members * 128, 128)
    pictures = jnp.pad(
        images.reshape(2, cams, tiles, 128), ((0, 0), (0, 0), (0, PROJ_ROWS - tiles), (0, 0))
    )
    vmem = pl.BlockSpec(memory_space=pltpu.VMEM)
    return pl.pallas_call(
        sweeps_kernel,
        out_shape=jax.ShapeDtypeStruct((2, columns, 128), jnp.float32),
        in_specs=[vmem] * 7,
        out_specs=vmem,
        scratch_shapes=[
            pltpu.VMEM((2, columns, 256), jnp.bfloat16),
            pltpu.VMEM((2, count, PROJ_ROWS, 128), jnp.float32),
            pltpu.VMEM((2, count, PROJ_ROWS, 128), jnp.float32),
            pltpu.VMEM((2, count * RATIO_ROWS, 128), jnp.bfloat16),
            pltpu.SemaphoreType.DMA((2, count)),
            pltpu.SemaphoreType.DMA((2, count)),
            pltpu.SemaphoreType.DMA((2, count)),
            pltpu.SemaphoreType.DMA((2, count)),
        ],
        compiler_params=pltpu.CompilerParams(
            collective_id=0, has_side_effects=True, vmem_limit_bytes=48 * 1024 * 1024
        ),
        name="sweeps",
    )(
        initial.reshape(2, columns, 128),
        pictures,
        forward,
        backward,
        lib.astype(jnp.bfloat16),
        gather.astype(jnp.bfloat16),
        spread.astype(jnp.bfloat16),
    ).reshape(initial.shape)


def split(values):
    high = values.astype(jnp.bfloat16)
    return high, (values - high.astype(jnp.float32)).astype(jnp.bfloat16)


def window_tables():
    bf16 = ml_dtypes.bfloat16
    turn = 2.0 * np.pi / WIN

    def parts(table):
        high = table.astype(bf16)
        return high, (table - high.astype(np.float64)).astype(bf16)

    waves = np.arange(WIN // 2 + 1)
    angle = turn * (waves[:, None] * np.arange(SPAN)[None, :] % WIN)
    left = np.zeros((2 * KEPT, SPAN))
    left[: len(waves)] = np.cos(angle)
    left[KEPT : KEPT + len(waves)] = -np.sin(angle)
    left_high, left_low = parts(left)
    left_table = np.zeros((2 * KEPT, 256), bf16)
    for place, table in enumerate((left_high, left_high, left_low)):
        left_table[:, place * SPAN : (place + 1) * SPAN] = table

    angle = turn * (np.arange(128)[:, None] * np.arange(WIN)[None, :] % WIN)
    cosine, sine = np.cos(angle), np.sin(angle)
    right = np.block([[cosine, -sine, -sine, cosine], [sine, cosine, cosine, sine]])
    right_table = np.stack(parts(right))

    shifts = np.arange(DISP) - DISP // 2
    weight = np.where(waves % (WIN // 2) == 0, 1.0, 2.0)
    angle = turn * shifts[:, None] * waves[None, :]
    inverse_left = np.zeros((2 * DISP, KEPT))
    inverse_left[:DISP, : len(waves)] = weight * np.cos(angle)
    inverse_left[DISP:, : len(waves)] = weight * np.sin(angle)
    angle = turn * np.arange(WIN)[:, None] * shifts[None, :]
    cosine, sine = np.cos(angle), np.sin(angle)
    inverse_right = np.zeros((512, 128))
    inverse_right[:, :DISP] = np.concatenate(
        [cosine, cosine, -sine, sine, -sine, -sine, -cosine, cosine]
    )
    row_weight = np.zeros((KEPT, 128))
    row_weight[: len(waves)] = weight[:, None]
    f32 = np.float32
    return (
        left_table, right_table,
        inverse_left.astype(f32), inverse_right.astype(f32), row_weight.astype(f32),
    )


def windows_kernel(
    place_ref, ext_ref, left_ref, right_ref, inv_left_ref, inv_right_ref, weight_ref,
    out_ref,
    high_ref, low_ref, mid_high, mid_low, spec0, spec1, corr_ref,
):
    f32 = jnp.float32
    half = DISP // 2
    wide_x = ext_ref.shape[1]
    brick = wide_x // 3

    def whole_sum(values):
        return jnp.sum(jnp.sum(values, axis=0, keepdims=True), axis=1, keepdims=True)

    for e in range(2):
        def add(x, total):
            return total + ext_ref[e, brick + x, brick : 2 * brick, :]

        total = lax.fori_loop(0, brick, add, jnp.zeros((brick, 128), f32), unroll=4)
        offset = whole_sum(total) * (1.0 / (brick * brick * 128))

        def part(x, _):
            high, low = split(ext_ref[e, x] - offset)
            high_ref[e, x] = high
            low_ref[e, x] = low
            return 0

        lax.fori_loop(0, wide_x, part, 0, unroll=2)

    def one_window(w, _):
        start_x, start_y, start_z = place_ref[0, w], place_ref[1, w], place_ref[2, w]
        from_y = pl.multiple_of(start_y // 16 * 16, 16)
        lead = start_y - from_y
        lane = lax.broadcasted_iota(jnp.int32, (2 * KEPT, 256), 1)
        spot = lax.rem(lane, SPAN)
        keep = (spot >= lead) & (spot < lead + WIN) & (lane < 3 * SPAN)
        left = jnp.where(keep, left_ref[...].astype(f32), 0.0).astype(jnp.bfloat16)
        row = lax.rem(lax.broadcasted_iota(jnp.int32, (256, 256), 0), 128)
        keep = (row >= start_z) & (row < start_z + WIN)
        right_high = jnp.where(keep, right_ref[0].astype(f32), 0.0).astype(jnp.bfloat16)
        right_low = jnp.where(keep, right_ref[1].astype(f32), 0.0).astype(jnp.bfloat16)

        def turn_y(x, _):
            rows = pl.ds(from_y, SPAN)
            sides = []
            for e in range(2):
                high = high_ref[e, start_x + x, rows, :]
                low = low_ref[e, start_x + x, rows, :]
                sides.append(jnp.concatenate([high, low, high, high[0:16]], axis=0))
            mixed = jnp.dot(left, jnp.concatenate(sides, axis=1), preferred_element_type=f32)
            high, low = split(mixed)
            for e in range(2):
                lanes = slice(e * 128, (e + 1) * 128)
                for source, target in ((high, mid_high), (low, mid_low)):
                    target[e, x, :, 0:128] = source[0:KEPT, lanes]
                    target[e, x, :, 128:256] = source[KEPT : 2 * KEPT, lanes]
            return 0

        lax.fori_loop(0, WIN, turn_y, 0, unroll=4)

        def turn_z(i, _):
            xs = pl.ds(i * 16, 16)
            for e in range(2):
                lanes = slice(0, 128 * (e + 1))
                high = mid_high[e, xs].reshape(16 * KEPT, 256)
                low = mid_low[e, xs].reshape(16 * KEPT, 256)
                value = jnp.dot(high, right_high[:, lanes], preferred_element_type=f32)
                value += jnp.dot(low, right_high[:, lanes], preferred_element_type=f32)
                value += jnp.dot(high, right_low[:, lanes], preferred_element_type=f32)
                if e == 0:
                    spec0[xs] = value.reshape(16, KEPT, 128)
                else:
                    spec1[pl.ds(i * 16 + half, 16)] = value.reshape(16, KEPT, 256)
            return 0

        lax.fori_loop(0, WIN // 16, turn_z, 0)

        def sums(x, carry):
            return carry[0] + spec0[x, 0:8, :], carry[1] + spec1[x + half, 0:8, :]

        mean0, mean1 = lax.fori_loop(
            0, WIN, sums, (jnp.zeros((8, 128), f32), jnp.zeros((8, 256), f32)), unroll=4
        )
        lane = lax.broadcasted_iota(jnp.int32, (8, 256), 1)
        row = lax.broadcasted_iota(jnp.int32, (8, 256), 0)
        mean1 = jnp.where((row == 0) & ((lane == 0) | (lane == 192)), mean1 * (1.0 / WIN), 0.0)
        mean0 = jnp.where((row == 0) & (lane == 0), mean0_wide(mean0), 0.0)[:, 0:128]

        def centre(x, carry):
            spec0[x, 0:8, :] = spec0[x, 0:8, :] - mean0
            spec1[x + half, 0:8, :] = spec1[x + half, 0:8, :] - mean1
            value0, value1 = spec0[x], spec1[x + half, :, 0:128]
            return carry[0] + value0 * value0, carry[1] + value1 * value1

        zero = jnp.zeros((KEPT, 128), f32)
        power0, power1 = lax.fori_loop(0, WIN, centre, (zero, zero), unroll=2)
        count = 1.0 / (WIN * WIN * WIN**3)
        rms0 = jnp.sqrt(whole_sum(power0 * weight_ref[...]) * count + 1e-6)
        rms1 = jnp.sqrt(whole_sum(power1 * weight_ref[...]) * count + 1e-6)
        spec1[0:half] = spec1[WIN : WIN + half]
        spec1[WIN + half : WIN + DISP] = spec1[half:DISP]

        def group(g, _):
            rows = pl.ds(pl.multiple_of(lax.rem(g, KEPT // 8) * 8, 8), 8)
            first = lax.div(g, KEPT // 8) * half

            def block(i, carry):
                carry = list(carry)
                base = i * 4
                ones = [spec0[base + j, rows, :] for j in range(4)]
                plain = [spec1[base + first + j, rows, 0:128] for j in range(half + 3)]
                swapped = [spec1[base + first + j, rows, 128:256] for j in range(half + 3)]
                for j in range(4):
                    for s in range(half):
                        carry[s] = carry[s] + ones[j] * plain[j + s]
                        carry[half + s] = carry[half + s] + ones[j] * swapped[j + s]
                return tuple(carry)

            zero = jnp.zeros((8, 128), f32)
            done = lax.fori_loop(0, WIN // 4, block, (zero,) * DISP)
            for s in range(half):
                corr_ref[first + s, rows, 0:128] = done[s]
                corr_ref[first + s, rows, 128:256] = done[half + s]
            return 0

        lax.fori_loop(0, 2 * (KEPT // 8), group, 0)

        highest = lax.Precision.HIGHEST
        turned = []
        for s in range(DISP):
            value = jnp.dot(
                inv_left_ref[...], corr_ref[s], precision=highest, preferred_element_type=f32
            )
            turned.append(jnp.concatenate([value[0:DISP], value[DISP : 2 * DISP]], axis=1))
        final = jnp.dot(
            jnp.concatenate(turned, axis=0), inv_right_ref[...],
            precision=highest, preferred_element_type=f32,
        )
        scale = 1.0 / (WIN * WIN * WIN**1.5)
        out_ref[w] = (final * (scale / (rms0 * rms1)))[:, 0:DISP]
        return 0

    lax.fori_loop(0, out_ref.shape[0], one_window, 0)


def mean0_wide(values):
    return jnp.concatenate([values, values], axis=1) * (1.0 / WIN)


def correlate(extended, win_x, win_y, win_z):
    windows = win_x.size
    places = jnp.stack([win_x.reshape(-1), win_y.reshape(-1), win_z.reshape(-1)])
    vmem = pl.BlockSpec(memory_space=pltpu.VMEM)
    bf16 = jnp.bfloat16
    shape = extended.shape
    return pl.pallas_call(
        windows_kernel,
        out_shape=jax.ShapeDtypeStruct((windows, DISP * DISP, DISP), jnp.float32),
        in_specs=[pl.BlockSpec(memory_space=pltpu.SMEM)] + [vmem] * 6,
        out_specs=vmem,
        scratch_shapes=[
            pltpu.VMEM(shape, bf16),
            pltpu.VMEM(shape, bf16),
            pltpu.VMEM((2, WIN, KEPT, 256), bf16),
            pltpu.VMEM((2, WIN, KEPT, 256), bf16),
            pltpu.VMEM((WIN, KEPT, 128), jnp.float32),
            pltpu.VMEM((WIN + DISP, KEPT, 256), jnp.float32),
            pltpu.VMEM((DISP, KEPT, 256), jnp.float32),
        ],
        compiler_params=pltpu.CompilerParams(vmem_limit_bytes=56 * 1024 * 1024),
        name="windows",
    )(places, extended, *[jnp.asarray(table) for table in window_tables()])


def body(initial, images, blocks, lib_index, tile_map, win_x, win_y, win_z):
    volume = reconstruct(initial, images, blocks, lib_index, tile_map)
    extended = padded_2(volume, (("wide", 1), ("narrow", 2)), WIN // 2)
    correlation = correlate(extended, win_x, win_y, win_z)
    return (volume, correlation.reshape(1, 1, win_x.size, DISP * DISP * DISP))


def solution(mesh):
    placed = (
        P(None, "wide", "narrow", None),
        P(None, None, "wide", "narrow", None),
        P(),
        P(None, "wide", "narrow"),
        P(None, "wide", "narrow"),
        P("wide", "narrow", None),
        P("wide", "narrow", None),
        P("wide", "narrow", None),
    )
    return jax.shard_map(
        body,
        mesh=mesh,
        in_specs=placed,
        out_specs=(P(None, "wide", "narrow", None), P("wide", "narrow", None, None)),
        check_vma=False,
    )
```

```python
import jax
import jax.numpy as jnp
import ml_dtypes
import numpy as np
from jax import lax
from jax.experimental import pallas as pl
from jax.experimental.pallas import tpu as pltpu
from jax.sharding import PartitionSpec as P

MESH = pl.DeviceIdType.MESH
PROJ_ROWS = 24
RATIO_ROWS = 32
CHUNK = 256
WIN = 64
DISP = 16
SWEEPS = 2
SPAN = 80
KEPT = 40
BRICK = 32
MARK = 16
STEPS = 65000.0


def split(values):
    high = values.astype(jnp.bfloat16)
    return high, (values - high.astype(jnp.float32)).astype(jnp.bfloat16)


def window_tables():
    bf16 = ml_dtypes.bfloat16
    turn = 2.0 * np.pi / WIN

    def parts(table):
        high = table.astype(bf16)
        return high, (table - high.astype(np.float64)).astype(bf16)

    waves = np.arange(WIN // 2 + 1)
    angle = turn * (waves[:, None] * np.arange(SPAN)[None, :] % WIN)
    left = np.zeros((2 * KEPT, SPAN))
    left[: len(waves)] = np.cos(angle)
    left[KEPT : KEPT + len(waves)] = -np.sin(angle)
    left_high, left_low = parts(left)
    left_table = np.zeros((2 * KEPT, 256), bf16)
    for place, table in enumerate((left_high, left_high, left_low)):
        left_table[:, place * SPAN : (place + 1) * SPAN] = table

    angle = turn * (np.arange(128)[:, None] * np.arange(WIN)[None, :] % WIN)
    cosine, sine = np.cos(angle), np.sin(angle)
    right = np.block([[cosine, -sine, -sine, cosine], [sine, cosine, cosine, sine]])
    right_table = np.stack(parts(right))

    shifts = np.arange(DISP) - DISP // 2
    weight = np.where(waves % (WIN // 2) == 0, 1.0, 2.0)
    angle = turn * shifts[:, None] * waves[None, :]
    inverse_left = np.zeros((2 * DISP, KEPT))
    inverse_left[:DISP, : len(waves)] = weight * np.cos(angle)
    inverse_left[DISP:, : len(waves)] = weight * np.sin(angle)
    angle = turn * np.arange(WIN)[:, None] * shifts[None, :]
    cosine, sine = np.cos(angle), np.sin(angle)
    inverse_right = np.zeros((512, 128))
    inverse_right[:, :DISP] = np.concatenate(
        [cosine, cosine, -sine, sine, -sine, -sine, -cosine, cosine]
    )
    row_weight = np.zeros((KEPT, 128))
    row_weight[: len(waves)] = weight[:, None]
    f32 = np.float32
    return (
        left_table, right_table,
        inverse_left.astype(f32), inverse_right.astype(f32), row_weight.astype(f32),
    )


def wrapped(index, count):
    return jnp.where(index >= count, index - count, index)


def whole(values, reduce):
    return reduce(reduce(values, axis=0, keepdims=True), axis=1, keepdims=True)


def chunks(rows, action, unroll):
    def step(i, carry):
        return action(pl.ds(pl.multiple_of(i * CHUNK, CHUNK), CHUNK), carry)

    return lambda init: lax.fori_loop(0, rows // CHUNK, step, init, unroll=unroll)


def reconstruct(refs, scratch, barrier_done, finish):
    init_ref, img_ref, fwd_ref, bwd_ref, lib_ref, gather_ref, spread_ref, vol_ref = refs
    cols_ref, part_ref, recv_ref, ratio_ref = scratch[:4]
    part_send, part_recv, ratio_send, ratio_recv = scratch[4:]
    f32, bf16 = jnp.float32, jnp.bfloat16
    count = lax.axis_size("wide")
    me = lax.axis_index("wide")
    cams = fwd_ref.shape[0]
    columns = init_ref.shape[1]

    def by_library(values, cam, rows, table):
        lib = lib_ref[cam, rows, :]
        zero = jnp.zeros_like(values)
        odd = (lib == 1) | (lib == 3) | (lib == 5) | (lib == 7)
        lhs = jnp.concatenate(
            [jnp.where(odd, zero, values), jnp.where(odd, values, zero)], axis=1
        )
        wide = jnp.dot(lhs, table, preferred_element_type=f32)
        pair = lib.astype(f32)
        low = jnp.where(pair < 2, wide[:, 0:128], wide[:, 128:256])
        high = jnp.where(pair < 6, wide[:, 256:384], wide[:, 384:512])
        return jnp.where(pair < 4, low, high)

    def project_rows(e, cam, rows, vol):
        proj = by_library(vol.astype(bf16), cam, rows, fwd_ref[cam])
        high, low = split(proj)
        cols_ref[e, rows, 0:128] = high
        cols_ref[e, rows, 128:256] = low

    def part_copy(e, d, owner):
        target = wrapped(me + d, count)
        return pltpu.make_async_remote_copy(
            src_ref=part_ref.at[e, target],
            dst_ref=recv_ref.at[e, owner],
            send_sem=part_send.at[e, d],
            recv_sem=part_recv.at[e, owner],
            device_id={"wide": target},
            device_id_type=MESH,
        )

    def strip(e, owner):
        return ratio_ref.at[e, pl.ds(pl.multiple_of(owner * RATIO_ROWS, RATIO_ROWS), RATIO_ROWS)]

    def ratio_copy(e, d, owner):
        return pltpu.make_async_remote_copy(
            src_ref=strip(e, me),
            dst_ref=strip(e, owner),
            send_sem=ratio_send.at[e, d],
            recv_sem=ratio_recv.at[e, owner],
            device_id={"wide": wrapped(me + d, count)},
            device_id_type=MESH,
        )

    def each(action):
        def step(d, _):
            action(d)
            return 0

        lax.fori_loop(1, count, step, 0, unroll=True)

    def send_parts(e, cam):
        both = jnp.dot(gather_ref[cam], cols_ref[e], preferred_element_type=f32)
        total = both[:, 0:128] + both[:, 128:256]
        part_ref[e] = total.reshape(part_ref.shape[1:])
        each(lambda d: part_copy(e, d, me).start())

    def send_ratio(e, cam):
        def take(d, total):
            source = wrapped(me + d, count)
            part_copy(e, d, source).wait_recv()
            return total + recv_ref[e, source]

        total = lax.fori_loop(1, count, take, part_ref[e, me], unroll=True)
        ratio = jnp.log(img_ref[e, cam] + 1.0) - jnp.log(total + 1.0)
        ratio = jnp.concatenate([ratio, jnp.zeros((RATIO_ROWS - PROJ_ROWS, 128), f32)], axis=0)
        ratio_ref[e, pl.ds(pl.multiple_of(me * RATIO_ROWS, RATIO_ROWS), RATIO_ROWS), :] = (
            ratio.astype(bf16)
        )
        each(lambda d: ratio_copy(e, d, me).start())

    def collect_ratio(e):
        each(lambda d: ratio_copy(e, d, wrapped(me + d, count)).wait_recv())
        each(lambda d: part_copy(e, d, me).wait_send())
        each(lambda d: ratio_copy(e, d, me).wait_send())

    def updated_rows(e, cam, rows):
        near = jnp.dot(spread_ref[cam, rows, :], ratio_ref[e], preferred_element_type=f32)
        back = by_library(near.astype(bf16), cam, rows, bwd_ref[cam])
        return vol_ref[e, rows, :] * jnp.exp(back)

    for e in range(2):
        def first(rows, _):
            vol = init_ref[e, rows, :]
            vol_ref[e, rows, :] = vol
            project_rows(e, 0, rows, vol)
            return 0

        chunks(columns, first, 2)(0)
        if e == 0:
            barrier_done()
        send_parts(e, 0)

    def round_step(r, _):
        cam = lax.rem(r, cams)
        following = lax.rem(r + 1, cams)
        for e in range(2):
            send_ratio(e, cam)
        for e in range(2):
            collect_ratio(e)

            def both(rows, _):
                vol = updated_rows(e, cam, rows)
                vol_ref[e, rows, :] = vol
                project_rows(e, following, rows, vol)
                return 0

            chunks(columns, both, 4)(0)
            send_parts(e, following)
        return 0

    lax.fori_loop(0, SWEEPS * cams - 1, round_step, 0)
    for e in range(2):
        send_ratio(e, cams - 1)
    for e in range(2):
        collect_ratio(e)

        def final(rows, carry):
            vol = updated_rows(e, cams - 1, rows)
            vol_ref[e, rows, :] = vol
            tiles = vol.reshape(CHUNK // 8, 8, 128)
            return (
                jnp.minimum(carry[0], jnp.min(tiles, axis=0)),
                jnp.maximum(carry[1], jnp.max(tiles, axis=0)),
                carry[2] + jnp.sum(tiles, axis=0),
            )

        low = jnp.full((8, 128), 3.0e38, f32)
        least, largest, total = chunks(columns, final, 2)((low, -low, jnp.zeros((8, 128), f32)))
        finish(e, whole(least, jnp.min), whole(largest, jnp.max), whole(total, jnp.sum))


def exchange(vol_ref, code_ref, high_ref, low_ref, send_own, send_on, arrive, stats):
    f32 = jnp.float32
    wide, narrow = lax.axis_size("wide"), lax.axis_size("narrow")
    me, row = lax.axis_index("wide"), lax.axis_index("narrow")
    columns = vol_ref.shape[1]
    has_wide = {-1: me > 0, 1: me < wide - 1}
    has_narrow = {-1: row > 0, 1: row < narrow - 1}

    def encode(e, least, largest):
        base = jnp.floor(jnp.log(least) * 64.0)
        extent = jnp.floor(jnp.log(largest) * 64.0) - base + 2.0
        scale = (64.0 * STEPS) / extent
        shift = base * (1.0 / 64.0)

        def step(rows, _):
            level = (jnp.log(vol_ref[e, rows, :]) - shift) * scale
            code_ref[1, 1, e, rows, :] = (
                jnp.round(level - STEPS / 2).astype(jnp.int32).astype(jnp.int16)
            )
            return 0

        chunks(columns, step, 1)(0)
        mark = jnp.where(lax.broadcasted_iota(jnp.int32, (MARK, 128), 0) < 8, base, extent)
        code_ref[1, 1, e, columns : columns + MARK, :] = mark.astype(jnp.int32).astype(jnp.int16)

    def side_copy(e, by, place):
        return pltpu.make_async_remote_copy(
            src_ref=code_ref.at[1, 1, e],
            dst_ref=code_ref.at[1 + place, 1, e],
            send_sem=send_own.at[0, (by + 1) // 2, e],
            recv_sem=arrive.at[1 + place, 1, e],
            device_id={"wide": me + by},
            device_id_type=MESH,
        )

    def row_copy(e, column, by, place):
        sem = send_own.at[1, (by + 1) // 2, e]
        if column != 0:
            sem = send_on.at[(column + 1) // 2, (by + 1) // 2, e]
        return pltpu.make_async_remote_copy(
            src_ref=code_ref.at[1 + column, 1, e],
            dst_ref=code_ref.at[1 + column, 1 + place, e],
            send_sem=sem,
            recv_sem=arrive.at[1 + column, 1 + place, e],
            device_id={"narrow": row + by},
            device_id_type=MESH,
        )

    def send(e):
        for by in (-1, 1):
            @pl.when(has_narrow[by])
            def _():
                row_copy(e, 0, by, -by).start()

            @pl.when(has_wide[by])
            def _():
                side_copy(e, by, -by).start()

    def pass_on(e):
        for side in (-1, 1):
            @pl.when(has_wide[side])
            def _():
                side_copy(e, side, side).wait_recv()
                for by in (-1, 1):
                    @pl.when(has_narrow[by])
                    def _():
                        row_copy(e, side, by, -by).start()

    def settle(e):
        for by in (-1, 1):
            @pl.when(has_narrow[by])
            def _():
                row_copy(e, 0, by, -by).wait_send()

            @pl.when(has_wide[by])
            def _():
                side_copy(e, by, -by).wait_send()
                for up in (-1, 1):
                    @pl.when(has_narrow[up])
                    def _():
                        row_copy(e, by, up, -up).wait_send()

    def place(e, i, j, values_of):
        def step(x, _):
            high, low = split(values_of(x))
            high_ref[e, (1 + i) * BRICK + x, (1 + j) * BRICK : (2 + j) * BRICK, :] = high
            low_ref[e, (1 + i) * BRICK + x, (1 + j) * BRICK : (2 + j) * BRICK, :] = low
            return 0

        lax.fori_loop(0, BRICK, step, 0, unroll=4)

    def place_own(e):
        place(e, 0, 0, lambda x: vol_ref[
            e, pl.ds(pl.multiple_of(x * BRICK, BRICK), BRICK), :] - stats[e])

    def place_code(e, i, j):
        mark = code_ref[1 + i, 1 + j, e, columns : columns + MARK, :].astype(f32)
        step = mark[8:9] * (1.0 / (64.0 * STEPS))
        shift = mark[0:1] * (1.0 / 64.0) + step * (STEPS / 2)

        def values_of(x):
            rows = pl.ds(pl.multiple_of(x * BRICK, BRICK), BRICK)
            code = code_ref[1 + i, 1 + j, e, rows, :].astype(f32)
            return jnp.exp(code * step + shift) - stats[e]

        place(e, i, j, values_of)

    def receive(e, i, j):
        here = has_narrow[j] if j else None
        if i:
            here = has_wide[i] if here is None else here & has_wide[i]

        @pl.when(here)
        def _():
            if j:
                row_copy(e, i, j, j).wait_recv()
            place_code(e, i, j)

        @pl.when(jnp.logical_not(here))
        def _():
            place(e, i, j, lambda x: jnp.zeros((BRICK, 128), f32) - stats[e])

    return encode, send, pass_on, settle, place_own, receive


def windows(place_ref, tables, high_ref, low_ref, mids, specs, corr_ref, out_ref):
    left_ref, right_ref, inv_left_ref, inv_right_ref, weight_ref = tables
    mid_high, mid_low = mids
    spec0, spec1 = specs
    f32, bf16 = jnp.float32, jnp.bfloat16
    half = DISP // 2
    wide_y = high_ref.shape[2]

    def transform(w, e, store):
        start_x, start_y, start_z = place_ref[0, w], place_ref[1, w], place_ref[2, w]
        lead = jnp.where(start_y >= 16, start_y - 16, start_y)
        later = lax.broadcasted_iota(jnp.int32, (SPAN, 128), 0) * 0 + start_y >= 16
        lane = lax.broadcasted_iota(jnp.int32, (2 * KEPT, 256), 1)
        spot = lax.rem(lane, SPAN)
        keep = (spot >= lead) & (spot < lead + WIN) & (lane < 3 * SPAN)
        left = jnp.where(keep, left_ref[...].astype(f32), 0.0).astype(bf16)
        wide = 128 * (e + 1)
        row = lax.rem(lax.broadcasted_iota(jnp.int32, (256, wide), 0), 128)
        keep = (row >= start_z) & (row < start_z + WIN)
        right_high = jnp.where(keep, right_ref[0, :, 0:wide].astype(f32), 0.0).astype(bf16)
        right_low = jnp.where(keep, right_ref[1, :, 0:wide].astype(f32), 0.0).astype(bf16)

        def turn_y(i, _):
            sides = []
            for j in range(2):
                high, low = high_ref[e, start_x + 2 * i + j], low_ref[e, start_x + 2 * i + j]
                high = jnp.where(later, high[wide_y - SPAN :], high[:SPAN])
                low = jnp.where(later, low[wide_y - SPAN :], low[:SPAN])
                sides.append(jnp.concatenate([high, low, high, high[0:16]], axis=0))
            mixed = jnp.dot(left, jnp.concatenate(sides, axis=1), preferred_element_type=f32)
            high, low = split(mixed)
            for j in range(2):
                lanes = slice(j * 128, (j + 1) * 128)
                for source, target in ((high, mid_high), (low, mid_low)):
                    target[2 * i + j, :, 0:128] = source[0:KEPT, lanes]
                    target[2 * i + j, :, 128:256] = source[KEPT : 2 * KEPT, lanes]
            return 0

        lax.fori_loop(0, WIN // 2, turn_y, 0, unroll=4)

        def turn_z(i, _):
            xs = pl.ds(i * 16, 16)
            high = mid_high[xs].reshape(16 * KEPT, 256)
            low = mid_low[xs].reshape(16 * KEPT, 256)
            value = jnp.dot(high, right_high, preferred_element_type=f32)
            value += jnp.dot(low, right_high, preferred_element_type=f32)
            value += jnp.dot(high, right_low, preferred_element_type=f32)
            store(i * 16, value.reshape(16, KEPT, wide))
            return 0

        lax.fori_loop(0, WIN // 16, turn_z, 0)

    def first(w, _):
        def store(x, value):
            spec0[w, pl.ds(x, 16)] = value

        transform(w, 0, store)
        return 0

    def second(w, _):
        def store(x, value):
            spec1[pl.ds(x + half, 16)] = value

        transform(w, 1, store)

        def sums(x, carry):
            return carry[0] + spec0[w, x, 0:8, :], carry[1] + spec1[x + half, 0:8, :]

        mean0, mean1 = lax.fori_loop(
            0, WIN, sums, (jnp.zeros((8, 128), f32), jnp.zeros((8, 256), f32)), unroll=4
        )
        lane = lax.broadcasted_iota(jnp.int32, (8, 256), 1)
        row = lax.broadcasted_iota(jnp.int32, (8, 256), 0)
        mean1 = jnp.where((row == 0) & ((lane == 0) | (lane == 192)), mean1 * (1.0 / WIN), 0.0)
        lane = lax.broadcasted_iota(jnp.int32, (8, 128), 1)
        row = lax.broadcasted_iota(jnp.int32, (8, 128), 0)
        mean0 = jnp.where((row == 0) & (lane == 0), mean0 * (1.0 / WIN), 0.0)

        def centre(x, carry):
            spec0[w, x, 0:8, :] = spec0[w, x, 0:8, :] - mean0
            spec1[x + half, 0:8, :] = spec1[x + half, 0:8, :] - mean1
            value0, value1 = spec0[w, x], spec1[x + half, :, 0:128]
            return carry[0] + value0 * value0, carry[1] + value1 * value1

        zero = jnp.zeros((KEPT, 128), f32)
        power0, power1 = lax.fori_loop(0, WIN, centre, (zero, zero), unroll=2)
        count = 1.0 / (WIN * WIN * WIN**3)
        rms0 = jnp.sqrt(whole(power0 * weight_ref[...], jnp.sum) * count + 1e-6)
        rms1 = jnp.sqrt(whole(power1 * weight_ref[...], jnp.sum) * count + 1e-6)
        spec1[0:half] = spec1[WIN : WIN + half]
        spec1[WIN + half : WIN + DISP] = spec1[half:DISP]

        def group(g, _):
            first = lax.div(g, KEPT // 8) * half
            rows = pl.ds(pl.multiple_of((g - lax.div(g, KEPT // 8) * (KEPT // 8)) * 8, 8), 8)

            def block(i, carry):
                carry = list(carry)
                base = i * 4
                ones = [spec0[w, base + j, rows, :] for j in range(4)]
                plain = [spec1[base + first + j, rows, 0:128] for j in range(half + 3)]
                swapped = [spec1[base + first + j, rows, 128:256] for j in range(half + 3)]
                for j in range(4):
                    for s in range(half):
                        carry[s] = carry[s] + ones[j] * plain[j + s]
                        carry[half + s] = carry[half + s] + ones[j] * swapped[j + s]
                return tuple(carry)

            zero = jnp.zeros((8, 128), f32)
            done = lax.fori_loop(0, WIN // 4, block, (zero,) * DISP)
            for s in range(half):
                corr_ref[first + s, rows, 0:128] = done[s]
                corr_ref[first + s, rows, 128:256] = done[half + s]
            return 0

        lax.fori_loop(0, 2 * (KEPT // 8), group, 0)

        highest = lax.Precision.HIGHEST
        turned = []
        for s in range(DISP):
            value = jnp.dot(
                inv_left_ref[...], corr_ref[s], precision=highest, preferred_element_type=f32
            )
            turned.append(jnp.concatenate([value[0:DISP], value[DISP : 2 * DISP]], axis=1))
        final = jnp.dot(
            jnp.concatenate(turned, axis=0), inv_right_ref[...],
            precision=highest, preferred_element_type=f32,
        )
        scale = 1.0 / (WIN * WIN * WIN**1.5)
        out_ref[w] = (final * (scale / (rms0 * rms1)))[:, 0:DISP]
        return 0

    return first, second


def piv_kernel(
    place_ref, init_ref, img_ref, fwd_ref, bwd_ref, lib_ref, gather_ref, spread_ref,
    left_ref, right_ref, inv_left_ref, inv_right_ref, weight_ref,
    vol_ref, out_ref,
    cols_ref, part_ref, recv_ref, ratio_ref,
    code_ref, high_ref, low_ref, mid_high, mid_low, spec0, spec1, corr_ref,
    part_send, part_recv, ratio_send, ratio_recv, send_own, send_on, arrive,
):
    count, depth = lax.axis_size("wide"), lax.axis_size("narrow")
    me, row = lax.axis_index("wide"), lax.axis_index("narrow")
    barrier = pltpu.get_barrier_semaphore()

    def greet(d, _):
        pl.semaphore_signal(
            barrier, inc=1, device_id={"wide": wrapped(me + d, count)}, device_id_type=MESH
        )
        return 0

    lax.fori_loop(1, count, greet, 0)
    for by in (1, depth - 1):
        pl.semaphore_signal(
            barrier, inc=1, device_id={"narrow": wrapped(row + by, depth)}, device_id_type=MESH
        )

    def barrier_done():
        pl.semaphore_wait(barrier, count + 1)

    stats = {}
    encode, send, pass_on, settle, place_own, receive = exchange(
        vol_ref, code_ref, high_ref, low_ref, send_own, send_on, arrive, stats
    )

    def finish(e, least, largest, total):
        stats[e] = total * (1.0 / (vol_ref.shape[1] * 128))
        encode(e, least, largest)
        send(e)

    reconstruct(
        (init_ref, img_ref, fwd_ref, bwd_ref, lib_ref, gather_ref, spread_ref, vol_ref),
        (cols_ref, part_ref, recv_ref, ratio_ref, part_send, part_recv, ratio_send, ratio_recv),
        barrier_done,
        finish,
    )
    place_own(0)
    pass_on(0)
    for i in (-1, 1):
        receive(0, i, 0)
    place_own(1)
    pass_on(1)
    for i, j in ((0, -1), (0, 1), (-1, -1), (-1, 1), (1, -1), (1, 1)):
        receive(0, i, j)
    first, second = windows(
        place_ref,
        (left_ref, right_ref, inv_left_ref, inv_right_ref, weight_ref),
        high_ref, low_ref, (mid_high, mid_low), (spec0, spec1), corr_ref, out_ref,
    )
    lax.fori_loop(0, out_ref.shape[0], first, 0)
    for i, j in ((-1, 0), (1, 0), (0, -1), (0, 1), (-1, -1), (-1, 1), (1, -1), (1, 1)):
        receive(1, i, j)
    for e in range(2):
        settle(e)
    lax.fori_loop(0, out_ref.shape[0], second, 0)


def body(initial, images, blocks, lib_index, tile_map, win_x, win_y, win_z):
    count = lax.axis_size("wide")
    own = lax.axis_index("wide")
    f32, bf16 = jnp.float32, jnp.bfloat16
    cams, members = blocks.shape[0], blocks.shape[1]
    columns = initial.shape[1] * initial.shape[2]
    tiles = images.shape[2] * images.shape[3]
    windows_count = win_x.size
    ids = tile_map.reshape(cams, columns)
    strips = own - count // 2 + ids // tiles
    inside = (strips >= 0) & (strips < count)
    gather_ids = jnp.where(inside, strips * PROJ_ROWS + ids % tiles, -1)
    spread_ids = jnp.where(inside, strips * RATIO_ROWS + ids % tiles, -1)
    gather = gather_ids[:, None, :] == lax.broadcasted_iota(
        jnp.int32, (cams, count * PROJ_ROWS, columns), 1
    )
    spread = spread_ids[:, :, None] == lax.broadcasted_iota(
        jnp.int32, (cams, columns, count * RATIO_ROWS), 2
    )
    lib = jnp.broadcast_to(lib_index.reshape(cams, columns, 1), (cams, columns, 128))
    pairs = blocks.reshape(cams, members // 2, 2, 128, 128)
    backward = pairs.transpose(0, 2, 3, 1, 4).reshape(cams, 256, members * 64)
    forward = pairs.transpose(0, 2, 4, 1, 3).reshape(cams, 256, members * 64)
    pictures = jnp.pad(
        images.reshape(2, cams, tiles, 128), ((0, 0), (0, 0), (0, PROJ_ROWS - tiles), (0, 0))
    )
    places = jnp.stack([win_x.reshape(-1), win_y.reshape(-1), win_z.reshape(-1)])
    vmem = pl.BlockSpec(memory_space=pltpu.VMEM)
    wide_x, wide_y = 3 * BRICK, 3 * BRICK
    volume, correlation = pl.pallas_call(
        piv_kernel,
        out_shape=(
            jax.ShapeDtypeStruct((2, columns, 128), f32),
            jax.ShapeDtypeStruct((windows_count, DISP * DISP, DISP), f32),
        ),
        in_specs=[pl.BlockSpec(memory_space=pltpu.SMEM)] + [vmem] * 12,
        out_specs=(vmem, vmem),
        scratch_shapes=[
            pltpu.VMEM((2, columns, 256), bf16),
            pltpu.VMEM((2, count, PROJ_ROWS, 128), f32),
            pltpu.VMEM((2, count, PROJ_ROWS, 128), f32),
            pltpu.VMEM((2, count * RATIO_ROWS, 128), bf16),
            pltpu.VMEM((3, 3, 2, columns + MARK, 128), jnp.int16),
            pltpu.VMEM((2, wide_x, wide_y, 128), bf16),
            pltpu.VMEM((2, wide_x, wide_y, 128), bf16),
            pltpu.VMEM((WIN, KEPT, 256), bf16),
            pltpu.VMEM((WIN, KEPT, 256), bf16),
            pltpu.VMEM((windows_count, WIN, KEPT, 128), f32),
            pltpu.VMEM((WIN + DISP, KEPT, 256), f32),
            pltpu.VMEM((DISP, KEPT, 256), f32),
            pltpu.SemaphoreType.DMA((2, count)),
            pltpu.SemaphoreType.DMA((2, count)),
            pltpu.SemaphoreType.DMA((2, count)),
            pltpu.SemaphoreType.DMA((2, count)),
            pltpu.SemaphoreType.DMA((2, 2, 2)),
            pltpu.SemaphoreType.DMA((2, 2, 2)),
            pltpu.SemaphoreType.DMA((3, 3, 2)),
        ],
        compiler_params=pltpu.CompilerParams(
            collective_id=0, has_side_effects=True, vmem_limit_bytes=60 * 1024 * 1024
        ),
        name="piv",
    )(
        places,
        initial.reshape(2, columns, 128),
        pictures,
        forward,
        backward,
        lib.astype(bf16),
        gather.astype(bf16),
        spread.astype(bf16),
        *[jnp.asarray(table) for table in window_tables()],
    )
    return (
        volume.reshape(initial.shape),
        correlation.reshape(1, 1, windows_count, DISP * DISP * DISP),
    )


def solution(mesh):
    placed = (
        P(None, "wide", "narrow", None),
        P(None, None, "wide", "narrow", None),
        P(),
        P(None, "wide", "narrow"),
        P(None, "wide", "narrow"),
        P("wide", "narrow", None),
        P("wide", "narrow", None),
        P("wide", "narrow", None),
    )
    return jax.shard_map(
        body,
        mesh=mesh,
        in_specs=placed,
        out_specs=(P(None, "wide", "narrow", None), P("wide", "narrow", None, None)),
        check_vma=False,
    )
```

```python
import jax
import jax.numpy as jnp
import ml_dtypes
import numpy as np
from jax import lax
from jax.experimental import pallas as pl
from jax.experimental.pallas import tpu as pltpu
from jax.sharding import PartitionSpec as P

MESH = pl.DeviceIdType.MESH
PROJ_ROWS = 24
RATIO_ROWS = 32
CHUNK = 256
WIN = 64
DISP = 16
SWEEPS = 2
SPAN = 80
KEPT = 40
BRICK = 32
MARK = 16
STEPS = 65000.0
TILES = 18


def split(values):
    high = values.astype(jnp.bfloat16)
    return high, (values - high.astype(jnp.float32)).astype(jnp.bfloat16)


def window_tables():
    bf16 = ml_dtypes.bfloat16
    turn = 2.0 * np.pi / WIN

    def parts(table):
        high = table.astype(bf16)
        return high, (table - high.astype(np.float64)).astype(bf16)

    waves = np.arange(WIN // 2 + 1)
    angle = turn * (waves[:, None] * np.arange(SPAN)[None, :] % WIN)
    left = np.zeros((2 * KEPT, SPAN))
    left[: len(waves)] = np.cos(angle)
    left[KEPT : KEPT + len(waves)] = -np.sin(angle)
    left_high, left_low = parts(left)
    left_table = np.zeros((2 * KEPT, 256), bf16)
    for place, table in enumerate((left_high, left_high, left_low)):
        left_table[:, place * SPAN : (place + 1) * SPAN] = table

    angle = turn * (np.arange(128)[:, None] * np.arange(WIN)[None, :] % WIN)
    cosine, sine = np.cos(angle), np.sin(angle)
    right = np.block([[cosine, -sine, -sine, cosine], [sine, cosine, cosine, sine]])
    right_table = np.stack(parts(right))

    shifts = np.arange(DISP) - DISP // 2
    weight = np.where(waves % (WIN // 2) == 0, 1.0, 2.0)
    angle = turn * shifts[:, None] * waves[None, :]
    inverse_left = np.zeros((2 * DISP, KEPT))
    inverse_left[:DISP, : len(waves)] = weight * np.cos(angle)
    inverse_left[DISP:, : len(waves)] = weight * np.sin(angle)
    angle = turn * np.arange(WIN)[:, None] * shifts[None, :]
    cosine, sine = np.cos(angle), np.sin(angle)
    inverse_right = np.tile(
        np.concatenate([cosine, cosine, -sine, sine, -sine, -sine, -cosine, cosine]),
        (1, 128 // DISP),
    )
    row_weight = np.zeros((KEPT, 128))
    row_weight[: len(waves)] = weight[:, None]
    f32 = np.float32
    return (
        left_table, right_table,
        inverse_left.astype(f32), inverse_right.astype(f32), row_weight.astype(f32),
    )


def wrapped(index, count):
    return jnp.where(index >= count, index - count, index)


def whole(values, reduce):
    return reduce(reduce(values, axis=0, keepdims=True), axis=1, keepdims=True)


def chunks(rows, action, unroll):
    def step(i, carry):
        return action(pl.ds(pl.multiple_of(i * CHUNK, CHUNK), CHUNK), carry)

    return lambda init: lax.fori_loop(0, rows // CHUNK, step, init, unroll=unroll)


def prepare(turned_ref, blocks_ref, ids_ref, marks_ref, fwd_ref, bwd_ref, lib_ref, gather_ref, spread_ref):
    f32, bf16 = jnp.float32, jnp.bfloat16
    count = lax.axis_size("wide")
    me = lax.axis_index("wide")
    cams, members = blocks_ref.shape[0], blocks_ref.shape[1]
    columns = lib_ref.shape[1]

    def strip_rows(ids, stride):
        slot = jnp.floor((ids + 0.5) * (1.0 / TILES))
        owner = slot + (me - count // 2).astype(f32)
        inside = (owner >= 0.0) & (owner < count)
        return jnp.where(inside, owner * stride + (ids - slot * TILES), -1.0)

    def camera(cam, _):
        for m in range(members):
            rows = slice(m % 2 * 128, m % 2 * 128 + 128)
            lanes = slice(m // 2 * 128, m // 2 * 128 + 128)
            fwd_ref[cam, rows, lanes] = turned_ref[cam, m]
            bwd_ref[cam, rows, lanes] = blocks_ref[cam, m]
        ids = strip_rows(ids_ref[cam].astype(f32), PROJ_ROWS)

        def gather(i, _):
            rows = pl.ds(pl.multiple_of(i * 32, 32), 32)
            row = lax.broadcasted_iota(jnp.int32, (32, columns), 0) + i * 32
            gather_ref[cam, rows, :] = jnp.where(row.astype(f32) == ids, 1.0, 0.0).astype(bf16)
            return 0

        lax.fori_loop(0, count * PROJ_ROWS // 32, gather, 0)

        def spread(i, _):
            rows = pl.ds(pl.multiple_of(i * 64, 64), 64)
            mark = marks_ref[cam, rows, :].astype(f32)
            lib = jnp.floor(mark * (1.0 / 512.0))
            lib_ref[cam, rows, :] = lib.astype(bf16)
            ids = strip_rows(mark - lib * 512.0, RATIO_ROWS)
            lane = lax.broadcasted_iota(jnp.int32, (64, 128), 1).astype(f32)
            for part in range(count * RATIO_ROWS // 128):
                here = jnp.where(lane + part * 128.0 == ids, 1.0, 0.0)
                spread_ref[cam, rows, part * 128 : (part + 1) * 128] = here.astype(bf16)
            return 0

        lax.fori_loop(0, columns // 64, spread, 0)
        return 0

    lax.fori_loop(0, cams, camera, 0)


def reconstruct(refs, scratch, barrier_done, finish):
    init_ref, img_ref, fwd_ref, bwd_ref, lib_ref, gather_ref, spread_ref, vol_ref = refs
    cols_ref, part_ref, recv_ref, ratio_ref = scratch[:4]
    part_send, part_recv, ratio_send, ratio_recv = scratch[4:]
    f32, bf16 = jnp.float32, jnp.bfloat16
    count = lax.axis_size("wide")
    me = lax.axis_index("wide")
    cams = fwd_ref.shape[0]
    columns = init_ref.shape[1]

    def by_library(values, cam, rows, table):
        lib = lib_ref[cam, rows, :]
        zero = jnp.zeros_like(values)
        odd = (lib == 1) | (lib == 3) | (lib == 5) | (lib == 7)
        lhs = jnp.concatenate(
            [jnp.where(odd, zero, values), jnp.where(odd, values, zero)], axis=1
        )
        wide = jnp.dot(lhs, table, preferred_element_type=f32)
        pair = lib.astype(f32)
        low = jnp.where(pair < 2, wide[:, 0:128], wide[:, 128:256])
        high = jnp.where(pair < 6, wide[:, 256:384], wide[:, 384:512])
        return jnp.where(pair < 4, low, high)

    def project_rows(e, cam, rows, vol):
        proj = by_library(vol.astype(bf16), cam, rows, fwd_ref[cam])
        high, low = split(proj)
        cols_ref[e, rows, 0:128] = high
        cols_ref[e, rows, 128:256] = low

    def part_copy(e, d, owner):
        target = wrapped(me + d, count)
        return pltpu.make_async_remote_copy(
            src_ref=part_ref.at[e, target],
            dst_ref=recv_ref.at[e, owner],
            send_sem=part_send.at[e, d],
            recv_sem=part_recv.at[e, owner],
            device_id={"wide": target},
            device_id_type=MESH,
        )

    def strip(e, owner):
        return ratio_ref.at[e, pl.ds(pl.multiple_of(owner * RATIO_ROWS, RATIO_ROWS), RATIO_ROWS)]

    def ratio_copy(e, d, owner):
        return pltpu.make_async_remote_copy(
            src_ref=strip(e, me),
            dst_ref=strip(e, owner),
            send_sem=ratio_send.at[e, d],
            recv_sem=ratio_recv.at[e, owner],
            device_id={"wide": wrapped(me + d, count)},
            device_id_type=MESH,
        )

    def each(action):
        def step(d, _):
            action(d)
            return 0

        lax.fori_loop(1, count, step, 0, unroll=True)

    def send_parts(e, cam):
        both = jnp.dot(gather_ref[cam], cols_ref[e], preferred_element_type=f32)
        total = both[:, 0:128] + both[:, 128:256]
        part_ref[e] = total.reshape(part_ref.shape[1:])
        each(lambda d: part_copy(e, d, me).start())

    def send_ratio(e, cam):
        def take(d, total):
            source = wrapped(me + d, count)
            part_copy(e, d, source).wait_recv()
            return total + recv_ref[e, source]

        total = lax.fori_loop(1, count, take, part_ref[e, me], unroll=True)
        tiles = img_ref.shape[2] * img_ref.shape[3]
        image = jnp.concatenate([img_ref[e, cam, i] for i in range(img_ref.shape[2])], axis=0)
        ratio = jnp.log(image + 1.0) - jnp.log(total[0:tiles] + 1.0)
        ratio = jnp.concatenate([ratio, jnp.zeros((RATIO_ROWS - tiles, 128), f32)], axis=0)
        ratio_ref[e, pl.ds(pl.multiple_of(me * RATIO_ROWS, RATIO_ROWS), RATIO_ROWS), :] = (
            ratio.astype(bf16)
        )
        each(lambda d: ratio_copy(e, d, me).start())

    def collect_ratio(e):
        each(lambda d: ratio_copy(e, d, wrapped(me + d, count)).wait_recv())
        each(lambda d: part_copy(e, d, me).wait_send())
        each(lambda d: ratio_copy(e, d, me).wait_send())

    def updated_rows(e, cam, rows):
        near = jnp.dot(spread_ref[cam, rows, :], ratio_ref[e], preferred_element_type=f32)
        back = by_library(near.astype(bf16), cam, rows, bwd_ref[cam])
        return vol_ref[e, rows, :] * jnp.exp(back)

    for e in range(2):
        def first(rows, _):
            vol = init_ref[e, rows, :]
            vol_ref[e, rows, :] = vol
            project_rows(e, 0, rows, vol)
            return 0

        chunks(columns, first, 2)(0)
        if e == 0:
            barrier_done()
        send_parts(e, 0)

    def round_step(r, _):
        cam = lax.rem(r, cams)
        following = lax.rem(r + 1, cams)
        for e in range(2):
            send_ratio(e, cam)
        for e in range(2):
            collect_ratio(e)

            def both(rows, _):
                vol = updated_rows(e, cam, rows)
                vol_ref[e, rows, :] = vol
                project_rows(e, following, rows, vol)
                return 0

            chunks(columns, both, 4)(0)
            send_parts(e, following)
        return 0

    lax.fori_loop(0, SWEEPS * cams - 1, round_step, 0)
    for e in range(2):
        send_ratio(e, cams - 1)
    for e in range(2):
        collect_ratio(e)

        def final(rows, carry):
            vol = updated_rows(e, cams - 1, rows)
            vol_ref[e, rows, :] = vol
            tiles = vol.reshape(CHUNK // 8, 8, 128)
            return (
                jnp.minimum(carry[0], jnp.min(tiles, axis=0)),
                jnp.maximum(carry[1], jnp.max(tiles, axis=0)),
                carry[2] + jnp.sum(tiles, axis=0),
            )

        low = jnp.full((8, 128), 3.0e38, f32)
        least, largest, total = chunks(columns, final, 2)((low, -low, jnp.zeros((8, 128), f32)))
        finish(e, whole(least, jnp.min), whole(largest, jnp.max), whole(total, jnp.sum))


def exchange(vol_ref, code_ref, high_ref, low_ref, send_own, send_on, arrive, stats):
    f32 = jnp.float32
    wide, narrow = lax.axis_size("wide"), lax.axis_size("narrow")
    me, row = lax.axis_index("wide"), lax.axis_index("narrow")
    columns = vol_ref.shape[1]
    has_wide = {-1: me > 0, 1: me < wide - 1}
    has_narrow = {-1: row > 0, 1: row < narrow - 1}

    def encode(e, least, largest):
        base = jnp.floor(jnp.log(least) * 64.0)
        extent = jnp.floor(jnp.log(largest) * 64.0) - base + 2.0
        scale = (64.0 * STEPS) / extent
        shift = base * (1.0 / 64.0)

        def step(rows, _):
            level = (jnp.log(vol_ref[e, rows, :]) - shift) * scale
            code_ref[1, 1, e, rows, :] = (
                jnp.round(level - STEPS / 2).astype(jnp.int32).astype(jnp.int16)
            )
            return 0

        chunks(columns, step, 1)(0)
        mark = jnp.where(lax.broadcasted_iota(jnp.int32, (MARK, 128), 0) < 8, base, extent)
        code_ref[1, 1, e, columns : columns + MARK, :] = mark.astype(jnp.int32).astype(jnp.int16)

    def side_copy(e, by, place):
        return pltpu.make_async_remote_copy(
            src_ref=code_ref.at[1, 1, e],
            dst_ref=code_ref.at[1 + place, 1, e],
            send_sem=send_own.at[0, (by + 1) // 2, e],
            recv_sem=arrive.at[1 + place, 1, e],
            device_id={"wide": me + by},
            device_id_type=MESH,
        )

    def row_copy(e, column, by, place):
        sem = send_own.at[1, (by + 1) // 2, e]
        if column != 0:
            sem = send_on.at[(column + 1) // 2, (by + 1) // 2, e]
        return pltpu.make_async_remote_copy(
            src_ref=code_ref.at[1 + column, 1, e],
            dst_ref=code_ref.at[1 + column, 1 + place, e],
            send_sem=sem,
            recv_sem=arrive.at[1 + column, 1 + place, e],
            device_id={"narrow": row + by},
            device_id_type=MESH,
        )

    def send(e):
        for by in (-1, 1):
            @pl.when(has_narrow[by])
            def _():
                row_copy(e, 0, by, -by).start()

            @pl.when(has_wide[by])
            def _():
                side_copy(e, by, -by).start()

    def pass_on(e):
        for side in (-1, 1):
            @pl.when(has_wide[side])
            def _():
                side_copy(e, side, side).wait_recv()
                for by in (-1, 1):
                    @pl.when(has_narrow[by])
                    def _():
                        row_copy(e, side, by, -by).start()

    def settle(e):
        for by in (-1, 1):
            @pl.when(has_narrow[by])
            def _():
                row_copy(e, 0, by, -by).wait_send()

            @pl.when(has_wide[by])
            def _():
                side_copy(e, by, -by).wait_send()
                for up in (-1, 1):
                    @pl.when(has_narrow[up])
                    def _():
                        row_copy(e, by, up, -up).wait_send()

    def place(e, i, j, values_of):
        def step(x, _):
            high, low = split(values_of(x))
            high_ref[e, (1 + i) * BRICK + x, (1 + j) * BRICK : (2 + j) * BRICK, :] = high
            low_ref[e, (1 + i) * BRICK + x, (1 + j) * BRICK : (2 + j) * BRICK, :] = low
            return 0

        lax.fori_loop(0, BRICK, step, 0, unroll=4)

    def place_own(e):
        place(e, 0, 0, lambda x: vol_ref[
            e, pl.ds(pl.multiple_of(x * BRICK, BRICK), BRICK), :] - stats[e])

    def place_code(e, i, j):
        mark = code_ref[1 + i, 1 + j, e, columns : columns + MARK, :].astype(f32)
        step = mark[8:9] * (1.0 / (64.0 * STEPS))
        shift = mark[0:1] * (1.0 / 64.0) + step * (STEPS / 2)

        def values_of(x):
            rows = pl.ds(pl.multiple_of(x * BRICK, BRICK), BRICK)
            code = code_ref[1 + i, 1 + j, e, rows, :].astype(f32)
            return jnp.exp(code * step + shift) - stats[e]

        place(e, i, j, values_of)

    def receive(e, i, j):
        here = has_narrow[j] if j else None
        if i:
            here = has_wide[i] if here is None else here & has_wide[i]

        @pl.when(here)
        def _():
            if j:
                row_copy(e, i, j, j).wait_recv()
            place_code(e, i, j)

        @pl.when(jnp.logical_not(here))
        def _():
            place(e, i, j, lambda x: jnp.zeros((BRICK, 128), f32) - stats[e])

    return encode, send, pass_on, settle, place_own, receive


def windows(place_ref, tables, high_ref, low_ref, mids, specs, corr_ref, res_ref):
    left_ref, right_ref, inv_left_ref, inv_right_ref, weight_ref = tables
    mid_high, mid_low = mids
    spec0, spec1 = specs
    f32, bf16 = jnp.float32, jnp.bfloat16
    half = DISP // 2
    wide_y = high_ref.shape[2]

    def transform(w, e, store):
        start_x, start_y, start_z = place_ref[0][w], place_ref[1][w], place_ref[2][w]
        lead = jnp.where(start_y >= 16, start_y - 16, start_y)
        later = lax.broadcasted_iota(jnp.int32, (SPAN, 128), 0) * 0 + start_y >= 16
        lane = lax.broadcasted_iota(jnp.int32, (2 * KEPT, 256), 1)
        spot = lax.rem(lane, SPAN)
        keep = (spot >= lead) & (spot < lead + WIN) & (lane < 3 * SPAN)
        left = jnp.where(keep, left_ref[...].astype(f32), 0.0).astype(bf16)
        wide = 128 * (e + 1)
        row = lax.rem(lax.broadcasted_iota(jnp.int32, (256, wide), 0), 128)
        keep = (row >= start_z) & (row < start_z + WIN)
        right_high = jnp.where(keep, right_ref[0, :, 0:wide].astype(f32), 0.0).astype(bf16)
        right_low = jnp.where(keep, right_ref[1, :, 0:wide].astype(f32), 0.0).astype(bf16)

        def turn_y(i, _):
            sides = []
            for j in range(2):
                high, low = high_ref[e, start_x + 2 * i + j], low_ref[e, start_x + 2 * i + j]
                high = jnp.where(later, high[wide_y - SPAN :], high[:SPAN])
                low = jnp.where(later, low[wide_y - SPAN :], low[:SPAN])
                sides.append(jnp.concatenate([high, low, high, high[0:16]], axis=0))
            mixed = jnp.dot(left, jnp.concatenate(sides, axis=1), preferred_element_type=f32)
            high, low = split(mixed)
            for j in range(2):
                lanes = slice(j * 128, (j + 1) * 128)
                for source, target in ((high, mid_high), (low, mid_low)):
                    target[2 * i + j, :, 0:128] = source[0:KEPT, lanes]
                    target[2 * i + j, :, 128:256] = source[KEPT : 2 * KEPT, lanes]
            return 0

        lax.fori_loop(0, WIN // 2, turn_y, 0, unroll=4)

        def turn_z(i, _):
            xs = pl.ds(i * 16, 16)
            high = mid_high[xs].reshape(16 * KEPT, 256)
            low = mid_low[xs].reshape(16 * KEPT, 256)
            value = jnp.dot(high, right_high, preferred_element_type=f32)
            value += jnp.dot(low, right_high, preferred_element_type=f32)
            value += jnp.dot(high, right_low, preferred_element_type=f32)
            store(i * 16, value.reshape(16, KEPT, wide))
            return 0

        lax.fori_loop(0, WIN // 16, turn_z, 0)

    def first(w, _):
        def store(x, value):
            spec0[w, pl.ds(x, 16)] = value

        transform(w, 0, store)
        return 0

    def second(w, _):
        def store(x, value):
            spec1[pl.ds(x + half, 16)] = value

        transform(w, 1, store)

        def sums(x, carry):
            return carry[0] + spec0[w, x, 0:8, :], carry[1] + spec1[x + half, 0:8, :]

        mean0, mean1 = lax.fori_loop(
            0, WIN, sums, (jnp.zeros((8, 128), f32), jnp.zeros((8, 256), f32)), unroll=4
        )
        lane = lax.broadcasted_iota(jnp.int32, (8, 256), 1)
        row = lax.broadcasted_iota(jnp.int32, (8, 256), 0)
        mean1 = jnp.where((row == 0) & ((lane == 0) | (lane == 192)), mean1 * (1.0 / WIN), 0.0)
        lane = lax.broadcasted_iota(jnp.int32, (8, 128), 1)
        row = lax.broadcasted_iota(jnp.int32, (8, 128), 0)
        mean0 = jnp.where((row == 0) & (lane == 0), mean0 * (1.0 / WIN), 0.0)

        def centre(x, carry):
            spec0[w, x, 0:8, :] = spec0[w, x, 0:8, :] - mean0
            spec1[x + half, 0:8, :] = spec1[x + half, 0:8, :] - mean1
            value0, value1 = spec0[w, x], spec1[x + half, :, 0:128]
            return carry[0] + value0 * value0, carry[1] + value1 * value1

        zero = jnp.zeros((KEPT, 128), f32)
        power0, power1 = lax.fori_loop(0, WIN, centre, (zero, zero), unroll=2)
        count = 1.0 / (WIN * WIN * WIN**3)
        rms0 = jnp.sqrt(whole(power0 * weight_ref[...], jnp.sum) * count + 1e-6)
        rms1 = jnp.sqrt(whole(power1 * weight_ref[...], jnp.sum) * count + 1e-6)
        spec1[0:half] = spec1[WIN : WIN + half]
        spec1[WIN + half : WIN + DISP] = spec1[half:DISP]

        def group(g, _):
            first = lax.div(g, KEPT // 8) * half
            rows = pl.ds(pl.multiple_of((g - lax.div(g, KEPT // 8) * (KEPT // 8)) * 8, 8), 8)

            def block(i, carry):
                carry = list(carry)
                base = i * 4
                ones = [spec0[w, base + j, rows, :] for j in range(4)]
                plain = [spec1[base + first + j, rows, 0:128] for j in range(half + 3)]
                swapped = [spec1[base + first + j, rows, 128:256] for j in range(half + 3)]
                for j in range(4):
                    for s in range(half):
                        carry[s] = carry[s] + ones[j] * plain[j + s]
                        carry[half + s] = carry[half + s] + ones[j] * swapped[j + s]
                return tuple(carry)

            zero = jnp.zeros((8, 128), f32)
            done = lax.fori_loop(0, WIN // 4, block, (zero,) * DISP)
            for s in range(half):
                corr_ref[first + s, rows, 0:128] = done[s]
                corr_ref[first + s, rows, 128:256] = done[half + s]
            return 0

        lax.fori_loop(0, 2 * (KEPT // 8), group, 0)

        highest = lax.Precision.HIGHEST
        turned = []
        for s in range(DISP):
            value = jnp.dot(
                inv_left_ref[...], corr_ref[s], precision=highest, preferred_element_type=f32
            )
            turned.append(jnp.concatenate([value[0:DISP], value[DISP : 2 * DISP]], axis=1))
        final = jnp.dot(
            jnp.concatenate(turned, axis=0), inv_right_ref[...],
            precision=highest, preferred_element_type=f32,
        )
        scale = 1.0 / (WIN * WIN * WIN**1.5)
        final = (final * (scale / (rms0 * rms1))).reshape(DISP * DISP // 8, 8, 128)
        lane = lax.broadcasted_iota(jnp.int32, final.shape, 2)
        row = lax.broadcasted_iota(jnp.int32, final.shape, 1)
        own = (lane >= row * DISP) & (lane < row * DISP + DISP)
        final = jnp.sum(jnp.where(own, final, 0.0), axis=1)
        res_ref[w] = final
        return 0

    return first, second


def piv_kernel(
    win_x_ref, win_y_ref, win_z_ref, init_ref, img_ref, turned_ref, blocks_ref, ids_ref, marks_ref,
    left_ref, right_ref, inv_left_ref, inv_right_ref, weight_ref,
    vol_ref, out_ref,
    fwd_ref, bwd_ref, lib_ref, gather_ref, spread_ref,
    cols_ref, part_ref, recv_ref, ratio_ref,
    code_ref, high_ref, low_ref, mid_high, mid_low, spec0, spec1, corr_ref, res_ref,
    part_send, part_recv, ratio_send, ratio_recv, send_own, send_on, arrive,
):
    count, depth = lax.axis_size("wide"), lax.axis_size("narrow")
    me, row = lax.axis_index("wide"), lax.axis_index("narrow")
    barrier = pltpu.get_barrier_semaphore()

    def greet(d, _):
        pl.semaphore_signal(
            barrier, inc=1, device_id={"wide": wrapped(me + d, count)}, device_id_type=MESH
        )
        return 0

    lax.fori_loop(1, count, greet, 0)
    for by in (1, depth - 1):
        pl.semaphore_signal(
            barrier, inc=1, device_id={"narrow": wrapped(row + by, depth)}, device_id_type=MESH
        )

    def barrier_done():
        pl.semaphore_wait(barrier, count + 1)

    prepare(
        turned_ref, blocks_ref, ids_ref, marks_ref,
        fwd_ref, bwd_ref, lib_ref, gather_ref, spread_ref,
    )
    stats = {}
    encode, send, pass_on, settle, place_own, receive = exchange(
        vol_ref, code_ref, high_ref, low_ref, send_own, send_on, arrive, stats
    )

    def finish(e, least, largest, total):
        stats[e] = total * (1.0 / (vol_ref.shape[1] * 128))
        encode(e, least, largest)
        send(e)

    reconstruct(
        (init_ref, img_ref, fwd_ref, bwd_ref, lib_ref, gather_ref, spread_ref, vol_ref),
        (cols_ref, part_ref, recv_ref, ratio_ref, part_send, part_recv, ratio_send, ratio_recv),
        barrier_done,
        finish,
    )
    place_own(0)
    pass_on(0)
    for i in (-1, 1):
        receive(0, i, 0)
    place_own(1)
    pass_on(1)
    for i, j in ((0, -1), (0, 1), (-1, -1), (-1, 1), (1, -1), (1, 1)):
        receive(0, i, j)
    first, second = windows(
        (win_x_ref, win_y_ref, win_z_ref),
        (left_ref, right_ref, inv_left_ref, inv_right_ref, weight_ref),
        high_ref, low_ref, (mid_high, mid_low), (spec0, spec1), corr_ref, res_ref,
    )
    lax.fori_loop(0, spec0.shape[0], first, 0)
    for i, j in ((-1, 0), (1, 0), (0, -1), (0, 1), (-1, -1), (-1, 1), (1, -1), (1, 1)):
        receive(1, i, j)
    for e in range(2):
        settle(e)
    lax.fori_loop(0, spec0.shape[0], second, 0)
    for w in range(out_ref.shape[0]):
        for s in range(res_ref.shape[1]):
            out_ref[w : w + 1, s * 128 : (s + 1) * 128] = res_ref[w, s : s + 1]


def body(initial, images, blocks, lib_index, tile_map, win_x, win_y, win_z):
    count = lax.axis_size("wide")
    f32, bf16 = jnp.float32, jnp.bfloat16
    cams, members = blocks.shape[0], blocks.shape[1]
    columns = initial.shape[1] * initial.shape[2]
    windows_count = win_x.size
    marks = (tile_map + 512 * lib_index).reshape(cams, columns, 1)
    vmem = pl.BlockSpec(memory_space=pltpu.VMEM)
    wide_x, wide_y = 3 * BRICK, 3 * BRICK
    volume, correlation = pl.pallas_call(
        piv_kernel,
        out_shape=(
            jax.ShapeDtypeStruct((2, columns, 128), f32),
            jax.ShapeDtypeStruct((windows_count, DISP * DISP * DISP), f32),
        ),
        in_specs=[pl.BlockSpec(memory_space=pltpu.SMEM)] * 3 + [vmem] * 11,
        out_specs=(vmem, vmem),
        scratch_shapes=[
            pltpu.VMEM((cams, 256, members * 64), bf16),
            pltpu.VMEM((cams, 256, members * 64), bf16),
            pltpu.VMEM((cams, columns, 128), bf16),
            pltpu.VMEM((cams, count * PROJ_ROWS, columns), bf16),
            pltpu.VMEM((cams, columns, count * RATIO_ROWS), bf16),
            pltpu.VMEM((2, columns, 256), bf16),
            pltpu.VMEM((2, count, PROJ_ROWS, 128), f32),
            pltpu.VMEM((2, count, PROJ_ROWS, 128), f32),
            pltpu.VMEM((2, count * RATIO_ROWS, 128), bf16),
            pltpu.VMEM((3, 3, 2, columns + MARK, 128), jnp.int16),
            pltpu.VMEM((2, wide_x, wide_y, 128), bf16),
            pltpu.VMEM((2, wide_x, wide_y, 128), bf16),
            pltpu.VMEM((WIN, KEPT, 256), bf16),
            pltpu.VMEM((WIN, KEPT, 256), bf16),
            pltpu.VMEM((windows_count, WIN, KEPT, 128), f32),
            pltpu.VMEM((WIN + DISP, KEPT, 256), f32),
            pltpu.VMEM((DISP, KEPT, 256), f32),
            pltpu.VMEM((windows_count, DISP * DISP * DISP // 128, 128), f32),
            pltpu.SemaphoreType.DMA((2, count)),
            pltpu.SemaphoreType.DMA((2, count)),
            pltpu.SemaphoreType.DMA((2, count)),
            pltpu.SemaphoreType.DMA((2, count)),
            pltpu.SemaphoreType.DMA((2, 2, 2)),
            pltpu.SemaphoreType.DMA((2, 2, 2)),
            pltpu.SemaphoreType.DMA((3, 3, 2)),
        ],
        compiler_params=pltpu.CompilerParams(
            collective_id=0, has_side_effects=True, vmem_limit_bytes=60 * 1024 * 1024
        ),
        name="piv",
    )(
        win_x.reshape(-1),
        win_y.reshape(-1),
        win_z.reshape(-1),
        initial.reshape(2, columns, 128),
        images,
        blocks.transpose(0, 1, 3, 2),
        blocks,
        tile_map.reshape(cams, 1, columns),
        jnp.broadcast_to(marks, (cams, columns, 128)),
        *[jnp.asarray(table) for table in window_tables()],
    )
    return (
        volume.reshape(initial.shape),
        correlation.reshape(1, 1, windows_count, DISP * DISP * DISP),
    )


def solution(mesh):
    placed = (
        P(None, "wide", "narrow", None),
        P(None, None, "wide", "narrow", None),
        P(),
        P(None, "wide", "narrow"),
        P(None, "wide", "narrow"),
        P("wide", "narrow", None),
        P("wide", "narrow", None),
        P("wide", "narrow", None),
    )
    return jax.shard_map(
        body,
        mesh=mesh,
        in_specs=placed,
        out_specs=(P(None, "wide", "narrow", None), P("wide", "narrow", None, None)),
        check_vma=False,
    )
```

```python
import jax
import jax.numpy as jnp
import ml_dtypes
import numpy as np
from jax import lax
from jax.experimental import pallas as pl
from jax.experimental.pallas import tpu as pltpu
from jax.sharding import PartitionSpec as P

MESH = pl.DeviceIdType.MESH
PROJ_ROWS = 24
RATIO_ROWS = 32
CHUNK = 256
WIN = 64
DISP = 16
SWEEPS = 2
SPAN = 80
KEPT = 40
BRICK = 32
MARK = 16
STEPS = 65000.0
TILES = 18


def split(values):
    high = values.astype(jnp.bfloat16)
    return high, (values - high.astype(jnp.float32)).astype(jnp.bfloat16)


def window_tables():
    bf16 = ml_dtypes.bfloat16
    turn = 2.0 * np.pi / WIN

    def parts(table):
        high = table.astype(bf16)
        return high, (table - high.astype(np.float64)).astype(bf16)

    waves = np.arange(WIN // 2 + 1)
    angle = turn * (waves[:, None] * np.arange(SPAN)[None, :] % WIN)
    left = np.zeros((2 * KEPT, SPAN))
    left[: len(waves)] = np.cos(angle)
    left[KEPT : KEPT + len(waves)] = -np.sin(angle)
    left_high, left_low = parts(left)
    left_table = np.zeros((2 * KEPT, 256), bf16)
    for place, table in enumerate((left_high, left_high, left_low)):
        left_table[:, place * SPAN : (place + 1) * SPAN] = table

    angle = turn * (np.arange(128)[:, None] * np.arange(WIN)[None, :] % WIN)
    cosine, sine = np.cos(angle), np.sin(angle)
    right = np.block([[cosine, -sine], [sine, cosine]])
    right_table = np.concatenate(parts(right), axis=1)

    shifts = np.arange(DISP) - DISP // 2
    weight = np.where(waves % (WIN // 2) == 0, 1.0, 2.0)
    angle = turn * shifts[:, None] * waves[None, :]
    inverse_left = np.zeros((2 * DISP, KEPT))
    inverse_left[:DISP, : len(waves)] = weight * np.cos(angle)
    inverse_left[DISP:, : len(waves)] = weight * np.sin(angle)
    angle = turn * np.arange(WIN)[:, None] * shifts[None, :]
    cosine, sine = np.cos(angle), np.sin(angle)
    inverse_right = np.tile(
        np.concatenate([cosine, cosine, -sine, sine, -sine, -sine, -cosine, cosine]),
        (1, 128 // DISP),
    )
    row_weight = np.zeros((KEPT, 128))
    row_weight[: len(waves)] = weight[:, None]
    f32 = np.float32
    return (
        left_table, right_table,
        inverse_left.astype(f32), inverse_right.astype(f32), row_weight.astype(f32),
    )


def wrapped(index, count):
    return jnp.where(index >= count, index - count, index)


def whole(values, reduce):
    return reduce(reduce(values, axis=0, keepdims=True), axis=1, keepdims=True)


def chunks(rows, action, unroll):
    def step(i, carry):
        return action(pl.ds(pl.multiple_of(i * CHUNK, CHUNK), CHUNK), carry)

    return lambda init: lax.fori_loop(0, rows // CHUNK, step, init, unroll=unroll)


def prepare(turned_ref, blocks_ref, ids_ref, marks_ref, fwd_ref, bwd_ref, lib_ref, gather_ref, spread_ref):
    f32, bf16 = jnp.float32, jnp.bfloat16
    count = lax.axis_size("wide")
    me = lax.axis_index("wide")
    cams, members = blocks_ref.shape[0], blocks_ref.shape[1]
    columns = lib_ref.shape[1]

    def strip_rows(ids, stride):
        slot = jnp.floor((ids + 0.5) * (1.0 / TILES))
        owner = slot + (me - count // 2).astype(f32)
        inside = (owner >= 0.0) & (owner < count)
        return jnp.where(inside, owner * stride + (ids - slot * TILES), -1.0)

    def camera(cam, _):
        for m in range(members):
            rows = slice(m % 2 * 128, m % 2 * 128 + 128)
            lanes = slice(m // 2 * 128, m // 2 * 128 + 128)
            fwd_ref[cam, rows, lanes] = turned_ref[cam, m]
            bwd_ref[cam, rows, lanes] = blocks_ref[cam, m]
        ids = strip_rows(ids_ref[cam].astype(f32), PROJ_ROWS)

        def gather(i, _):
            rows = pl.ds(pl.multiple_of(i * 32, 32), 32)
            row = lax.broadcasted_iota(jnp.int32, (32, columns), 0) + i * 32
            gather_ref[cam, rows, :] = jnp.where(row.astype(f32) == ids, 1.0, 0.0).astype(bf16)
            return 0

        lax.fori_loop(0, count * PROJ_ROWS // 32, gather, 0)

        def spread(i, _):
            rows = pl.ds(pl.multiple_of(i * 64, 64), 64)
            mark = marks_ref[cam, rows, :].astype(f32)
            lib = jnp.floor(mark * (1.0 / 512.0))
            lib_ref[cam, rows, :] = lib.astype(bf16)
            ids = strip_rows(mark - lib * 512.0, RATIO_ROWS)
            lane = lax.broadcasted_iota(jnp.int32, (64, 128), 1).astype(f32)
            for part in range(count * RATIO_ROWS // 128):
                here = jnp.where(lane + part * 128.0 == ids, 1.0, 0.0)
                spread_ref[cam, rows, part * 128 : (part + 1) * 128] = here.astype(bf16)
            return 0

        lax.fori_loop(0, columns // 64, spread, 0)
        return 0

    lax.fori_loop(0, cams, camera, 0)


def reconstruct(refs, scratch, barrier_done, finish):
    init_ref, img_ref, fwd_ref, bwd_ref, lib_ref, gather_ref, spread_ref, vol_ref = refs
    cols_ref, part_ref, recv_ref, ratio_ref = scratch[:4]
    part_send, part_recv, ratio_send, ratio_recv = scratch[4:]
    f32, bf16 = jnp.float32, jnp.bfloat16
    count = lax.axis_size("wide")
    me = lax.axis_index("wide")
    cams = fwd_ref.shape[0]
    columns = init_ref.shape[1]

    def by_library(values, cam, rows, table):
        lib = lib_ref[cam, rows, :]
        zero = jnp.zeros_like(values)
        odd = (lib == 1) | (lib == 3) | (lib == 5) | (lib == 7)
        lhs = jnp.concatenate(
            [jnp.where(odd, zero, values), jnp.where(odd, values, zero)], axis=1
        )
        wide = jnp.dot(lhs, table, preferred_element_type=f32)
        pair = lib.astype(f32)
        low = jnp.where(pair < 2, wide[:, 0:128], wide[:, 128:256])
        high = jnp.where(pair < 6, wide[:, 256:384], wide[:, 384:512])
        return jnp.where(pair < 4, low, high)

    def project_rows(e, cam, rows, vol):
        proj = by_library(vol.astype(bf16), cam, rows, fwd_ref[cam])
        high, low = split(proj)
        cols_ref[e, rows, 0:128] = high
        cols_ref[e, rows, 128:256] = low

    def part_copy(e, d, owner):
        target = wrapped(me + d, count)
        return pltpu.make_async_remote_copy(
            src_ref=part_ref.at[e, target],
            dst_ref=recv_ref.at[e, owner],
            send_sem=part_send.at[e],
            recv_sem=part_recv.at[e],
            device_id={"wide": target},
            device_id_type=MESH,
        )

    def strip(e, owner):
        return ratio_ref.at[e, pl.ds(pl.multiple_of(owner * RATIO_ROWS, RATIO_ROWS), RATIO_ROWS)]

    def ratio_copy(e, d, owner):
        return pltpu.make_async_remote_copy(
            src_ref=strip(e, me),
            dst_ref=strip(e, owner),
            send_sem=ratio_send.at[e],
            recv_sem=ratio_recv.at[e],
            device_id={"wide": wrapped(me + d, count)},
            device_id_type=MESH,
        )

    def parts_done(e, sem):
        slots = recv_ref.at[e, pl.ds(0, count - 1)]
        pltpu.make_async_copy(slots, slots, sem.at[e]).wait()

    def ratios_done(e, sem):
        strips = ratio_ref.at[e, pl.ds(0, (count - 1) * RATIO_ROWS)]
        pltpu.make_async_copy(strips, strips, sem.at[e]).wait()

    far_first = sorted(range(1, count), key=lambda d: -(2 - abs(d % 4 - 2)) - (2 - abs(d // 4 - 2)))

    def send_parts(e, cam):
        both = jnp.dot(gather_ref[cam], cols_ref[e], preferred_element_type=f32)
        total = both[:, 0:128] + both[:, 128:256]
        part_ref[e] = total.reshape(part_ref.shape[1:])
        for d in far_first:
            part_copy(e, d, me).start()

    def send_ratio(e, cam):
        def take(d, total):
            return total + recv_ref[e, wrapped(me + d, count)]

        parts_done(e, part_recv)
        total = lax.fori_loop(1, count, take, part_ref[e, me], unroll=True)
        tiles = img_ref.shape[2] * img_ref.shape[3]
        image = jnp.concatenate([img_ref[e, cam, i] for i in range(img_ref.shape[2])], axis=0)
        ratio = jnp.log(image + 1.0) - jnp.log(total[0:tiles] + 1.0)
        ratio = jnp.concatenate([ratio, jnp.zeros((RATIO_ROWS - tiles, 128), f32)], axis=0)
        ratio_ref[e, pl.ds(pl.multiple_of(me * RATIO_ROWS, RATIO_ROWS), RATIO_ROWS), :] = (
            ratio.astype(bf16)
        )
        for d in far_first:
            ratio_copy(e, d, me).start()

    def collect_ratio(e):
        ratios_done(e, ratio_recv)
        parts_done(e, part_send)
        ratios_done(e, ratio_send)

    def updated_rows(e, cam, rows):
        near = jnp.dot(spread_ref[cam, rows, :], ratio_ref[e], preferred_element_type=f32)
        back = by_library(near.astype(bf16), cam, rows, bwd_ref[cam])
        return vol_ref[e, rows, :] * jnp.exp(back)

    for e in range(2):
        def first(rows, _):
            vol = init_ref[e, rows, :]
            vol_ref[e, rows, :] = vol
            project_rows(e, 0, rows, vol)
            return 0

        chunks(columns, first, 2)(0)
        if e == 0:
            barrier_done()
        send_parts(e, 0)

    def round_step(r, _):
        cam = lax.rem(r, cams)
        following = lax.rem(r + 1, cams)
        for e in range(2):
            send_ratio(e, cam)
        for e in range(2):
            collect_ratio(e)

            def both(rows, _):
                vol = updated_rows(e, cam, rows)
                vol_ref[e, rows, :] = vol
                project_rows(e, following, rows, vol)
                return 0

            chunks(columns, both, 4)(0)
            send_parts(e, following)
        return 0

    lax.fori_loop(0, SWEEPS * cams - 1, round_step, 0)
    for e in range(2):
        send_ratio(e, cams - 1)
    for e in range(2):
        collect_ratio(e)

        def final(rows, carry):
            vol = updated_rows(e, cams - 1, rows)
            vol_ref[e, rows, :] = vol
            tiles = vol.reshape(CHUNK // 8, 8, 128)
            return (
                jnp.minimum(carry[0], jnp.min(tiles, axis=0)),
                jnp.maximum(carry[1], jnp.max(tiles, axis=0)),
                carry[2] + jnp.sum(tiles, axis=0),
            )

        low = jnp.full((8, 128), 3.0e38, f32)
        least, largest, total = chunks(columns, final, 2)((low, -low, jnp.zeros((8, 128), f32)))
        finish(e, whole(least, jnp.min), whole(largest, jnp.max), whole(total, jnp.sum))


def exchange(vol_ref, code_ref, high_ref, low_ref, send_own, send_on, arrive, stats):
    f32 = jnp.float32
    wide, narrow = lax.axis_size("wide"), lax.axis_size("narrow")
    me, row = lax.axis_index("wide"), lax.axis_index("narrow")
    columns = vol_ref.shape[1]
    has_wide = {-1: me > 0, 1: me < wide - 1}
    has_narrow = {-1: row > 0, 1: row < narrow - 1}

    def encode(e, least, largest):
        base = jnp.floor(jnp.log(least) * 64.0)
        extent = jnp.floor(jnp.log(largest) * 64.0) - base + 2.0
        scale = (64.0 * STEPS) / extent
        shift = base * (1.0 / 64.0)

        def step(rows, _):
            level = (jnp.log(vol_ref[e, rows, :]) - shift) * scale
            code_ref[1, 1, e, rows, :] = (
                jnp.round(level - STEPS / 2).astype(jnp.int32).astype(jnp.int16)
            )
            return 0

        chunks(columns, step, 1)(0)
        mark = jnp.where(lax.broadcasted_iota(jnp.int32, (MARK, 128), 0) < 8, base, extent)
        code_ref[1, 1, e, columns : columns + MARK, :] = mark.astype(jnp.int32).astype(jnp.int16)

    def side_copy(e, by, place):
        return pltpu.make_async_remote_copy(
            src_ref=code_ref.at[1, 1, e],
            dst_ref=code_ref.at[1 + place, 1, e],
            send_sem=send_own.at[0, (by + 1) // 2, e],
            recv_sem=arrive.at[1 + place, 1, e],
            device_id={"wide": me + by},
            device_id_type=MESH,
        )

    def row_copy(e, column, by, place):
        sem = send_own.at[1, (by + 1) // 2, e]
        if column != 0:
            sem = send_on.at[(column + 1) // 2, (by + 1) // 2, e]
        return pltpu.make_async_remote_copy(
            src_ref=code_ref.at[1 + column, 1, e],
            dst_ref=code_ref.at[1 + column, 1 + place, e],
            send_sem=sem,
            recv_sem=arrive.at[1 + column, 1 + place, e],
            device_id={"narrow": row + by},
            device_id_type=MESH,
        )

    def send(e):
        for by in (-1, 1):
            @pl.when(has_narrow[by])
            def _():
                row_copy(e, 0, by, -by).start()

            @pl.when(has_wide[by])
            def _():
                side_copy(e, by, -by).start()

    def pass_on(e):
        for side in (-1, 1):
            @pl.when(has_wide[side])
            def _():
                side_copy(e, side, side).wait_recv()
                for by in (-1, 1):
                    @pl.when(has_narrow[by])
                    def _():
                        row_copy(e, side, by, -by).start()

    def settle(e):
        for by in (-1, 1):
            @pl.when(has_narrow[by])
            def _():
                row_copy(e, 0, by, -by).wait_send()

            @pl.when(has_wide[by])
            def _():
                side_copy(e, by, -by).wait_send()
                for up in (-1, 1):
                    @pl.when(has_narrow[up])
                    def _():
                        row_copy(e, by, up, -up).wait_send()

    def place(e, i, j, values_of):
        def step(x, _):
            high, low = split(values_of(x))
            high_ref[e, (1 + i) * BRICK + x, (1 + j) * BRICK : (2 + j) * BRICK, :] = high
            low_ref[e, (1 + i) * BRICK + x, (1 + j) * BRICK : (2 + j) * BRICK, :] = low
            return 0

        lax.fori_loop(0, BRICK, step, 0, unroll=4)

    def place_own(e):
        place(e, 0, 0, lambda x: vol_ref[
            e, pl.ds(pl.multiple_of(x * BRICK, BRICK), BRICK), :] - stats[e])

    def place_code(e, i, j):
        mark = code_ref[1 + i, 1 + j, e, columns : columns + MARK, :].astype(f32)
        step = mark[8:9] * (1.0 / (64.0 * STEPS))
        shift = mark[0:1] * (1.0 / 64.0) + step * (STEPS / 2)

        def values_of(x):
            rows = pl.ds(pl.multiple_of(x * BRICK, BRICK), BRICK)
            code = code_ref[1 + i, 1 + j, e, rows, :].astype(f32)
            return jnp.exp(code * step + shift) - stats[e]

        place(e, i, j, values_of)

    def receive(e, i, j):
        here = has_narrow[j] if j else None
        if i:
            here = has_wide[i] if here is None else here & has_wide[i]

        @pl.when(here)
        def _():
            if j:
                row_copy(e, i, j, j).wait_recv()
            place_code(e, i, j)

        @pl.when(jnp.logical_not(here))
        def _():
            place(e, i, j, lambda x: jnp.zeros((BRICK, 128), f32) - stats[e])

    return encode, send, pass_on, settle, place_own, receive


def windows(place_ref, tables, high_ref, low_ref, mids, specs, corr_ref, res_ref):
    left_ref, right_ref, inv_left_ref, inv_right_ref, weight_ref = tables
    mid_high, mid_low = mids
    spec0, spec1 = specs
    f32, bf16 = jnp.float32, jnp.bfloat16
    half = DISP // 2
    wide_y = high_ref.shape[2]

    def transform(w, e, store):
        start_x, start_y, start_z = place_ref[0][w], place_ref[1][w], place_ref[2][w]
        lead = jnp.where(start_y >= 16, start_y - 16, start_y)
        later = lax.broadcasted_iota(jnp.int32, (SPAN, 128), 0) * 0 + start_y >= 16
        lane = lax.broadcasted_iota(jnp.int32, (2 * KEPT, 256), 1)
        spot = lax.rem(lane, SPAN)
        keep = (spot >= lead) & (spot < lead + WIN) & (lane < 3 * SPAN)
        left = jnp.where(keep, left_ref[...].astype(f32), 0.0).astype(bf16)
        row = lax.rem(lax.broadcasted_iota(jnp.int32, (256, 256), 0), 128)
        keep = (row >= start_z) & (row < start_z + WIN)
        right = jnp.where(keep, right_ref[...].astype(f32), 0.0).astype(bf16)

        def turn_y(i, _):
            sides = []
            for j in range(2):
                high, low = high_ref[e, start_x + 2 * i + j], low_ref[e, start_x + 2 * i + j]
                high = jnp.where(later, high[wide_y - SPAN :], high[:SPAN])
                low = jnp.where(later, low[wide_y - SPAN :], low[:SPAN])
                sides.append(jnp.concatenate([high, low, high, high[0:16]], axis=0))
            mixed = jnp.dot(left, jnp.concatenate(sides, axis=1), preferred_element_type=f32)
            high, low = split(mixed)
            for j in range(2):
                lanes = slice(j * 128, (j + 1) * 128)
                for source, target in ((high, mid_high), (low, mid_low)):
                    target[2 * i + j, :, 0:128] = source[0:KEPT, lanes]
                    target[2 * i + j, :, 128:256] = source[KEPT : 2 * KEPT, lanes]
            return 0

        lax.fori_loop(0, WIN // 2, turn_y, 0, unroll=4)

        def turn_z(i, _):
            xs = pl.ds(i * 16, 16)
            high = mid_high[xs].reshape(16 * KEPT, 256)
            low = mid_low[xs].reshape(16 * KEPT, 256)
            value = jnp.dot(high, right, preferred_element_type=f32)
            rest = jnp.dot(low, right[:, 0:128], preferred_element_type=f32)
            value = value[:, 0:128] + (value[:, 128:256] + rest)
            if e == 1:
                value = jnp.concatenate([value, pltpu.roll(value, WIN, 1)], axis=1)
            store(i * 16, value.reshape(16, KEPT, 128 * (e + 1)))
            return 0

        lax.fori_loop(0, WIN // 16, turn_z, 0)

    def first(w, _):
        def store(x, value):
            spec0[w, pl.ds(x, 16)] = value

        transform(w, 0, store)
        return 0

    def second(w, _):
        def store(x, value):
            spec1[pl.ds(x + half, 16)] = value

        transform(w, 1, store)

        def sums(x, carry):
            return carry[0] + spec0[w, x, 0:8, :], carry[1] + spec1[x + half, 0:8, :]

        mean0, mean1 = lax.fori_loop(
            0, WIN, sums, (jnp.zeros((8, 128), f32), jnp.zeros((8, 256), f32)), unroll=4
        )
        lane = lax.broadcasted_iota(jnp.int32, (8, 256), 1)
        row = lax.broadcasted_iota(jnp.int32, (8, 256), 0)
        mean1 = jnp.where((row == 0) & ((lane == 0) | (lane == 192)), mean1 * (1.0 / WIN), 0.0)
        lane = lax.broadcasted_iota(jnp.int32, (8, 128), 1)
        row = lax.broadcasted_iota(jnp.int32, (8, 128), 0)
        mean0 = jnp.where((row == 0) & (lane == 0), mean0 * (1.0 / WIN), 0.0)

        def centre(x, carry):
            spec0[w, x, 0:8, :] = spec0[w, x, 0:8, :] - mean0
            spec1[x + half, 0:8, :] = spec1[x + half, 0:8, :] - mean1
            value0, value1 = spec0[w, x], spec1[x + half, :, 0:128]
            return carry[0] + value0 * value0, carry[1] + value1 * value1

        zero = jnp.zeros((KEPT, 128), f32)
        power0, power1 = lax.fori_loop(0, WIN, centre, (zero, zero), unroll=2)
        count = 1.0 / (WIN * WIN * WIN**3)
        rms0 = jnp.sqrt(whole(power0 * weight_ref[...], jnp.sum) * count + 1e-6)
        rms1 = jnp.sqrt(whole(power1 * weight_ref[...], jnp.sum) * count + 1e-6)
        spec1[0:half] = spec1[WIN : WIN + half]
        spec1[WIN + half : WIN + DISP] = spec1[half:DISP]

        def group(g, _):
            first = lax.div(g, KEPT // 8) * half
            rows = pl.ds(pl.multiple_of((g - lax.div(g, KEPT // 8) * (KEPT // 8)) * 8, 8), 8)

            def block(i, carry):
                carry = list(carry)
                base = i * 4
                ones = [spec0[w, base + j, rows, :] for j in range(4)]
                plain = [spec1[base + first + j, rows, 0:128] for j in range(half + 3)]
                swapped = [spec1[base + first + j, rows, 128:256] for j in range(half + 3)]
                for j in range(4):
                    for s in range(half):
                        carry[s] = carry[s] + ones[j] * plain[j + s]
                        carry[half + s] = carry[half + s] + ones[j] * swapped[j + s]
                return tuple(carry)

            zero = jnp.zeros((8, 128), f32)
            done = lax.fori_loop(0, WIN // 4, block, (zero,) * DISP)
            for s in range(half):
                corr_ref[first + s, rows, 0:128] = done[s]
                corr_ref[first + s, rows, 128:256] = done[half + s]
            return 0

        lax.fori_loop(0, 2 * (KEPT // 8), group, 0)

        highest = lax.Precision.HIGHEST
        turned = []
        for s in range(DISP):
            value = jnp.dot(
                inv_left_ref[...], corr_ref[s], precision=highest, preferred_element_type=f32
            )
            turned.append(jnp.concatenate([value[0:DISP], value[DISP : 2 * DISP]], axis=1))
        final = jnp.dot(
            jnp.concatenate(turned, axis=0), inv_right_ref[...],
            precision=highest, preferred_element_type=f32,
        )
        scale = 1.0 / (WIN * WIN * WIN**1.5)
        final = (final * (scale / (rms0 * rms1))).reshape(DISP * DISP // 8, 8, 128)
        lane = lax.broadcasted_iota(jnp.int32, final.shape, 2)
        row = lax.broadcasted_iota(jnp.int32, final.shape, 1)
        own = (lane >= row * DISP) & (lane < row * DISP + DISP)
        final = jnp.sum(jnp.where(own, final, 0.0), axis=1)
        res_ref[w] = final
        return 0

    return first, second


def piv_kernel(
    win_x_ref, win_y_ref, win_z_ref, init_ref, img_ref, turned_ref, blocks_ref, ids_ref, marks_ref,
    left_ref, right_ref, inv_left_ref, inv_right_ref, weight_ref,
    vol_ref, out_ref,
    fwd_ref, bwd_ref, lib_ref, gather_ref, spread_ref,
    cols_ref, part_ref, recv_ref, ratio_ref,
    code_ref, high_ref, low_ref, mid_high, mid_low, spec0, spec1, corr_ref, res_ref,
    part_send, part_recv, ratio_send, ratio_recv, send_own, send_on, arrive,
):
    count, depth = lax.axis_size("wide"), lax.axis_size("narrow")
    me, row = lax.axis_index("wide"), lax.axis_index("narrow")
    barrier = pltpu.get_barrier_semaphore()

    def greet(d, _):
        pl.semaphore_signal(
            barrier, inc=1, device_id={"wide": wrapped(me + d, count)}, device_id_type=MESH
        )
        return 0

    lax.fori_loop(1, count, greet, 0)
    for by in (1, depth - 1):
        pl.semaphore_signal(
            barrier, inc=1, device_id={"narrow": wrapped(row + by, depth)}, device_id_type=MESH
        )

    def barrier_done():
        pl.semaphore_wait(barrier, count + 1)

    prepare(
        turned_ref, blocks_ref, ids_ref, marks_ref,
        fwd_ref, bwd_ref, lib_ref, gather_ref, spread_ref,
    )
    stats = {}
    encode, send, pass_on, settle, place_own, receive = exchange(
        vol_ref, code_ref, high_ref, low_ref, send_own, send_on, arrive, stats
    )

    def finish(e, least, largest, total):
        stats[e] = total * (1.0 / (vol_ref.shape[1] * 128))
        encode(e, least, largest)
        send(e)

    reconstruct(
        (init_ref, img_ref, fwd_ref, bwd_ref, lib_ref, gather_ref, spread_ref, vol_ref),
        (cols_ref, part_ref, recv_ref, ratio_ref, part_send, part_recv, ratio_send, ratio_recv),
        barrier_done,
        finish,
    )
    place_own(0)
    pass_on(0)
    for i in (-1, 1):
        receive(0, i, 0)
    place_own(1)
    pass_on(1)
    for i, j in ((0, -1), (0, 1), (-1, -1), (-1, 1), (1, -1), (1, 1)):
        receive(0, i, j)
    first, second = windows(
        (win_x_ref, win_y_ref, win_z_ref),
        (left_ref, right_ref, inv_left_ref, inv_right_ref, weight_ref),
        high_ref, low_ref, (mid_high, mid_low), (spec0, spec1), corr_ref, res_ref,
    )
    lax.fori_loop(0, spec0.shape[0], first, 0)
    for i, j in ((-1, 0), (1, 0), (0, -1), (0, 1), (-1, -1), (-1, 1), (1, -1), (1, 1)):
        receive(1, i, j)
    for e in range(2):
        settle(e)
    lax.fori_loop(0, spec0.shape[0], second, 0)
    for w in range(out_ref.shape[0]):
        for s in range(res_ref.shape[1]):
            out_ref[w : w + 1, s * 128 : (s + 1) * 128] = res_ref[w, s : s + 1]


def body(initial, images, blocks, lib_index, tile_map, win_x, win_y, win_z):
    count = lax.axis_size("wide")
    f32, bf16 = jnp.float32, jnp.bfloat16
    cams, members = blocks.shape[0], blocks.shape[1]
    columns = initial.shape[1] * initial.shape[2]
    windows_count = win_x.size
    marks = (tile_map + 512 * lib_index).reshape(cams, columns, 1)
    vmem = pl.BlockSpec(memory_space=pltpu.VMEM)
    wide_x, wide_y = 3 * BRICK, 3 * BRICK
    volume, correlation = pl.pallas_call(
        piv_kernel,
        out_shape=(
            jax.ShapeDtypeStruct((2, columns, 128), f32),
            jax.ShapeDtypeStruct((windows_count, DISP * DISP * DISP), f32),
        ),
        in_specs=[pl.BlockSpec(memory_space=pltpu.SMEM)] * 3 + [vmem] * 11,
        out_specs=(vmem, vmem),
        scratch_shapes=[
            pltpu.VMEM((cams, 256, members * 64), bf16),
            pltpu.VMEM((cams, 256, members * 64), bf16),
            pltpu.VMEM((cams, columns, 128), bf16),
            pltpu.VMEM((cams, count * PROJ_ROWS, columns), bf16),
            pltpu.VMEM((cams, columns, count * RATIO_ROWS), bf16),
            pltpu.VMEM((2, columns, 256), bf16),
            pltpu.VMEM((2, count, PROJ_ROWS, 128), f32),
            pltpu.VMEM((2, count, PROJ_ROWS, 128), f32),
            pltpu.VMEM((2, count * RATIO_ROWS, 128), bf16),
            pltpu.VMEM((3, 3, 2, columns + MARK, 128), jnp.int16),
            pltpu.VMEM((2, wide_x, wide_y, 128), bf16),
            pltpu.VMEM((2, wide_x, wide_y, 128), bf16),
            pltpu.VMEM((WIN, KEPT, 256), bf16),
            pltpu.VMEM((WIN, KEPT, 256), bf16),
            pltpu.VMEM((windows_count, WIN, KEPT, 128), f32),
            pltpu.VMEM((WIN + DISP, KEPT, 256), f32),
            pltpu.VMEM((DISP, KEPT, 256), f32),
            pltpu.VMEM((windows_count, DISP * DISP * DISP // 128, 128), f32),
            pltpu.SemaphoreType.DMA((2,)),
            pltpu.SemaphoreType.DMA((2,)),
            pltpu.SemaphoreType.DMA((2,)),
            pltpu.SemaphoreType.DMA((2,)),
            pltpu.SemaphoreType.DMA((2, 2, 2)),
            pltpu.SemaphoreType.DMA((2, 2, 2)),
            pltpu.SemaphoreType.DMA((3, 3, 2)),
        ],
        compiler_params=pltpu.CompilerParams(
            collective_id=0, has_side_effects=True, vmem_limit_bytes=60 * 1024 * 1024
        ),
        name="piv",
    )(
        win_x.reshape(-1),
        win_y.reshape(-1),
        win_z.reshape(-1),
        initial.reshape(2, columns, 128),
        images,
        blocks.transpose(0, 1, 3, 2),
        blocks,
        tile_map.reshape(cams, 1, columns),
        jnp.broadcast_to(marks, (cams, columns, 128)),
        *[jnp.asarray(table) for table in window_tables()],
    )
    return (
        volume.reshape(initial.shape),
        correlation.reshape(1, 1, windows_count, DISP * DISP * DISP),
    )


def solution(mesh):
    placed = (
        P(None, "wide", "narrow", None),
        P(None, None, "wide", "narrow", None),
        P(),
        P(None, "wide", "narrow"),
        P(None, "wide", "narrow"),
        P("wide", "narrow", None),
        P("wide", "narrow", None),
        P("wide", "narrow", None),
    )
    return jax.shard_map(
        body,
        mesh=mesh,
        in_specs=placed,
        out_specs=(P(None, "wide", "narrow", None), P("wide", "narrow", None, None)),
        check_vma=False,
    )
```

```python
import jax
import jax.numpy as jnp
import ml_dtypes
import numpy as np
from jax import lax
from jax.experimental import pallas as pl
from jax.experimental.pallas import tpu as pltpu
from jax.sharding import PartitionSpec as P

MESH = pl.DeviceIdType.MESH
PROJ_ROWS = 24
RATIO_ROWS = 32
CHUNK = 256
WIN = 64
DISP = 16
SWEEPS = 2
SPAN = 80
KEPT = 40
BRICK = 32
MARK = 16
STEPS = 65000.0
TILES = 18


def split(values):
    high = values.astype(jnp.bfloat16)
    return high, (values - high.astype(jnp.float32)).astype(jnp.bfloat16)


def window_tables():
    bf16 = ml_dtypes.bfloat16
    turn = 2.0 * np.pi / WIN

    def parts(table):
        high = table.astype(bf16)
        return high, (table - high.astype(np.float64)).astype(bf16)

    waves = np.arange(WIN // 2 + 1)
    angle = turn * (waves[:, None] * np.arange(SPAN)[None, :] % WIN)
    left = np.zeros((2 * KEPT, SPAN))
    left[: len(waves)] = np.cos(angle)
    left[KEPT : KEPT + len(waves)] = -np.sin(angle)
    left_high, left_low = parts(left)
    left_table = np.zeros((2 * KEPT, 256), bf16)
    for place, table in enumerate((left_high, left_high, left_low)):
        left_table[:, place * SPAN : (place + 1) * SPAN] = table

    angle = turn * (np.arange(128)[:, None] * np.arange(WIN)[None, :] % WIN)
    cosine, sine = np.cos(angle), np.sin(angle)
    right = np.block([[cosine, -sine], [sine, cosine]])
    right_table = np.concatenate(parts(right), axis=1)

    shifts = np.arange(DISP) - DISP // 2
    weight = np.where(waves % (WIN // 2) == 0, 1.0, 2.0)
    angle = turn * shifts[:, None] * waves[None, :]
    inverse_left = np.zeros((2 * DISP, KEPT))
    inverse_left[:DISP, : len(waves)] = weight * np.cos(angle)
    inverse_left[DISP:, : len(waves)] = weight * np.sin(angle)
    angle = turn * np.arange(WIN)[:, None] * shifts[None, :]
    cosine, sine = np.cos(angle), np.sin(angle)
    inverse_right = np.tile(
        np.concatenate([cosine, cosine, -sine, sine, -sine, -sine, -cosine, cosine]),
        (1, 128 // DISP),
    )
    row_weight = np.zeros((KEPT, 128))
    row_weight[: len(waves)] = weight[:, None]
    f32 = np.float32
    return (
        left_table, right_table,
        inverse_left.astype(f32), inverse_right.astype(f32), row_weight.astype(f32),
    )


def wrapped(index, count):
    return jnp.where(index >= count, index - count, index)


def whole(values, reduce):
    return reduce(reduce(values, axis=0, keepdims=True), axis=1, keepdims=True)


def chunks(rows, action, unroll):
    def step(i, carry):
        return action(pl.ds(pl.multiple_of(i * CHUNK, CHUNK), CHUNK), carry)

    return lambda init: lax.fori_loop(0, rows // CHUNK, step, init, unroll=unroll)


def prepare(turned_ref, blocks_ref, ids_ref, marks_ref, fwd_ref, bwd_ref, lib_ref, gather_ref, spread_ref):
    f32, bf16 = jnp.float32, jnp.bfloat16
    count = lax.axis_size("wide")
    me = lax.axis_index("wide")
    cams, members = blocks_ref.shape[0], blocks_ref.shape[1]
    columns = lib_ref.shape[1]

    def strip_rows(ids, stride):
        slot = jnp.floor((ids + 0.5) * (1.0 / TILES))
        owner = slot + (me - count // 2).astype(f32)
        inside = (owner >= 0.0) & (owner < count)
        return jnp.where(inside, owner * stride + (ids - slot * TILES), -1.0)

    def camera(cam, _):
        for m in range(members):
            rows = slice(m % 2 * 128, m % 2 * 128 + 128)
            lanes = slice(m // 2 * 128, m // 2 * 128 + 128)
            fwd_ref[cam, rows, lanes] = turned_ref[cam, m]
            bwd_ref[cam, rows, lanes] = blocks_ref[cam, m]
        ids = strip_rows(ids_ref[cam].astype(f32), PROJ_ROWS)

        def gather(i, _):
            rows = pl.ds(pl.multiple_of(i * 32, 32), 32)
            row = lax.broadcasted_iota(jnp.int32, (32, columns), 0) + i * 32
            gather_ref[cam, rows, :] = jnp.where(row.astype(f32) == ids, 1.0, 0.0).astype(bf16)
            return 0

        lax.fori_loop(0, count * PROJ_ROWS // 32, gather, 0)

        def spread(i, _):
            rows = pl.ds(pl.multiple_of(i * 64, 64), 64)
            mark = marks_ref[cam, rows, :].astype(f32)
            lib = jnp.floor(mark * (1.0 / 512.0))
            lib_ref[cam, rows, :] = lib.astype(bf16)
            ids = strip_rows(mark - lib * 512.0, RATIO_ROWS)
            lane = lax.broadcasted_iota(jnp.int32, (64, 128), 1).astype(f32)
            for part in range(count * RATIO_ROWS // 128):
                here = jnp.where(lane + part * 128.0 == ids, 1.0, 0.0)
                spread_ref[cam, rows, part * 128 : (part + 1) * 128] = here.astype(bf16)
            return 0

        lax.fori_loop(0, columns // 64, spread, 0)
        return 0

    lax.fori_loop(0, cams, camera, 0)


def reconstruct(refs, scratch, barrier_done, finish):
    init_ref, img_ref, fwd_ref, bwd_ref, lib_ref, gather_ref, spread_ref, vol_ref = refs
    cols_ref, part_ref, recv_ref, ratio_ref = scratch[:4]
    part_send, part_recv, ratio_send, ratio_recv = scratch[4:]
    f32, bf16 = jnp.float32, jnp.bfloat16
    count = lax.axis_size("wide")
    me = lax.axis_index("wide")
    cams = fwd_ref.shape[0]
    columns = init_ref.shape[1]

    def by_library(values, cam, rows, table):
        lib = lib_ref[cam, rows, :]
        zero = jnp.zeros_like(values)
        odd = (lib == 1) | (lib == 3) | (lib == 5) | (lib == 7)
        lhs = jnp.concatenate(
            [jnp.where(odd, zero, values), jnp.where(odd, values, zero)], axis=1
        )
        wide = jnp.dot(lhs, table, preferred_element_type=f32)
        pair = lib.astype(f32)
        low = jnp.where(pair < 2, wide[:, 0:128], wide[:, 128:256])
        high = jnp.where(pair < 6, wide[:, 256:384], wide[:, 384:512])
        return jnp.where(pair < 4, low, high)

    def project_rows(e, cam, rows, vol):
        proj = by_library(vol.astype(bf16), cam, rows, fwd_ref[cam])
        high, low = split(proj)
        cols_ref[e, rows, 0:128] = high
        cols_ref[e, rows, 128:256] = low

    def part_copy(e, d, owner):
        target = wrapped(me + d, count)
        return pltpu.make_async_remote_copy(
            src_ref=part_ref.at[e, target],
            dst_ref=recv_ref.at[e, owner],
            send_sem=part_send.at[e],
            recv_sem=part_recv.at[e],
            device_id={"wide": target},
            device_id_type=MESH,
        )

    def strip(e, owner):
        return ratio_ref.at[e, pl.ds(pl.multiple_of(owner * RATIO_ROWS, RATIO_ROWS), RATIO_ROWS)]

    def ratio_copy(e, d, owner):
        return pltpu.make_async_remote_copy(
            src_ref=strip(e, me),
            dst_ref=strip(e, owner),
            send_sem=ratio_send.at[e],
            recv_sem=ratio_recv.at[e],
            device_id={"wide": wrapped(me + d, count)},
            device_id_type=MESH,
        )

    def parts_done(e, sem):
        slots = recv_ref.at[e, pl.ds(0, count - 1)]
        pltpu.make_async_copy(slots, slots, sem.at[e]).wait()

    def ratios_done(e, sem):
        strips = ratio_ref.at[e, pl.ds(0, (count - 1) * RATIO_ROWS)]
        pltpu.make_async_copy(strips, strips, sem.at[e]).wait()

    far_first = sorted(range(1, count), key=lambda d: -(2 - abs(d % 4 - 2)) - (2 - abs(d // 4 - 2)))

    def send_parts(e, cam):
        both = jnp.dot(gather_ref[cam], cols_ref[e], preferred_element_type=f32)
        total = both[:, 0:128] + both[:, 128:256]
        part_ref[e] = total.reshape(count, PROJ_ROWS, 128)[:, 0 : part_ref.shape[2]]
        for d in far_first:
            part_copy(e, d, me).start()

    def send_ratio(e, cam):
        def take(d, total):
            return total + recv_ref[e, wrapped(me + d, count)]

        parts_done(e, part_recv)
        total = lax.fori_loop(1, count, take, part_ref[e, me], unroll=True)
        tiles = img_ref.shape[2] * img_ref.shape[3]
        image = jnp.concatenate([img_ref[e, cam, i] for i in range(img_ref.shape[2])], axis=0)
        ratio = jnp.log(image + 1.0) - jnp.log(total + 1.0)
        ratio = jnp.concatenate([ratio, jnp.zeros((RATIO_ROWS - tiles, 128), f32)], axis=0)
        ratio_ref[e, pl.ds(pl.multiple_of(me * RATIO_ROWS, RATIO_ROWS), RATIO_ROWS), :] = (
            ratio.astype(bf16)
        )
        for d in far_first:
            ratio_copy(e, d, me).start()

    def collect_ratio(e):
        ratios_done(e, ratio_recv)
        parts_done(e, part_send)
        ratios_done(e, ratio_send)

    def updated_rows(e, cam, rows):
        near = jnp.dot(spread_ref[cam, rows, :], ratio_ref[e], preferred_element_type=f32)
        back = by_library(near.astype(bf16), cam, rows, bwd_ref[cam])
        return vol_ref[e, rows, :] * jnp.exp(back)

    for e in range(2):
        def first(rows, _):
            vol = init_ref[e, rows, :]
            vol_ref[e, rows, :] = vol
            project_rows(e, 0, rows, vol)
            return 0

        chunks(columns, first, 2)(0)
        if e == 0:
            barrier_done()
        send_parts(e, 0)

    def round_step(r, _):
        cam = lax.rem(r, cams)
        following = lax.rem(r + 1, cams)
        for e in range(2):
            send_ratio(e, cam)
        for e in range(2):
            collect_ratio(e)

            def both(rows, _):
                vol = updated_rows(e, cam, rows)
                vol_ref[e, rows, :] = vol
                project_rows(e, following, rows, vol)
                return 0

            chunks(columns, both, 4)(0)
            send_parts(e, following)
        return 0

    lax.fori_loop(0, SWEEPS * cams - 1, round_step, 0)
    for e in range(2):
        send_ratio(e, cams - 1)
    for e in range(2):
        collect_ratio(e)

        def final(rows, carry):
            vol = updated_rows(e, cams - 1, rows)
            vol_ref[e, rows, :] = vol
            tiles = vol.reshape(CHUNK // 8, 8, 128)
            return (
                jnp.minimum(carry[0], jnp.min(tiles, axis=0)),
                jnp.maximum(carry[1], jnp.max(tiles, axis=0)),
                carry[2] + jnp.sum(tiles, axis=0),
            )

        low = jnp.full((8, 128), 3.0e38, f32)
        least, largest, total = chunks(columns, final, 2)((low, -low, jnp.zeros((8, 128), f32)))
        finish(e, whole(least, jnp.min), whole(largest, jnp.max), whole(total, jnp.sum))


def exchange(vol_ref, code_ref, high_ref, low_ref, send_own, send_on, arrive, stats):
    f32 = jnp.float32
    wide, narrow = lax.axis_size("wide"), lax.axis_size("narrow")
    me, row = lax.axis_index("wide"), lax.axis_index("narrow")
    columns = vol_ref.shape[1]
    has_wide = {-1: me > 0, 1: me < wide - 1}
    has_narrow = {-1: row > 0, 1: row < narrow - 1}

    def encode(e, least, largest):
        base = jnp.floor(jnp.log(least) * 64.0)
        extent = jnp.floor(jnp.log(largest) * 64.0) - base + 2.0
        scale = (64.0 * STEPS) / extent
        shift = base * (1.0 / 64.0)

        def step(rows, _):
            level = (jnp.log(vol_ref[e, rows, :]) - shift) * scale
            code_ref[1, 1, e, rows, :] = (
                jnp.round(level - STEPS / 2).astype(jnp.int32).astype(jnp.int16)
            )
            return 0

        chunks(columns, step, 1)(0)
        mark = jnp.where(lax.broadcasted_iota(jnp.int32, (MARK, 128), 0) < 8, base, extent)
        code_ref[1, 1, e, columns : columns + MARK, :] = mark.astype(jnp.int32).astype(jnp.int16)

    def side_copy(e, by, place):
        return pltpu.make_async_remote_copy(
            src_ref=code_ref.at[1, 1, e],
            dst_ref=code_ref.at[1 + place, 1, e],
            send_sem=send_own.at[0, (by + 1) // 2, e],
            recv_sem=arrive.at[1 + place, 1, e],
            device_id={"wide": me + by},
            device_id_type=MESH,
        )

    def row_copy(e, column, by, place):
        sem = send_own.at[1, (by + 1) // 2, e]
        if column != 0:
            sem = send_on.at[(column + 1) // 2, (by + 1) // 2, e]
        return pltpu.make_async_remote_copy(
            src_ref=code_ref.at[1 + column, 1, e],
            dst_ref=code_ref.at[1 + column, 1 + place, e],
            send_sem=sem,
            recv_sem=arrive.at[1 + column, 1 + place, e],
            device_id={"narrow": row + by},
            device_id_type=MESH,
        )

    def send_rows(e):
        for by in (-1, 1):
            @pl.when(has_narrow[by])
            def _():
                row_copy(e, 0, by, -by).start()

    def send_sides(e):
        for by in (-1, 1):
            @pl.when(has_wide[by])
            def _():
                side_copy(e, by, -by).start()

    def pass_on(e):
        for side in (-1, 1):
            @pl.when(has_wide[side])
            def _():
                side_copy(e, side, side).wait_recv()
                for by in (-1, 1):
                    @pl.when(has_narrow[by])
                    def _():
                        row_copy(e, side, by, -by).start()

    def settle(e):
        for by in (-1, 1):
            @pl.when(has_narrow[by])
            def _():
                row_copy(e, 0, by, -by).wait_send()

            @pl.when(has_wide[by])
            def _():
                side_copy(e, by, -by).wait_send()
                for up in (-1, 1):
                    @pl.when(has_narrow[up])
                    def _():
                        row_copy(e, by, up, -up).wait_send()

    def place(e, i, j, values_of):
        def step(x, _):
            high, low = split(values_of(x))
            high_ref[e, (1 + i) * BRICK + x, (1 + j) * BRICK : (2 + j) * BRICK, :] = high
            low_ref[e, (1 + i) * BRICK + x, (1 + j) * BRICK : (2 + j) * BRICK, :] = low
            return 0

        lax.fori_loop(0, BRICK, step, 0, unroll=4)

    def place_own(e):
        place(e, 0, 0, lambda x: vol_ref[
            e, pl.ds(pl.multiple_of(x * BRICK, BRICK), BRICK), :] - stats[e])

    def place_code(e, i, j):
        mark = code_ref[1 + i, 1 + j, e, columns : columns + MARK, :].astype(f32)
        step = mark[8:9] * (1.0 / (64.0 * STEPS))
        shift = mark[0:1] * (1.0 / 64.0) + step * (STEPS / 2)

        def values_of(x):
            rows = pl.ds(pl.multiple_of(x * BRICK, BRICK), BRICK)
            code = code_ref[1 + i, 1 + j, e, rows, :].astype(f32)
            return jnp.exp(code * step + shift) - stats[e]

        place(e, i, j, values_of)

    def receive(e, i, j):
        here = has_narrow[j] if j else None
        if i:
            here = has_wide[i] if here is None else here & has_wide[i]

        @pl.when(here)
        def _():
            if j:
                row_copy(e, i, j, j).wait_recv()
            place_code(e, i, j)

        @pl.when(jnp.logical_not(here))
        def _():
            place(e, i, j, lambda x: jnp.zeros((BRICK, 128), f32) - stats[e])

    return encode, send_rows, send_sides, pass_on, settle, place_own, receive


def windows(place_ref, tables, high_ref, low_ref, mids, specs, corr_ref, res_ref):
    left_ref, right_ref, inv_left_ref, inv_right_ref, weight_ref = tables
    mid_high, mid_low = mids
    spec0, spec1 = specs
    f32, bf16 = jnp.float32, jnp.bfloat16
    half = DISP // 2
    wide_y = high_ref.shape[2]

    def transform(w, e, store):
        start_x, start_y, start_z = place_ref[0][w], place_ref[1][w], place_ref[2][w]
        lead = jnp.where(start_y >= 16, start_y - 16, start_y)
        later = lax.broadcasted_iota(jnp.int32, (SPAN, 128), 0) * 0 + start_y >= 16
        lane = lax.broadcasted_iota(jnp.int32, (2 * KEPT, 256), 1)
        spot = lax.rem(lane, SPAN)
        keep = (spot >= lead) & (spot < lead + WIN) & (lane < 3 * SPAN)
        left = jnp.where(keep, left_ref[...].astype(f32), 0.0).astype(bf16)
        row = lax.rem(lax.broadcasted_iota(jnp.int32, (256, 256), 0), 128)
        keep = (row >= start_z) & (row < start_z + WIN)
        right = jnp.where(keep, right_ref[...].astype(f32), 0.0).astype(bf16)

        def turn_y(i, _):
            sides = []
            for j in range(2):
                high, low = high_ref[e, start_x + 2 * i + j], low_ref[e, start_x + 2 * i + j]
                high = jnp.where(later, high[wide_y - SPAN :], high[:SPAN])
                low = jnp.where(later, low[wide_y - SPAN :], low[:SPAN])
                sides.append(jnp.concatenate([high, low, high, high[0:16]], axis=0))
            mixed = jnp.dot(left, jnp.concatenate(sides, axis=1), preferred_element_type=f32)
            high, low = split(mixed)
            for j in range(2):
                lanes = slice(j * 128, (j + 1) * 128)
                for source, target in ((high, mid_high), (low, mid_low)):
                    target[2 * i + j, :, 0:128] = source[0:KEPT, lanes]
                    target[2 * i + j, :, 128:256] = source[KEPT : 2 * KEPT, lanes]
            return 0

        lax.fori_loop(0, WIN // 2, turn_y, 0, unroll=4)

        def turn_z(i, _):
            xs = pl.ds(i * 16, 16)
            high = mid_high[xs].reshape(16 * KEPT, 256)
            low = mid_low[xs].reshape(16 * KEPT, 256)
            value = jnp.dot(high, right, preferred_element_type=f32)
            rest = jnp.dot(low, right[:, 0:128], preferred_element_type=f32)
            value = value[:, 0:128] + (value[:, 128:256] + rest)
            if e == 1:
                value = jnp.concatenate([value, pltpu.roll(value, WIN, 1)], axis=1)
            store(i * 16, value.reshape(16, KEPT, 128 * (e + 1)))
            return 0

        lax.fori_loop(0, WIN // 16, turn_z, 0)

    def first(w, _):
        def store(x, value):
            spec0[w, pl.ds(x, 16)] = value

        transform(w, 0, store)
        return 0

    def second(w, _):
        def store(x, value):
            spec1[pl.ds(x + half, 16)] = value

        transform(w, 1, store)

        def sums(x, carry):
            return carry[0] + spec0[w, x, 0:8, :], carry[1] + spec1[x + half, 0:8, :]

        mean0, mean1 = lax.fori_loop(
            0, WIN, sums, (jnp.zeros((8, 128), f32), jnp.zeros((8, 256), f32)), unroll=4
        )
        lane = lax.broadcasted_iota(jnp.int32, (8, 256), 1)
        row = lax.broadcasted_iota(jnp.int32, (8, 256), 0)
        mean1 = jnp.where((row == 0) & ((lane == 0) | (lane == 192)), mean1 * (1.0 / WIN), 0.0)
        lane = lax.broadcasted_iota(jnp.int32, (8, 128), 1)
        row = lax.broadcasted_iota(jnp.int32, (8, 128), 0)
        mean0 = jnp.where((row == 0) & (lane == 0), mean0 * (1.0 / WIN), 0.0)

        def centre(x, carry):
            spec0[w, x, 0:8, :] = spec0[w, x, 0:8, :] - mean0
            spec1[x + half, 0:8, :] = spec1[x + half, 0:8, :] - mean1
            value0, value1 = spec0[w, x], spec1[x + half, :, 0:128]
            return carry[0] + value0 * value0, carry[1] + value1 * value1

        zero = jnp.zeros((KEPT, 128), f32)
        power0, power1 = lax.fori_loop(0, WIN, centre, (zero, zero), unroll=2)
        count = 1.0 / (WIN * WIN * WIN**3)
        rms0 = jnp.sqrt(whole(power0 * weight_ref[...], jnp.sum) * count + 1e-6)
        rms1 = jnp.sqrt(whole(power1 * weight_ref[...], jnp.sum) * count + 1e-6)
        spec1[0:half] = spec1[WIN : WIN + half]
        spec1[WIN + half : WIN + DISP] = spec1[half:DISP]

        def group(g, _):
            first = lax.div(g, KEPT // 8) * half
            rows = pl.ds(pl.multiple_of((g - lax.div(g, KEPT // 8) * (KEPT // 8)) * 8, 8), 8)

            def block(i, carry):
                carry = list(carry)
                base = i * 4
                ones = [spec0[w, base + j, rows, :] for j in range(4)]
                plain = [spec1[base + first + j, rows, 0:128] for j in range(half + 3)]
                swapped = [spec1[base + first + j, rows, 128:256] for j in range(half + 3)]
                for j in range(4):
                    for s in range(half):
                        carry[s] = carry[s] + ones[j] * plain[j + s]
                        carry[half + s] = carry[half + s] + ones[j] * swapped[j + s]
                return tuple(carry)

            zero = jnp.zeros((8, 128), f32)
            done = lax.fori_loop(0, WIN // 4, block, (zero,) * DISP)
            for s in range(half):
                corr_ref[first + s, rows, 0:128] = done[s]
                corr_ref[first + s, rows, 128:256] = done[half + s]
            return 0

        lax.fori_loop(0, 2 * (KEPT // 8), group, 0)

        highest = lax.Precision.HIGHEST
        turned = []
        for s in range(DISP):
            value = jnp.dot(
                inv_left_ref[...], corr_ref[s], precision=highest, preferred_element_type=f32
            )
            turned.append(jnp.concatenate([value[0:DISP], value[DISP : 2 * DISP]], axis=1))
        final = jnp.dot(
            jnp.concatenate(turned, axis=0), inv_right_ref[...],
            precision=highest, preferred_element_type=f32,
        )
        scale = 1.0 / (WIN * WIN * WIN**1.5)
        final = (final * (scale / (rms0 * rms1))).reshape(DISP * DISP // 8, 8, 128)
        lane = lax.broadcasted_iota(jnp.int32, final.shape, 2)
        row = lax.broadcasted_iota(jnp.int32, final.shape, 1)
        own = (lane >= row * DISP) & (lane < row * DISP + DISP)
        final = jnp.sum(jnp.where(own, final, 0.0), axis=1)
        res_ref[w] = final
        return 0

    return first, second


def piv_kernel(
    win_x_ref, win_y_ref, win_z_ref, init_ref, img_ref, turned_ref, blocks_ref, ids_ref, marks_ref,
    left_ref, right_ref, inv_left_ref, inv_right_ref, weight_ref,
    vol_ref, out_ref,
    fwd_ref, bwd_ref, lib_ref, gather_ref, spread_ref,
    cols_ref, part_ref, recv_ref, ratio_ref,
    code_ref, high_ref, low_ref, mid_high, mid_low, spec0, spec1, corr_ref, res_ref,
    part_send, part_recv, ratio_send, ratio_recv, send_own, send_on, arrive,
):
    count, depth = lax.axis_size("wide"), lax.axis_size("narrow")
    me, row = lax.axis_index("wide"), lax.axis_index("narrow")
    barrier = pltpu.get_barrier_semaphore()

    def greet(d, _):
        pl.semaphore_signal(
            barrier, inc=1, device_id={"wide": wrapped(me + d, count)}, device_id_type=MESH
        )
        return 0

    lax.fori_loop(1, count, greet, 0)
    for by in (1, depth - 1):
        pl.semaphore_signal(
            barrier, inc=1, device_id={"narrow": wrapped(row + by, depth)}, device_id_type=MESH
        )

    def barrier_done():
        pl.semaphore_wait(barrier, count + 1)

    prepare(
        turned_ref, blocks_ref, ids_ref, marks_ref,
        fwd_ref, bwd_ref, lib_ref, gather_ref, spread_ref,
    )
    stats = {}
    encode, send_rows, send_sides, pass_on, settle, place_own, receive = exchange(
        vol_ref, code_ref, high_ref, low_ref, send_own, send_on, arrive, stats
    )

    def finish(e, least, largest, total):
        stats[e] = total * (1.0 / (vol_ref.shape[1] * 128))
        encode(e, least, largest)
        if e == 0:
            send_sides(e)
        send_rows(e)

    reconstruct(
        (init_ref, img_ref, fwd_ref, bwd_ref, lib_ref, gather_ref, spread_ref, vol_ref),
        (cols_ref, part_ref, recv_ref, ratio_ref, part_send, part_recv, ratio_send, ratio_recv),
        barrier_done,
        finish,
    )
    place_own(0)
    pass_on(0)
    send_sides(1)
    place_own(1)
    for i, j in ((-1, 0), (1, 0), (0, -1), (0, 1)):
        receive(0, i, j)
    pass_on(1)
    for i, j in ((-1, -1), (-1, 1), (1, -1), (1, 1)):
        receive(0, i, j)
    first, second = windows(
        (win_x_ref, win_y_ref, win_z_ref),
        (left_ref, right_ref, inv_left_ref, inv_right_ref, weight_ref),
        high_ref, low_ref, (mid_high, mid_low), (spec0, spec1), corr_ref, res_ref,
    )
    lax.fori_loop(0, spec0.shape[0], first, 0)
    for i, j in ((-1, 0), (1, 0), (0, -1), (0, 1), (-1, -1), (-1, 1), (1, -1), (1, 1)):
        receive(1, i, j)
    for e in range(2):
        settle(e)
    lax.fori_loop(0, spec0.shape[0], second, 0)
    for w in range(out_ref.shape[0]):
        for s in range(res_ref.shape[1]):
            out_ref[w : w + 1, s * 128 : (s + 1) * 128] = res_ref[w, s : s + 1]


def body(initial, images, blocks, lib_index, tile_map, win_x, win_y, win_z):
    count = lax.axis_size("wide")
    f32, bf16 = jnp.float32, jnp.bfloat16
    cams, members = blocks.shape[0], blocks.shape[1]
    columns = initial.shape[1] * initial.shape[2]
    windows_count = win_x.size
    marks = (tile_map + 512 * lib_index).reshape(cams, columns, 1)
    vmem = pl.BlockSpec(memory_space=pltpu.VMEM)
    wide_x, wide_y = 3 * BRICK, 3 * BRICK
    volume, correlation = pl.pallas_call(
        piv_kernel,
        out_shape=(
            jax.ShapeDtypeStruct((2, columns, 128), f32),
            jax.ShapeDtypeStruct((windows_count, DISP * DISP * DISP), f32),
        ),
        in_specs=[pl.BlockSpec(memory_space=pltpu.SMEM)] * 3 + [vmem] * 11,
        out_specs=(vmem, vmem),
        scratch_shapes=[
            pltpu.VMEM((cams, 256, members * 64), bf16),
            pltpu.VMEM((cams, 256, members * 64), bf16),
            pltpu.VMEM((cams, columns, 128), bf16),
            pltpu.VMEM((cams, count * PROJ_ROWS, columns), bf16),
            pltpu.VMEM((cams, columns, count * RATIO_ROWS), bf16),
            pltpu.VMEM((2, columns, 256), bf16),
            pltpu.VMEM((2, count, TILES, 128), f32),
            pltpu.VMEM((2, count, TILES, 128), f32),
            pltpu.VMEM((2, count * RATIO_ROWS, 128), bf16),
            pltpu.VMEM((3, 3, 2, columns + MARK, 128), jnp.int16),
            pltpu.VMEM((2, wide_x, wide_y, 128), bf16),
            pltpu.VMEM((2, wide_x, wide_y, 128), bf16),
            pltpu.VMEM((WIN, KEPT, 256), bf16),
            pltpu.VMEM((WIN, KEPT, 256), bf16),
            pltpu.VMEM((windows_count, WIN, KEPT, 128), f32),
            pltpu.VMEM((WIN + DISP, KEPT, 256), f32),
            pltpu.VMEM((DISP, KEPT, 256), f32),
            pltpu.VMEM((windows_count, DISP * DISP * DISP // 128, 128), f32),
            pltpu.SemaphoreType.DMA((2,)),
            pltpu.SemaphoreType.DMA((2,)),
            pltpu.SemaphoreType.DMA((2,)),
            pltpu.SemaphoreType.DMA((2,)),
            pltpu.SemaphoreType.DMA((2, 2, 2)),
            pltpu.SemaphoreType.DMA((2, 2, 2)),
            pltpu.SemaphoreType.DMA((3, 3, 2)),
        ],
        compiler_params=pltpu.CompilerParams(
            collective_id=0, has_side_effects=True, vmem_limit_bytes=60 * 1024 * 1024
        ),
        name="piv",
    )(
        win_x.reshape(-1),
        win_y.reshape(-1),
        win_z.reshape(-1),
        initial.reshape(2, columns, 128),
        images,
        blocks.transpose(0, 1, 3, 2),
        blocks,
        tile_map.reshape(cams, 1, columns),
        jnp.broadcast_to(marks, (cams, columns, 128)),
        *[jnp.asarray(table) for table in window_tables()],
    )
    return (
        volume.reshape(initial.shape),
        correlation.reshape(1, 1, windows_count, DISP * DISP * DISP),
    )


def solution(mesh):
    placed = (
        P(None, "wide", "narrow", None),
        P(None, None, "wide", "narrow", None),
        P(),
        P(None, "wide", "narrow"),
        P(None, "wide", "narrow"),
        P("wide", "narrow", None),
        P("wide", "narrow", None),
        P("wide", "narrow", None),
    )
    return jax.shard_map(
        body,
        mesh=mesh,
        in_specs=placed,
        out_specs=(P(None, "wide", "narrow", None), P("wide", "narrow", None, None)),
        check_vma=False,
    )
```

```python
import jax
import jax.numpy as jnp
import ml_dtypes
import numpy as np
from jax import lax
from jax.experimental import pallas as pl
from jax.experimental.pallas import tpu as pltpu
from jax.sharding import PartitionSpec as P

MESH = pl.DeviceIdType.MESH
PROJ_ROWS = 24
RATIO_ROWS = 32
CHUNK = 256
WIN = 64
DISP = 16
SWEEPS = 2
SPAN = 80
KEPT = 40
BRICK = 32
MARK = 16
STEPS = 65000.0
TILES = 18


def split(values):
    high = values.astype(jnp.bfloat16)
    return high, (values - high.astype(jnp.float32)).astype(jnp.bfloat16)


def window_tables():
    bf16 = ml_dtypes.bfloat16
    turn = 2.0 * np.pi / WIN

    def parts(table):
        high = table.astype(bf16)
        return high, (table - high.astype(np.float64)).astype(bf16)

    waves = np.arange(WIN // 2 + 1)
    angle = turn * (waves[:, None] * np.arange(SPAN)[None, :] % WIN)
    left = np.zeros((2 * KEPT, SPAN))
    left[: len(waves)] = np.cos(angle)
    left[KEPT : KEPT + len(waves)] = -np.sin(angle)
    left_high, left_low = parts(left)
    left_table = np.zeros((2 * KEPT, 256), bf16)
    for place, table in enumerate((left_high, left_high, left_low)):
        left_table[:, place * SPAN : (place + 1) * SPAN] = table

    angle = turn * (np.arange(128)[:, None] * np.arange(WIN)[None, :] % WIN)
    cosine, sine = np.cos(angle), np.sin(angle)
    right = np.block([[cosine, -sine], [sine, cosine]])
    right_table = np.concatenate(parts(right), axis=1)

    shifts = np.arange(DISP) - DISP // 2
    weight = np.where(waves % (WIN // 2) == 0, 1.0, 2.0)
    angle = turn * shifts[:, None] * waves[None, :]
    inverse_left = np.zeros((2 * DISP, KEPT))
    inverse_left[:DISP, : len(waves)] = weight * np.cos(angle)
    inverse_left[DISP:, : len(waves)] = weight * np.sin(angle)
    angle = turn * np.arange(WIN)[:, None] * shifts[None, :]
    cosine, sine = np.cos(angle), np.sin(angle)
    inverse_right = np.stack([
        np.tile(
            np.concatenate([
                cosine + sine, cosine - sine, even * -sine, odd * -sine,
                cosine - sine, -sine - cosine, even * -cosine, odd * -cosine,
            ]) + 0.0,
            (1, 128 // DISP),
        )
        for even, odd in ((1, 0), (0, 1))
    ])
    row_weight = np.zeros((KEPT, 128))
    row_weight[: len(waves)] = weight[:, None]
    f32 = np.float32
    return (
        left_table, right_table,
        inverse_left.astype(f32), inverse_right.astype(f32), row_weight.astype(f32),
    )


def wrapped(index, count):
    return jnp.where(index >= count, index - count, index)


def whole(values, reduce):
    return reduce(reduce(values, axis=0, keepdims=True), axis=1, keepdims=True)


def chunks(rows, action, unroll):
    def step(i, carry):
        return action(pl.ds(pl.multiple_of(i * CHUNK, CHUNK), CHUNK), carry)

    return lambda init: lax.fori_loop(0, rows // CHUNK, step, init, unroll=unroll)


def prepare(
    turned_ref, blocks_ref, ids_ref, marks_ref, fwd_ref, bwd_ref, lib_ref, gather_ref, spread_ref
):
    f32, bf16 = jnp.float32, jnp.bfloat16
    count = lax.axis_size("wide")
    me = lax.axis_index("wide")
    cams, members = blocks_ref.shape[0], blocks_ref.shape[1]
    columns = lib_ref.shape[1]

    def strip_rows(ids, stride):
        slot = jnp.floor((ids + 0.5) * (1.0 / TILES))
        owner = slot + (me - count // 2).astype(f32)
        inside = (owner >= 0.0) & (owner < count)
        return jnp.where(inside, owner * stride + (ids - slot * TILES), -1.0)

    def camera(cam):
        for m in range(members):
            rows = slice(m % 2 * 128, m % 2 * 128 + 128)
            lanes = slice(m // 2 * 128, m // 2 * 128 + 128)
            fwd_ref[cam, rows, lanes] = turned_ref[cam, m]
            bwd_ref[cam, rows, lanes] = blocks_ref[cam, m]
        mark = ids_ref[cam : cam + 1, :].astype(f32)
        ids = strip_rows(mark - jnp.floor(mark * (1.0 / 512.0)) * 512.0, PROJ_ROWS)

        def gather(i, _):
            rows = pl.ds(pl.multiple_of(i * 32, 32), 32)
            row = lax.broadcasted_iota(jnp.int32, (32, columns), 0) + i * 32
            gather_ref[cam, rows, :] = jnp.where(row.astype(f32) == ids, 1.0, 0.0).astype(bf16)
            return 0

        lax.fori_loop(0, count * PROJ_ROWS // 32, gather, 0)

        def spread(i, _):
            rows = pl.ds(pl.multiple_of(i * 64, 64), 64)
            mark = marks_ref[cam, rows, :].astype(f32)
            lib = jnp.floor(mark * (1.0 / 512.0))
            lib_ref[cam, rows, :] = lib.astype(bf16)
            ids = strip_rows(mark - lib * 512.0, RATIO_ROWS)
            lane = lax.broadcasted_iota(jnp.int32, (64, 128), 1).astype(f32)
            for part in range(count * RATIO_ROWS // 128):
                here = jnp.where(lane + part * 128.0 == ids, 1.0, 0.0)
                spread_ref[cam, rows, part * 128 : (part + 1) * 128] = here.astype(bf16)
            return 0

        lax.fori_loop(0, columns // 64, spread, 0)

    for cam in range(cams):
        camera(cam)


def reconstruct(refs, scratch, barrier_done, finish):
    init_ref, img_ref, fwd_ref, bwd_ref, lib_ref, gather_ref, spread_ref, vol_ref = refs
    cols_ref, part_ref, recv_ref, ratio_ref = scratch[:4]
    part_send, part_recv, ratio_send, ratio_recv = scratch[4:]
    f32, bf16 = jnp.float32, jnp.bfloat16
    count = lax.axis_size("wide")
    me = lax.axis_index("wide")
    cams = fwd_ref.shape[0]
    columns = init_ref.shape[1]

    def by_library(values, cam, rows, table):
        lib = lib_ref[cam, rows, :]
        zero = jnp.zeros_like(values)
        odd = (lib == 1) | (lib == 3) | (lib == 5) | (lib == 7)
        lhs = jnp.concatenate(
            [jnp.where(odd, zero, values), jnp.where(odd, values, zero)], axis=1
        )
        wide = jnp.dot(lhs, table, preferred_element_type=f32)
        pair = lib.astype(f32)
        low = jnp.where(pair < 2, wide[:, 0:128], wide[:, 128:256])
        high = jnp.where(pair < 6, wide[:, 256:384], wide[:, 384:512])
        return jnp.where(pair < 4, low, high)

    def project_rows(e, cam, rows, vol):
        proj = by_library(vol.astype(bf16), cam, rows, fwd_ref[cam])
        high, low = split(proj)
        cols_ref[e, rows, 0:128] = high
        cols_ref[e, rows, 128:256] = low

    def part_copy(e, d, owner):
        target = wrapped(me + d, count)
        return pltpu.make_async_remote_copy(
            src_ref=part_ref.at[e, target],
            dst_ref=recv_ref.at[e, owner],
            send_sem=part_send.at[e],
            recv_sem=part_recv.at[e],
            device_id={"wide": target},
            device_id_type=MESH,
        )

    def strip(e, owner):
        return ratio_ref.at[e, pl.ds(pl.multiple_of(owner * RATIO_ROWS, RATIO_ROWS), RATIO_ROWS)]

    def ratio_copy(e, d, owner):
        return pltpu.make_async_remote_copy(
            src_ref=strip(e, me),
            dst_ref=strip(e, owner),
            send_sem=ratio_send.at[e],
            recv_sem=ratio_recv.at[e],
            device_id={"wide": wrapped(me + d, count)},
            device_id_type=MESH,
        )

    def parts_done(e, sem):
        slots = recv_ref.at[e, pl.ds(0, count - 1)]
        pltpu.make_async_copy(slots, slots, sem.at[e]).wait()

    def ratios_done(e, sem):
        strips = ratio_ref.at[e, pl.ds(0, (count - 1) * RATIO_ROWS)]
        pltpu.make_async_copy(strips, strips, sem.at[e]).wait()

    far_first = sorted(range(1, count), key=lambda d: -(2 - abs(d % 4 - 2)) - (2 - abs(d // 4 - 2)))

    def send_parts(e, cam):
        both = jnp.dot(gather_ref[cam], cols_ref[e], preferred_element_type=f32)
        total = both[:, 0:128] + both[:, 128:256]
        part_ref[e] = total.reshape(count, PROJ_ROWS, 128)[:, 0 : part_ref.shape[2]]
        for d in far_first:
            part_copy(e, d, me).start()

    def send_ratio(e, cam):
        def take(d, total):
            return total + recv_ref[e, wrapped(me + d, count)]

        parts_done(e, part_recv)
        total = lax.fori_loop(1, count, take, part_ref[e, me], unroll=True)
        tiles = img_ref.shape[2] * img_ref.shape[3]
        image = jnp.concatenate([img_ref[e, cam, i] for i in range(img_ref.shape[2])], axis=0)
        ratio = jnp.log(image + 1.0) - jnp.log(total + 1.0)
        ratio = jnp.concatenate([ratio, jnp.zeros((RATIO_ROWS - tiles, 128), f32)], axis=0)
        ratio_ref[e, pl.ds(pl.multiple_of(me * RATIO_ROWS, RATIO_ROWS), RATIO_ROWS), :] = (
            ratio.astype(bf16)
        )
        for d in far_first:
            ratio_copy(e, d, me).start()

    def collect_ratio(e):
        ratios_done(e, ratio_recv)
        parts_done(e, part_send)
        ratios_done(e, ratio_send)

    def updated_rows(e, cam, rows):
        near = jnp.dot(spread_ref[cam, rows, :], ratio_ref[e], preferred_element_type=f32)
        back = by_library(near.astype(bf16), cam, rows, bwd_ref[cam])
        return vol_ref[e, rows, :] * jnp.exp(back)

    for e in range(2):
        def first(rows, _):
            vol = init_ref[e, rows, :]
            vol_ref[e, rows, :] = vol
            project_rows(e, 0, rows, vol)
            return 0

        chunks(columns, first, 2)(0)
        if e == 0:
            barrier_done()
        send_parts(e, 0)

    def round_step(r, _):
        cam = lax.rem(r, cams)
        following = lax.rem(r + 1, cams)
        for e in range(2):
            send_ratio(e, cam)
        for e in range(2):
            collect_ratio(e)

            def both(rows, _):
                vol = updated_rows(e, cam, rows)
                vol_ref[e, rows, :] = vol
                project_rows(e, following, rows, vol)
                return 0

            chunks(columns, both, 4)(0)
            send_parts(e, following)
        return 0

    lax.fori_loop(0, SWEEPS * cams - 1, round_step, 0)
    for e in range(2):
        send_ratio(e, cams - 1)
    for e in range(2):
        collect_ratio(e)

        def final(rows, carry):
            vol = updated_rows(e, cams - 1, rows)
            vol_ref[e, rows, :] = vol
            tiles = vol.reshape(CHUNK // 8, 8, 128)
            return (
                jnp.minimum(carry[0], jnp.min(tiles, axis=0)),
                jnp.maximum(carry[1], jnp.max(tiles, axis=0)),
                carry[2] + jnp.sum(tiles, axis=0),
            )

        low = jnp.full((8, 128), 3.0e38, f32)
        least, largest, total = chunks(columns, final, 2)((low, -low, jnp.zeros((8, 128), f32)))
        finish(e, whole(least, jnp.min), whole(largest, jnp.max), whole(total, jnp.sum))


def exchange(vol_ref, code_ref, high_ref, low_ref, send_own, send_on, arrive, stats):
    f32 = jnp.float32
    wide, narrow = lax.axis_size("wide"), lax.axis_size("narrow")
    me, row = lax.axis_index("wide"), lax.axis_index("narrow")
    columns = vol_ref.shape[1]
    has_wide = {-1: me > 0, 1: me < wide - 1}
    has_narrow = {-1: row > 0, 1: row < narrow - 1}

    def encode(e, least, largest):
        base = jnp.floor(jnp.log(least) * 64.0)
        extent = jnp.floor(jnp.log(largest) * 64.0) - base + 2.0
        scale = (64.0 * STEPS) / extent
        shift = base * (1.0 / 64.0)

        def step(rows, _):
            level = (jnp.log(vol_ref[e, rows, :]) - shift) * scale
            code_ref[1, 1, e, rows, :] = (
                jnp.round(level - STEPS / 2).astype(jnp.int32).astype(jnp.int16)
            )
            return 0

        chunks(columns, step, 1)(0)
        mark = jnp.where(lax.broadcasted_iota(jnp.int32, (MARK, 128), 0) < 8, base, extent)
        code_ref[1, 1, e, columns : columns + MARK, :] = mark.astype(jnp.int32).astype(jnp.int16)

    def side_copy(e, by, place):
        return pltpu.make_async_remote_copy(
            src_ref=code_ref.at[1, 1, e],
            dst_ref=code_ref.at[1 + place, 1, e],
            send_sem=send_own.at[0, (by + 1) // 2, e],
            recv_sem=arrive.at[1 + place, 1, e],
            device_id={"wide": me + by},
            device_id_type=MESH,
        )

    def row_copy(e, column, by, place):
        sem = send_own.at[1, (by + 1) // 2, e]
        if column != 0:
            sem = send_on.at[(column + 1) // 2, (by + 1) // 2, e]
        return pltpu.make_async_remote_copy(
            src_ref=code_ref.at[1 + column, 1, e],
            dst_ref=code_ref.at[1 + column, 1 + place, e],
            send_sem=sem,
            recv_sem=arrive.at[1 + column, 1 + place, e],
            device_id={"narrow": row + by},
            device_id_type=MESH,
        )

    def send_rows(e):
        for by in (-1, 1):
            @pl.when(has_narrow[by])
            def _():
                row_copy(e, 0, by, -by).start()

    def send_sides(e):
        for by in (-1, 1):
            @pl.when(has_wide[by])
            def _():
                side_copy(e, by, -by).start()

    def pass_on(e):
        for side in (-1, 1):
            @pl.when(has_wide[side])
            def _():
                side_copy(e, side, side).wait_recv()
                for by in (-1, 1):
                    @pl.when(has_narrow[by])
                    def _():
                        row_copy(e, side, by, -by).start()

    def settle(e):
        for by in (-1, 1):
            @pl.when(has_narrow[by])
            def _():
                row_copy(e, 0, by, -by).wait_send()

            @pl.when(has_wide[by])
            def _():
                side_copy(e, by, -by).wait_send()
                for up in (-1, 1):
                    @pl.when(has_narrow[up])
                    def _():
                        row_copy(e, by, up, -up).wait_send()

    def place(e, i, j, values_of):
        def step(x, _):
            high, low = split(values_of(x))
            high_ref[e, (1 + i) * BRICK + x, (1 + j) * BRICK : (2 + j) * BRICK, :] = high
            low_ref[e, (1 + i) * BRICK + x, (1 + j) * BRICK : (2 + j) * BRICK, :] = low
            return 0

        lax.fori_loop(0, BRICK, step, 0, unroll=4)

    def place_own(e):
        place(e, 0, 0, lambda x: vol_ref[
            e, pl.ds(pl.multiple_of(x * BRICK, BRICK), BRICK), :] - stats[e])

    def place_code(e, i, j):
        mark = code_ref[1 + i, 1 + j, e, columns : columns + MARK, :].astype(f32)
        step = mark[8:9] * (1.0 / (64.0 * STEPS))
        shift = mark[0:1] * (1.0 / 64.0) + step * (STEPS / 2)

        def values_of(x):
            rows = pl.ds(pl.multiple_of(x * BRICK, BRICK), BRICK)
            code = code_ref[1 + i, 1 + j, e, rows, :].astype(f32)
            return jnp.exp(code * step + shift) - stats[e]

        place(e, i, j, values_of)

    def receive(e, i, j):
        here = has_narrow[j] if j else None
        if i:
            here = has_wide[i] if here is None else here & has_wide[i]

        @pl.when(here)
        def _():
            if j:
                row_copy(e, i, j, j).wait_recv()
            place_code(e, i, j)

        @pl.when(jnp.logical_not(here))
        def _():
            place(e, i, j, lambda x: jnp.zeros((BRICK, 128), f32) - stats[e])

    return encode, send_rows, send_sides, pass_on, settle, place_own, receive


def windows(place_ref, tables, high_ref, low_ref, mids, specs, corr_ref, res_ref):
    left_ref, right_ref, inv_left_ref, inv_right_ref, weight_ref = tables
    mid_high, mid_low = mids
    spec0, spec1 = specs
    f32, bf16 = jnp.float32, jnp.bfloat16
    half = DISP // 2
    wide_y = high_ref.shape[2]

    def transform(w, e, store):
        start_x, start_y, start_z = place_ref[0][w], place_ref[1][w], place_ref[2][w]
        lead = jnp.where(start_y >= 16, start_y - 16, start_y)
        later = lax.broadcasted_iota(jnp.int32, (SPAN, 128), 0) * 0 + start_y >= 16
        lane = lax.broadcasted_iota(jnp.int32, (2 * KEPT, 256), 1)
        spot = lax.rem(lane, SPAN)
        keep = (spot >= lead) & (spot < lead + WIN) & (lane < 3 * SPAN)
        left = jnp.where(keep, left_ref[...].astype(f32), 0.0).astype(bf16)
        row = lax.rem(lax.broadcasted_iota(jnp.int32, (256, 256), 0), 128)
        keep = (row >= start_z) & (row < start_z + WIN)
        right = jnp.where(keep, right_ref[...].astype(f32), 0.0).astype(bf16)

        def turn_y(i, _):
            sides = []
            for j in range(2):
                high, low = high_ref[e, start_x + 2 * i + j], low_ref[e, start_x + 2 * i + j]
                high = jnp.where(later, high[wide_y - SPAN :], high[:SPAN])
                low = jnp.where(later, low[wide_y - SPAN :], low[:SPAN])
                sides.append(jnp.concatenate([high, low, high, high[0:16]], axis=0))
            mixed = jnp.dot(left, jnp.concatenate(sides, axis=1), preferred_element_type=f32)
            high, low = split(mixed)
            for j in range(2):
                lanes = slice(j * 128, (j + 1) * 128)
                for source, target in ((high, mid_high), (low, mid_low)):
                    target[2 * i + j, :, 0:128] = source[0:KEPT, lanes]
                    target[2 * i + j, :, 128:256] = source[KEPT : 2 * KEPT, lanes]
            return 0

        lax.fori_loop(0, WIN // 2, turn_y, 0, unroll=4)

        def turn_z(i, _):
            xs = pl.ds(i * 16, 16)
            high = mid_high[xs].reshape(16 * KEPT, 256)
            low = mid_low[xs].reshape(16 * KEPT, 256)
            value = jnp.dot(high, right, preferred_element_type=f32)
            rest = jnp.dot(low, right[:, 0:128], preferred_element_type=f32)
            value = value[:, 0:128] + (value[:, 128:256] + rest)
            other = pltpu.roll(value, WIN, 1)
            if e == 0:
                lane = lax.broadcasted_iota(jnp.int32, value.shape, 1)
                other = jnp.where(lane < WIN, value - other, other - value)
            else:
                other = value + other
            value = jnp.concatenate([value, other], axis=1)
            store(i * 16, value.reshape(16, KEPT, 256))
            return 0

        lax.fori_loop(0, WIN // 16, turn_z, 0)

    def first(w, _):
        def store(x, value):
            spec0[w, pl.ds(x, 16)] = value

        transform(w, 0, store)
        return 0

    def second(w, _):
        def store(x, value):
            spec1[pl.ds(x + half, 16)] = value

        transform(w, 1, store)

        def sums(x, carry):
            return carry[0] + spec0[w, x, 0:8, :], carry[1] + spec1[x + half, 0:8, :]

        mean0, mean1 = lax.fori_loop(
            0, WIN, sums, (jnp.zeros((8, 256), f32), jnp.zeros((8, 256), f32)), unroll=4
        )
        lane = lax.broadcasted_iota(jnp.int32, (8, 256), 1)
        row = lax.broadcasted_iota(jnp.int32, (8, 256), 0)
        still = (row == 0) & ((lane == 0) | (lane == 128) | (lane == 192))
        mean0 = jnp.where(still, mean0 * (1.0 / WIN), 0.0)
        mean1 = jnp.where(still, mean1 * (1.0 / WIN), 0.0)

        def centre(x, carry):
            spec0[w, x, 0:8, :] = spec0[w, x, 0:8, :] - mean0
            spec1[x + half, 0:8, :] = spec1[x + half, 0:8, :] - mean1
            value0, value1 = spec0[w, x, :, 0:128], spec1[x + half, :, 0:128]
            return carry[0] + value0 * value0, carry[1] + value1 * value1

        zero = jnp.zeros((KEPT, 128), f32)
        power0, power1 = lax.fori_loop(0, WIN, centre, (zero, zero), unroll=2)
        count = 1.0 / (WIN * WIN * WIN**3)
        rms0 = jnp.sqrt(whole(power0 * weight_ref[...], jnp.sum) * count + 1e-6)
        rms1 = jnp.sqrt(whole(power1 * weight_ref[...], jnp.sum) * count + 1e-6)
        spec1[0:half] = spec1[WIN : WIN + half]
        spec1[WIN + half : WIN + DISP] = spec1[half:DISP]
        lower = lax.broadcasted_iota(jnp.int32, (KEPT, 128), 1) < WIN

        def pair(x, _):
            spec1[x, :, 128:256] = jnp.where(lower, spec1[x, :, 128:256], spec1[x + 1, :, 128:256])
            return 0

        lax.fori_loop(0, WIN + DISP - 2, pair, 0, unroll=2)

        def group(g, _):
            first = lax.div(g, KEPT // 8) * half
            rows = pl.ds(pl.multiple_of((g - lax.div(g, KEPT // 8) * (KEPT // 8)) * 8, 8), 8)

            def block(i, carry):
                carry = list(carry)
                base = i * 4
                ones = [spec0[w, base + j, rows, 0:128] for j in range(4)]
                sums = [spec0[w, base + j, rows, 128:256] for j in range(4)]
                plain = [spec1[base + first + j, rows, 0:128] for j in range(half + 3)]
                paired = [spec1[base + first + j, rows, 128:256] for j in range(half + 2)]
                for j in range(4):
                    for s in range(half):
                        carry[s] = carry[s] + ones[j] * plain[j + s]
                    for s in range(0, half, 2):
                        carry[half + s // 2] = carry[half + s // 2] + sums[j] * paired[j + s]
                return tuple(carry)

            zero = jnp.zeros((8, 128), f32)
            done = lax.fori_loop(0, WIN // 4, block, (zero,) * (half + half // 2))
            for s in range(half):
                corr_ref[first + s, rows, 0:128] = done[s]
                corr_ref[first + s, rows, 128:256] = done[half + s // 2]
            return 0

        lax.fori_loop(0, 2 * (KEPT // 8), group, 0)

        highest = lax.Precision.HIGHEST
        turned = []
        for s in range(DISP):
            value = jnp.dot(
                inv_left_ref[...], corr_ref[s], precision=highest, preferred_element_type=f32
            )
            turned.append(jnp.concatenate([value[0:DISP], value[DISP : 2 * DISP]], axis=1))
        sides = [
            jnp.dot(
                jnp.concatenate(turned[side::2], axis=0), inv_right_ref[side],
                precision=highest, preferred_element_type=f32,
            )
            for side in range(2)
        ]
        final = jnp.concatenate(
            [sides[s % 2][s // 2 * DISP : (s // 2 + 1) * DISP] for s in range(DISP)], axis=0
        )
        scale = 1.0 / (WIN * WIN * WIN**1.5)
        final = (final * (scale / (rms0 * rms1))).reshape(DISP * DISP // 8, 8, 128)
        lane = lax.broadcasted_iota(jnp.int32, final.shape, 2)
        row = lax.broadcasted_iota(jnp.int32, final.shape, 1)
        own = (lane >= row * DISP) & (lane < row * DISP + DISP)
        final = jnp.sum(jnp.where(own, final, 0.0), axis=1)
        res_ref[w] = final
        return 0

    return first, second


def piv_kernel(
    win_x_ref, win_y_ref, win_z_ref, init_ref, img_ref, turned_ref, blocks_ref, ids_ref, marks_ref,
    left_ref, right_ref, inv_left_ref, inv_right_ref, weight_ref,
    vol_ref, out_ref,
    fwd_ref, bwd_ref, lib_ref, gather_ref, spread_ref,
    cols_ref, part_ref, recv_ref, ratio_ref,
    code_ref, high_ref, low_ref, mid_high, mid_low, spec0, spec1, corr_ref, res_ref,
    part_send, part_recv, ratio_send, ratio_recv, send_own, send_on, arrive,
):
    count, depth = lax.axis_size("wide"), lax.axis_size("narrow")
    me, row = lax.axis_index("wide"), lax.axis_index("narrow")
    barrier = pltpu.get_barrier_semaphore()

    def greet(d, _):
        pl.semaphore_signal(
            barrier, inc=1, device_id={"wide": wrapped(me + d, count)}, device_id_type=MESH
        )
        return 0

    lax.fori_loop(1, count, greet, 0)
    for by in (1, depth - 1):
        pl.semaphore_signal(
            barrier, inc=1, device_id={"narrow": wrapped(row + by, depth)}, device_id_type=MESH
        )

    def barrier_done():
        pl.semaphore_wait(barrier, count + 1)

    prepare(
        turned_ref, blocks_ref, ids_ref, marks_ref,
        fwd_ref, bwd_ref, lib_ref, gather_ref, spread_ref,
    )
    stats = {}
    encode, send_rows, send_sides, pass_on, settle, place_own, receive = exchange(
        vol_ref, code_ref, high_ref, low_ref, send_own, send_on, arrive, stats
    )

    def finish(e, least, largest, total):
        stats[e] = total * (1.0 / (vol_ref.shape[1] * 128))
        encode(e, least, largest)
        if e == 0:
            send_sides(e)
        send_rows(e)

    reconstruct(
        (init_ref, img_ref, fwd_ref, bwd_ref, lib_ref, gather_ref, spread_ref, vol_ref),
        (cols_ref, part_ref, recv_ref, ratio_ref, part_send, part_recv, ratio_send, ratio_recv),
        barrier_done,
        finish,
    )
    place_own(0)
    pass_on(0)
    send_sides(1)
    place_own(1)
    for i, j in ((-1, 0), (1, 0), (0, -1), (0, 1)):
        receive(0, i, j)
    pass_on(1)
    for i, j in ((-1, -1), (-1, 1), (1, -1), (1, 1)):
        receive(0, i, j)
    first, second = windows(
        (win_x_ref, win_y_ref, win_z_ref),
        (left_ref, right_ref, inv_left_ref, inv_right_ref, weight_ref),
        high_ref, low_ref, (mid_high, mid_low), (spec0, spec1), corr_ref, res_ref,
    )
    lax.fori_loop(0, spec0.shape[0], first, 0)
    for i, j in ((-1, 0), (1, 0), (0, -1), (0, 1), (-1, -1), (-1, 1), (1, -1), (1, 1)):
        receive(1, i, j)
    for e in range(2):
        settle(e)
    lax.fori_loop(0, spec0.shape[0], second, 0)
    for w in range(out_ref.shape[0]):
        for s in range(res_ref.shape[1]):
            out_ref[w : w + 1, s * 128 : (s + 1) * 128] = res_ref[w, s : s + 1]


def body(initial, images, blocks, lib_index, tile_map, win_x, win_y, win_z):
    count = lax.axis_size("wide")
    f32, bf16 = jnp.float32, jnp.bfloat16
    cams, members = blocks.shape[0], blocks.shape[1]
    columns = initial.shape[1] * initial.shape[2]
    windows_count = win_x.size
    marks = (tile_map + 512 * lib_index).reshape(cams, columns)
    vmem = pl.BlockSpec(memory_space=pltpu.VMEM)
    wide_x, wide_y = 3 * BRICK, 3 * BRICK
    volume, correlation = pl.pallas_call(
        piv_kernel,
        out_shape=(
            jax.ShapeDtypeStruct((2, columns, 128), f32),
            jax.ShapeDtypeStruct((windows_count, DISP * DISP * DISP), f32),
        ),
        in_specs=[pl.BlockSpec(memory_space=pltpu.SMEM)] * 3 + [vmem] * 11,
        out_specs=(vmem, vmem),
        scratch_shapes=[
            pltpu.VMEM((cams, 256, members * 64), bf16),
            pltpu.VMEM((cams, 256, members * 64), bf16),
            pltpu.VMEM((cams, columns, 128), bf16),
            pltpu.VMEM((cams, count * PROJ_ROWS, columns), bf16),
            pltpu.VMEM((cams, columns, count * RATIO_ROWS), bf16),
            pltpu.VMEM((2, columns, 256), bf16),
            pltpu.VMEM((2, count, TILES, 128), f32),
            pltpu.VMEM((2, count, TILES, 128), f32),
            pltpu.VMEM((2, count * RATIO_ROWS, 128), bf16),
            pltpu.VMEM((3, 3, 2, columns + MARK, 128), jnp.int16),
            pltpu.VMEM((2, wide_x, wide_y, 128), bf16),
            pltpu.VMEM((2, wide_x, wide_y, 128), bf16),
            pltpu.VMEM((WIN, KEPT, 256), bf16),
            pltpu.VMEM((WIN, KEPT, 256), bf16),
            pltpu.VMEM((windows_count, WIN, KEPT, 256), f32),
            pltpu.VMEM((WIN + DISP, KEPT, 256), f32),
            pltpu.VMEM((DISP, KEPT, 256), f32),
            pltpu.VMEM((windows_count, DISP * DISP * DISP // 128, 128), f32),
            pltpu.SemaphoreType.DMA((2,)),
            pltpu.SemaphoreType.DMA((2,)),
            pltpu.SemaphoreType.DMA((2,)),
            pltpu.SemaphoreType.DMA((2,)),
            pltpu.SemaphoreType.DMA((2, 2, 2)),
            pltpu.SemaphoreType.DMA((2, 2, 2)),
            pltpu.SemaphoreType.DMA((3, 3, 2)),
        ],
        compiler_params=pltpu.CompilerParams(
            collective_id=0, has_side_effects=True, vmem_limit_bytes=60 * 1024 * 1024
        ),
        name="piv",
    )(
        win_x.reshape(-1),
        win_y.reshape(-1),
        win_z.reshape(-1),
        initial.reshape(2, columns, 128),
        images,
        blocks.transpose(0, 1, 3, 2),
        blocks,
        marks,
        jnp.broadcast_to(marks[:, :, None], (cams, columns, 128)),
        *[jnp.asarray(table) for table in window_tables()],
    )
    return (
        volume.reshape(initial.shape),
        correlation.reshape(1, 1, windows_count, DISP * DISP * DISP),
    )


def solution(mesh):
    placed = (
        P(None, "wide", "narrow", None),
        P(None, None, "wide", "narrow", None),
        P(),
        P(None, "wide", "narrow"),
        P(None, "wide", "narrow"),
        P("wide", "narrow", None),
        P("wide", "narrow", None),
        P("wide", "narrow", None),
    )
    return jax.shard_map(
        body,
        mesh=mesh,
        in_specs=placed,
        out_specs=(P(None, "wide", "narrow", None), P("wide", "narrow", None, None)),
        check_vma=False,
    )
```

```python
import jax
import jax.numpy as jnp
import ml_dtypes
import numpy as np
from jax import lax
from jax.experimental import pallas as pl
from jax.experimental.pallas import tpu as pltpu
from jax.sharding import PartitionSpec as P

MESH = pl.DeviceIdType.MESH
PROJ_ROWS = 24
RATIO_ROWS = 32
CHUNK = 256
WIN = 64
DISP = 16
SWEEPS = 2
SPAN = 80
KEPT = 40
BRICK = 32
MARK = 16
STEPS = 65000.0
TILES = 18


def split(values):
    high = values.astype(jnp.bfloat16)
    return high, (values - high.astype(jnp.float32)).astype(jnp.bfloat16)


def window_tables():
    bf16 = ml_dtypes.bfloat16
    turn = 2.0 * np.pi / WIN

    def parts(table):
        high = table.astype(bf16)
        return high, (table - high.astype(np.float64)).astype(bf16)

    waves = np.arange(WIN // 2 + 1)
    angle = turn * (waves[:, None] * np.arange(SPAN)[None, :] % WIN)
    left = np.zeros((2 * KEPT, SPAN))
    left[: len(waves)] = np.cos(angle)
    left[KEPT : KEPT + len(waves)] = -np.sin(angle)
    left_high, left_low = parts(left)
    left_table = np.zeros((2 * KEPT, 256), bf16)
    for place, table in enumerate((left_high, left_high, left_low)):
        left_table[:, place * SPAN : (place + 1) * SPAN] = table

    angle = turn * (np.arange(128)[:, None] * np.arange(WIN)[None, :] % WIN)
    cosine, sine = np.cos(angle), np.sin(angle)
    right = np.block([[cosine, -sine], [sine, cosine]])
    right_table = np.concatenate(parts(right), axis=1)

    shifts = np.arange(DISP) - DISP // 2
    weight = np.where(waves % (WIN // 2) == 0, 1.0, 2.0)
    angle = turn * shifts[:, None] * waves[None, :]
    inverse_left = np.zeros((2 * DISP, KEPT))
    inverse_left[:DISP, : len(waves)] = weight * np.cos(angle)
    inverse_left[DISP:, : len(waves)] = weight * np.sin(angle)
    angle = turn * np.arange(WIN)[:, None] * shifts[None, :]
    cosine, sine = np.cos(angle), np.sin(angle)
    inverse_right = np.stack([
        np.tile(
            np.concatenate([
                cosine + sine, cosine - sine, even * -sine, odd * -sine,
                cosine - sine, -sine - cosine, even * -cosine, odd * -cosine,
            ]) + 0.0,
            (1, 128 // DISP),
        )
        for even, odd in ((1, 0), (0, 1))
    ])
    row_weight = np.zeros((KEPT, 128))
    row_weight[: len(waves)] = weight[:, None]
    f32 = np.float32
    return (
        left_table, right_table,
        inverse_left.astype(f32), inverse_right.astype(f32), row_weight.astype(f32),
    )


def wrapped(index, count):
    return jnp.where(index >= count, index - count, index)


def whole(values, reduce):
    return reduce(reduce(values, axis=0, keepdims=True), axis=1, keepdims=True)


def chunks(rows, action, unroll):
    def step(i, carry):
        return action(pl.ds(pl.multiple_of(i * CHUNK, CHUNK), CHUNK), carry)

    return lambda init: lax.fori_loop(0, rows // CHUNK, step, init, unroll=unroll)


def prepare(
    img_ref, blocks_ref, ids_ref, marks_ref, logs_ref, fwd_ref, bwd_ref, lib_ref, gather_ref,
    spread_ref,
):
    f32, bf16 = jnp.float32, jnp.bfloat16
    count = lax.axis_size("wide")
    me = lax.axis_index("wide")
    cams, members = blocks_ref.shape[0], blocks_ref.shape[1]
    columns = lib_ref.shape[1]

    def strip_rows(ids, stride):
        slot = jnp.floor((ids + 0.5) * (1.0 / TILES))
        owner = slot + (me - count // 2).astype(f32)
        inside = (owner >= 0.0) & (owner < count)
        return jnp.where(inside, owner * stride + (ids - slot * TILES), -1.0)

    def camera(cam):
        for m in range(members):
            rows = slice(m % 2 * 128, m % 2 * 128 + 128)
            lanes = slice(m // 2 * 128, m // 2 * 128 + 128)
            fwd_ref[cam, rows, lanes] = blocks_ref[cam, m].astype(f32).T.astype(bf16)
            bwd_ref[cam, rows, lanes] = blocks_ref[cam, m]
        mark = ids_ref[cam : cam + 1, :].astype(f32)
        ids = strip_rows(mark - jnp.floor(mark * (1.0 / 512.0)) * 512.0, PROJ_ROWS)

        def gather(i, _):
            rows = pl.ds(pl.multiple_of(i * 32, 32), 32)
            row = lax.broadcasted_iota(jnp.int32, (32, columns), 0) + i * 32
            gather_ref[cam, rows, :] = jnp.where(row.astype(f32) == ids, 1.0, 0.0).astype(bf16)
            return 0

        lax.fori_loop(0, count * PROJ_ROWS // 32, gather, 0)

        def spread(i, _):
            rows = pl.ds(pl.multiple_of(i * 64, 64), 64)
            mark = marks_ref[cam, rows, :].astype(f32)
            lib = jnp.floor(mark * (1.0 / 512.0))
            lib_ref[cam, rows, :] = lib.astype(bf16)
            ids = strip_rows(mark - lib * 512.0, RATIO_ROWS)
            lane = lax.broadcasted_iota(jnp.int32, (64, 128), 1).astype(f32)
            for part in range(count * RATIO_ROWS // 128):
                here = jnp.where(lane + part * 128.0 == ids, 1.0, 0.0)
                spread_ref[cam, rows, part * 128 : (part + 1) * 128] = here.astype(bf16)
            return 0

        lax.fori_loop(0, columns // 64, spread, 0)

    def pictures():
        for e in range(2):
            for i in range(img_ref.shape[1]):
                for j in range(img_ref.shape[2]):
                    tile = jnp.log(img_ref[e, i, j] + 1.0)
                    at = i * img_ref.shape[2] + j
                    for cam in range(cams):
                        logs_ref[e, cam, at : at + 1, :] = tile[cam : cam + 1]

    def rest():
        pictures()
        for cam in range(1, cams):
            camera(cam)

    camera(0)
    return rest


def reconstruct(refs, scratch, barrier_done, meanwhile, finish):
    init_ref, logs_ref, fwd_ref, bwd_ref, lib_ref, gather_ref, spread_ref, vol_ref = refs
    cols_ref, part_ref, recv_ref, ratio_ref = scratch[:4]
    part_send, part_recv, ratio_send, ratio_recv = scratch[4:]
    f32, bf16 = jnp.float32, jnp.bfloat16
    count = lax.axis_size("wide")
    me = lax.axis_index("wide")
    cams = fwd_ref.shape[0]
    columns = init_ref.shape[1]

    def by_library(values, cam, rows, table):
        lib = lib_ref[cam, rows, :]
        zero = jnp.zeros_like(values)
        odd = (lib == 1) | (lib == 3) | (lib == 5) | (lib == 7)
        lhs = jnp.concatenate(
            [jnp.where(odd, zero, values), jnp.where(odd, values, zero)], axis=1
        )
        wide = jnp.dot(lhs, table, preferred_element_type=f32)
        pair = lib.astype(f32)
        low = jnp.where(pair < 2, wide[:, 0:128], wide[:, 128:256])
        high = jnp.where(pair < 6, wide[:, 256:384], wide[:, 384:512])
        return jnp.where(pair < 4, low, high)

    def project_rows(e, cam, rows, vol):
        proj = by_library(vol.astype(bf16), cam, rows, fwd_ref[cam])
        high, low = split(proj)
        cols_ref[e, rows, 0:128] = high
        cols_ref[e, rows, 128:256] = low

    def part_copy(e, d, owner):
        target = wrapped(me + d, count)
        return pltpu.make_async_remote_copy(
            src_ref=part_ref.at[e, target],
            dst_ref=recv_ref.at[e, owner],
            send_sem=part_send.at[e],
            recv_sem=part_recv.at[e],
            device_id={"wide": target},
            device_id_type=MESH,
        )

    def strip(e, owner):
        return ratio_ref.at[e, pl.ds(pl.multiple_of(owner * RATIO_ROWS, RATIO_ROWS), RATIO_ROWS)]

    def ratio_copy(e, d, owner):
        return pltpu.make_async_remote_copy(
            src_ref=strip(e, me),
            dst_ref=strip(e, owner),
            send_sem=ratio_send.at[e],
            recv_sem=ratio_recv.at[e],
            device_id={"wide": wrapped(me + d, count)},
            device_id_type=MESH,
        )

    def parts_done(e, sem):
        slots = recv_ref.at[e, pl.ds(0, count - 1)]
        pltpu.make_async_copy(slots, slots, sem.at[e]).wait()

    def ratios_done(e, sem):
        strips = ratio_ref.at[e, pl.ds(0, (count - 1) * RATIO_ROWS)]
        pltpu.make_async_copy(strips, strips, sem.at[e]).wait()

    far_first = sorted(range(1, count), key=lambda d: -(2 - abs(d % 4 - 2)) - (2 - abs(d // 4 - 2)))

    def send_parts(e, cam):
        both = jnp.dot(gather_ref[cam], cols_ref[e], preferred_element_type=f32)
        total = both[:, 0:128] + both[:, 128:256]
        part_ref[e] = total.reshape(count, PROJ_ROWS, 128)[:, 0 : part_ref.shape[2]]
        for d in far_first:
            part_copy(e, d, me).start()

    def send_ratio(e, cam):
        def take(d, total):
            return total + recv_ref[e, wrapped(me + d, count)]

        parts_done(e, part_recv)
        total = lax.fori_loop(1, count, take, part_ref[e, me], unroll=True)
        tiles = logs_ref.shape[2]
        ratio = logs_ref[e, cam] - jnp.log(total + 1.0)
        ratio = jnp.concatenate([ratio, jnp.zeros((RATIO_ROWS - tiles, 128), f32)], axis=0)
        ratio_ref[e, pl.ds(pl.multiple_of(me * RATIO_ROWS, RATIO_ROWS), RATIO_ROWS), :] = (
            ratio.astype(bf16)
        )
        for d in far_first:
            ratio_copy(e, d, me).start()

    def collect_ratio(e):
        ratios_done(e, ratio_recv)
        parts_done(e, part_send)
        ratios_done(e, ratio_send)

    def updated_rows(e, cam, rows):
        near = jnp.dot(spread_ref[cam, rows, :], ratio_ref[e], preferred_element_type=f32)
        back = by_library(near.astype(bf16), cam, rows, bwd_ref[cam])
        return vol_ref[e, rows, :] * jnp.exp(back)

    for e in range(2):
        def first(rows, _):
            vol = init_ref[e, rows, :]
            vol_ref[e, rows, :] = vol
            project_rows(e, 0, rows, vol)
            return 0

        chunks(columns, first, 2)(0)
        if e == 0:
            barrier_done()
        send_parts(e, 0)

    meanwhile()

    def round_step(r, _):
        cam = lax.rem(r, cams)
        following = lax.rem(r + 1, cams)
        for e in range(2):
            send_ratio(e, cam)
        for e in range(2):
            collect_ratio(e)

            def both(rows, _):
                vol = updated_rows(e, cam, rows)
                vol_ref[e, rows, :] = vol
                project_rows(e, following, rows, vol)
                return 0

            chunks(columns, both, 4)(0)
            send_parts(e, following)
        return 0

    lax.fori_loop(0, SWEEPS * cams - 1, round_step, 0)
    for e in range(2):
        send_ratio(e, cams - 1)
    for e in range(2):
        collect_ratio(e)

        def final(rows, carry):
            vol = updated_rows(e, cams - 1, rows)
            vol_ref[e, rows, :] = vol
            tiles = vol.reshape(CHUNK // 8, 8, 128)
            return (
                jnp.minimum(carry[0], jnp.min(tiles, axis=0)),
                jnp.maximum(carry[1], jnp.max(tiles, axis=0)),
                carry[2] + jnp.sum(tiles, axis=0),
            )

        low = jnp.full((8, 128), 3.0e38, f32)
        least, largest, total = chunks(columns, final, 2)((low, -low, jnp.zeros((8, 128), f32)))
        finish(e, whole(least, jnp.min), whole(largest, jnp.max), whole(total, jnp.sum))


def exchange(vol_ref, code_ref, high_ref, low_ref, send_own, send_on, arrive, stats):
    f32 = jnp.float32
    wide, narrow = lax.axis_size("wide"), lax.axis_size("narrow")
    me, row = lax.axis_index("wide"), lax.axis_index("narrow")
    columns = vol_ref.shape[1]
    has_wide = {-1: me > 0, 1: me < wide - 1}
    has_narrow = {-1: row > 0, 1: row < narrow - 1}

    def encode(e, least, largest):
        base = jnp.floor(jnp.log(least) * 64.0)
        extent = jnp.floor(jnp.log(largest) * 64.0) - base + 2.0
        scale = (64.0 * STEPS) / extent
        shift = base * (1.0 / 64.0)

        def step(rows, _):
            level = (jnp.log(vol_ref[e, rows, :]) - shift) * scale
            code_ref[1, 1, e, rows, :] = (
                jnp.round(level - STEPS / 2).astype(jnp.int32).astype(jnp.int16)
            )
            return 0

        chunks(columns, step, 1)(0)
        mark = jnp.where(lax.broadcasted_iota(jnp.int32, (MARK, 128), 0) < 8, base, extent)
        code_ref[1, 1, e, columns : columns + MARK, :] = mark.astype(jnp.int32).astype(jnp.int16)

    def side_copy(e, by, place):
        return pltpu.make_async_remote_copy(
            src_ref=code_ref.at[1, 1, e],
            dst_ref=code_ref.at[1 + place, 1, e],
            send_sem=send_own.at[0, (by + 1) // 2, e],
            recv_sem=arrive.at[1 + place, 1, e],
            device_id={"wide": me + by},
            device_id_type=MESH,
        )

    def row_copy(e, column, by, place):
        sem = send_own.at[1, (by + 1) // 2, e]
        if column != 0:
            sem = send_on.at[(column + 1) // 2, (by + 1) // 2, e]
        return pltpu.make_async_remote_copy(
            src_ref=code_ref.at[1 + column, 1, e],
            dst_ref=code_ref.at[1 + column, 1 + place, e],
            send_sem=sem,
            recv_sem=arrive.at[1 + column, 1 + place, e],
            device_id={"narrow": row + by},
            device_id_type=MESH,
        )

    def send_rows(e):
        for by in (-1, 1):
            @pl.when(has_narrow[by])
            def _():
                row_copy(e, 0, by, -by).start()

    def send_sides(e):
        for by in (-1, 1):
            @pl.when(has_wide[by])
            def _():
                side_copy(e, by, -by).start()

    def pass_on(e):
        for side in (-1, 1):
            @pl.when(has_wide[side])
            def _():
                side_copy(e, side, side).wait_recv()
                for by in (-1, 1):
                    @pl.when(has_narrow[by])
                    def _():
                        row_copy(e, side, by, -by).start()

    def settle(e):
        for by in (-1, 1):
            @pl.when(has_narrow[by])
            def _():
                row_copy(e, 0, by, -by).wait_send()

            @pl.when(has_wide[by])
            def _():
                side_copy(e, by, -by).wait_send()
                for up in (-1, 1):
                    @pl.when(has_narrow[up])
                    def _():
                        row_copy(e, by, up, -up).wait_send()

    def place(e, i, j, values_of):
        def step(x, _):
            high, low = split(values_of(x))
            high_ref[e, (1 + i) * BRICK + x, (1 + j) * BRICK : (2 + j) * BRICK, :] = high
            low_ref[e, (1 + i) * BRICK + x, (1 + j) * BRICK : (2 + j) * BRICK, :] = low
            return 0

        lax.fori_loop(0, BRICK, step, 0, unroll=4)

    def place_own(e):
        place(e, 0, 0, lambda x: vol_ref[
            e, pl.ds(pl.multiple_of(x * BRICK, BRICK), BRICK), :] - stats[e])

    def place_code(e, i, j):
        mark = code_ref[1 + i, 1 + j, e, columns : columns + MARK, :].astype(f32)
        step = mark[8:9] * (1.0 / (64.0 * STEPS))
        shift = mark[0:1] * (1.0 / 64.0) + step * (STEPS / 2)

        def values_of(x):
            rows = pl.ds(pl.multiple_of(x * BRICK, BRICK), BRICK)
            code = code_ref[1 + i, 1 + j, e, rows, :].astype(f32)
            return jnp.exp(code * step + shift) - stats[e]

        place(e, i, j, values_of)

    def receive(e, i, j):
        here = has_narrow[j] if j else None
        if i:
            here = has_wide[i] if here is None else here & has_wide[i]

        @pl.when(here)
        def _():
            if j:
                row_copy(e, i, j, j).wait_recv()
            place_code(e, i, j)

        @pl.when(jnp.logical_not(here))
        def _():
            place(e, i, j, lambda x: jnp.zeros((BRICK, 128), f32) - stats[e])

    return encode, send_rows, send_sides, pass_on, settle, place_own, receive


def windows(place_ref, tables, high_ref, low_ref, mids, specs, corr_ref, res_ref):
    left_ref, right_ref, inv_left_ref, inv_right_ref, weight_ref = tables
    mid_high, mid_low = mids
    spec0, spec1 = specs
    f32, bf16 = jnp.float32, jnp.bfloat16
    half = DISP // 2
    wide_y = high_ref.shape[2]

    def transform(w, e, store):
        start_x, start_y, start_z = place_ref[0][w], place_ref[1][w], place_ref[2][w]
        lead = jnp.where(start_y >= 16, start_y - 16, start_y)
        later = lax.broadcasted_iota(jnp.int32, (SPAN, 128), 0) * 0 + start_y >= 16
        lane = lax.broadcasted_iota(jnp.int32, (2 * KEPT, 256), 1)
        spot = lax.rem(lane, SPAN)
        keep = (spot >= lead) & (spot < lead + WIN) & (lane < 3 * SPAN)
        left = jnp.where(keep, left_ref[...].astype(f32), 0.0).astype(bf16)
        row = lax.rem(lax.broadcasted_iota(jnp.int32, (256, 256), 0), 128)
        keep = (row >= start_z) & (row < start_z + WIN)
        right = jnp.where(keep, right_ref[...].astype(f32), 0.0).astype(bf16)

        def turn_y(i, _):
            sides = []
            for j in range(2):
                high, low = high_ref[e, start_x + 2 * i + j], low_ref[e, start_x + 2 * i + j]
                high = jnp.where(later, high[wide_y - SPAN :], high[:SPAN])
                low = jnp.where(later, low[wide_y - SPAN :], low[:SPAN])
                sides.append(jnp.concatenate([high, low, high, high[0:16]], axis=0))
            mixed = jnp.dot(left, jnp.concatenate(sides, axis=1), preferred_element_type=f32)
            high, low = split(mixed)
            for j in range(2):
                lanes = slice(j * 128, (j + 1) * 128)
                for source, target in ((high, mid_high), (low, mid_low)):
                    target[2 * i + j, :, 0:128] = source[0:KEPT, lanes]
                    target[2 * i + j, :, 128:256] = source[KEPT : 2 * KEPT, lanes]
            return 0

        lax.fori_loop(0, WIN // 2, turn_y, 0, unroll=4)

        def turn_z(i, _):
            xs = pl.ds(i * 16, 16)
            high = mid_high[xs].reshape(16 * KEPT, 256)
            low = mid_low[xs].reshape(16 * KEPT, 256)
            value = jnp.dot(high, right, preferred_element_type=f32)
            rest = jnp.dot(low, right[:, 0:128], preferred_element_type=f32)
            value = value[:, 0:128] + (value[:, 128:256] + rest)
            other = pltpu.roll(value, WIN, 1)
            if e == 0:
                lane = lax.broadcasted_iota(jnp.int32, value.shape, 1)
                other = jnp.where(lane < WIN, value - other, other - value)
            else:
                other = value + other
            value = jnp.concatenate([value, other], axis=1)
            store(i * 16, value.reshape(16, KEPT, 256))
            return 0

        lax.fori_loop(0, WIN // 16, turn_z, 0)

    def first(w, _):
        def store(x, value):
            spec0[w, pl.ds(x, 16)] = value

        transform(w, 0, store)
        return 0

    def second(w, _):
        def store(x, value):
            spec1[pl.ds(x + half, 16)] = value

        transform(w, 1, store)

        def sums(x, carry):
            return carry[0] + spec0[w, x, 0:8, :], carry[1] + spec1[x + half, 0:8, :]

        mean0, mean1 = lax.fori_loop(
            0, WIN, sums, (jnp.zeros((8, 256), f32), jnp.zeros((8, 256), f32)), unroll=4
        )
        lane = lax.broadcasted_iota(jnp.int32, (8, 256), 1)
        row = lax.broadcasted_iota(jnp.int32, (8, 256), 0)
        still = (row == 0) & ((lane == 0) | (lane == 128) | (lane == 192))
        mean0 = jnp.where(still, mean0 * (1.0 / WIN), 0.0)
        mean1 = jnp.where(still, mean1 * (1.0 / WIN), 0.0)

        def centre(x, carry):
            spec0[w, x, 0:8, :] = spec0[w, x, 0:8, :] - mean0
            spec1[x + half, 0:8, :] = spec1[x + half, 0:8, :] - mean1
            value0, value1 = spec0[w, x, :, 0:128], spec1[x + half, :, 0:128]
            return carry[0] + value0 * value0, carry[1] + value1 * value1

        zero = jnp.zeros((KEPT, 128), f32)
        power0, power1 = lax.fori_loop(0, WIN, centre, (zero, zero), unroll=2)
        count = 1.0 / (WIN * WIN * WIN**3)
        rms0 = jnp.sqrt(whole(power0 * weight_ref[...], jnp.sum) * count + 1e-6)
        rms1 = jnp.sqrt(whole(power1 * weight_ref[...], jnp.sum) * count + 1e-6)
        spec1[0:half] = spec1[WIN : WIN + half]
        spec1[WIN + half : WIN + DISP] = spec1[half:DISP]
        lower = lax.broadcasted_iota(jnp.int32, (KEPT, 128), 1) < WIN

        def pair(x, _):
            spec1[x, :, 128:256] = jnp.where(lower, spec1[x, :, 128:256], spec1[x + 1, :, 128:256])
            return 0

        lax.fori_loop(0, WIN + DISP - 2, pair, 0, unroll=2)

        def group(g, _):
            first = lax.div(g, KEPT // 8) * half
            rows = pl.ds(pl.multiple_of((g - lax.div(g, KEPT // 8) * (KEPT // 8)) * 8, 8), 8)

            def block(i, carry):
                carry = list(carry)
                base = i * 4
                ones = [spec0[w, base + j, rows, 0:128] for j in range(4)]
                sums = [spec0[w, base + j, rows, 128:256] for j in range(4)]
                plain = [spec1[base + first + j, rows, 0:128] for j in range(half + 3)]
                paired = [spec1[base + first + j, rows, 128:256] for j in range(half + 2)]
                for j in range(4):
                    for s in range(half):
                        carry[s] = carry[s] + ones[j] * plain[j + s]
                    for s in range(0, half, 2):
                        carry[half + s // 2] = carry[half + s // 2] + sums[j] * paired[j + s]
                return tuple(carry)

            zero = jnp.zeros((8, 128), f32)
            done = lax.fori_loop(0, WIN // 4, block, (zero,) * (half + half // 2))
            for s in range(half):
                corr_ref[first + s, rows, 0:128] = done[s]
                corr_ref[first + s, rows, 128:256] = done[half + s // 2]
            return 0

        lax.fori_loop(0, 2 * (KEPT // 8), group, 0)

        highest = lax.Precision.HIGHEST
        turned = []
        for s in range(DISP):
            value = jnp.dot(
                inv_left_ref[...], corr_ref[s], precision=highest, preferred_element_type=f32
            )
            turned.append(jnp.concatenate([value[0:DISP], value[DISP : 2 * DISP]], axis=1))
        sides = [
            jnp.dot(
                jnp.concatenate(turned[side::2], axis=0), inv_right_ref[side],
                precision=highest, preferred_element_type=f32,
            )
            for side in range(2)
        ]
        final = jnp.concatenate(
            [sides[s % 2][s // 2 * DISP : (s // 2 + 1) * DISP] for s in range(DISP)], axis=0
        )
        scale = 1.0 / (WIN * WIN * WIN**1.5)
        final = (final * (scale / (rms0 * rms1))).reshape(DISP * DISP // 8, 8, 128)
        lane = lax.broadcasted_iota(jnp.int32, final.shape, 2)
        row = lax.broadcasted_iota(jnp.int32, final.shape, 1)
        own = (lane >= row * DISP) & (lane < row * DISP + DISP)
        final = jnp.sum(jnp.where(own, final, 0.0), axis=1)
        res_ref[w] = final
        return 0

    return first, second


def piv_kernel(
    win_x_ref, win_y_ref, win_z_ref, init_ref, img_ref, blocks_ref, ids_ref, marks_ref,
    left_ref, right_ref, inv_left_ref, inv_right_ref, weight_ref,
    vol_ref, out_ref,
    logs_ref, fwd_ref, bwd_ref, lib_ref, gather_ref, spread_ref,
    cols_ref, part_ref, recv_ref, ratio_ref,
    code_ref, high_ref, low_ref, mid_high, mid_low, spec0, spec1, corr_ref, res_ref,
    part_send, part_recv, ratio_send, ratio_recv, send_own, send_on, arrive,
):
    count, depth = lax.axis_size("wide"), lax.axis_size("narrow")
    me, row = lax.axis_index("wide"), lax.axis_index("narrow")
    barrier = pltpu.get_barrier_semaphore()

    def greet(d, _):
        pl.semaphore_signal(
            barrier, inc=1, device_id={"wide": wrapped(me + d, count)}, device_id_type=MESH
        )
        return 0

    lax.fori_loop(1, count, greet, 0)
    for by in (1, depth - 1):
        pl.semaphore_signal(
            barrier, inc=1, device_id={"narrow": wrapped(row + by, depth)}, device_id_type=MESH
        )

    def barrier_done():
        pl.semaphore_wait(barrier, count + 1)

    rest = prepare(
        img_ref, blocks_ref, ids_ref, marks_ref,
        logs_ref, fwd_ref, bwd_ref, lib_ref, gather_ref, spread_ref,
    )
    stats = {}
    encode, send_rows, send_sides, pass_on, settle, place_own, receive = exchange(
        vol_ref, code_ref, high_ref, low_ref, send_own, send_on, arrive, stats
    )

    def finish(e, least, largest, total):
        stats[e] = total * (1.0 / (vol_ref.shape[1] * 128))
        encode(e, least, largest)
        if e == 0:
            send_sides(e)
        send_rows(e)

    reconstruct(
        (init_ref, logs_ref, fwd_ref, bwd_ref, lib_ref, gather_ref, spread_ref, vol_ref),
        (cols_ref, part_ref, recv_ref, ratio_ref, part_send, part_recv, ratio_send, ratio_recv),
        barrier_done,
        rest,
        finish,
    )
    place_own(0)
    pass_on(0)
    send_sides(1)
    place_own(1)
    for i, j in ((-1, 0), (1, 0), (0, -1), (0, 1)):
        receive(0, i, j)
    pass_on(1)
    for i, j in ((-1, -1), (-1, 1), (1, -1), (1, 1)):
        receive(0, i, j)
    first, second = windows(
        (win_x_ref, win_y_ref, win_z_ref),
        (left_ref, right_ref, inv_left_ref, inv_right_ref, weight_ref),
        high_ref, low_ref, (mid_high, mid_low), (spec0, spec1), corr_ref, res_ref,
    )
    lax.fori_loop(0, spec0.shape[0], first, 0)
    for i, j in ((-1, 0), (1, 0), (0, -1), (0, 1), (-1, -1), (-1, 1), (1, -1), (1, 1)):
        receive(1, i, j)
    for e in range(2):
        settle(e)
    lax.fori_loop(0, spec0.shape[0], second, 0)
    for w in range(out_ref.shape[0]):
        for s in range(res_ref.shape[1]):
            out_ref[w : w + 1, s * 128 : (s + 1) * 128] = res_ref[w, s : s + 1]


def body(initial, images, blocks, lib_index, tile_map, win_x, win_y, win_z):
    count = lax.axis_size("wide")
    f32, bf16 = jnp.float32, jnp.bfloat16
    cams, members = blocks.shape[0], blocks.shape[1]
    columns = initial.shape[1] * initial.shape[2]
    windows_count = win_x.size
    marks = (tile_map + 512 * lib_index).reshape(cams, columns)
    vmem = pl.BlockSpec(memory_space=pltpu.VMEM)
    wide_x, wide_y = 3 * BRICK, 3 * BRICK
    volume, correlation = pl.pallas_call(
        piv_kernel,
        out_shape=(
            jax.ShapeDtypeStruct((2, columns, 128), f32),
            jax.ShapeDtypeStruct((windows_count, DISP * DISP * DISP), f32),
        ),
        in_specs=[pl.BlockSpec(memory_space=pltpu.SMEM)] * 3 + [vmem] * 10,
        out_specs=(vmem, vmem),
        scratch_shapes=[
            pltpu.VMEM((2, cams, TILES, 128), f32),
            pltpu.VMEM((cams, 256, members * 64), bf16),
            pltpu.VMEM((cams, 256, members * 64), bf16),
            pltpu.VMEM((cams, columns, 128), bf16),
            pltpu.VMEM((cams, count * PROJ_ROWS, columns), bf16),
            pltpu.VMEM((cams, columns, count * RATIO_ROWS), bf16),
            pltpu.VMEM((2, columns, 256), bf16),
            pltpu.VMEM((2, count, TILES, 128), f32),
            pltpu.VMEM((2, count, TILES, 128), f32),
            pltpu.VMEM((2, count * RATIO_ROWS, 128), bf16),
            pltpu.VMEM((3, 3, 2, columns + MARK, 128), jnp.int16),
            pltpu.VMEM((2, wide_x, wide_y, 128), bf16),
            pltpu.VMEM((2, wide_x, wide_y, 128), bf16),
            pltpu.VMEM((WIN, KEPT, 256), bf16),
            pltpu.VMEM((WIN, KEPT, 256), bf16),
            pltpu.VMEM((windows_count, WIN, KEPT, 256), f32),
            pltpu.VMEM((WIN + DISP, KEPT, 256), f32),
            pltpu.VMEM((DISP, KEPT, 256), f32),
            pltpu.VMEM((windows_count, DISP * DISP * DISP // 128, 128), f32),
            pltpu.SemaphoreType.DMA((2,)),
            pltpu.SemaphoreType.DMA((2,)),
            pltpu.SemaphoreType.DMA((2,)),
            pltpu.SemaphoreType.DMA((2,)),
            pltpu.SemaphoreType.DMA((2, 2, 2)),
            pltpu.SemaphoreType.DMA((2, 2, 2)),
            pltpu.SemaphoreType.DMA((3, 3, 2)),
        ],
        compiler_params=pltpu.CompilerParams(
            collective_id=0, has_side_effects=True, vmem_limit_bytes=60 * 1024 * 1024
        ),
        name="piv",
    )(
        win_x.reshape(-1),
        win_y.reshape(-1),
        win_z.reshape(-1),
        initial.reshape(2, columns, 128),
        images.transpose(0, 2, 3, 1, 4),
        blocks,
        marks,
        jnp.broadcast_to(marks[:, :, None], (cams, columns, 128)),
        *[jnp.asarray(table) for table in window_tables()],
    )
    return (
        volume.reshape(initial.shape),
        correlation.reshape(1, 1, windows_count, DISP * DISP * DISP),
    )


def solution(mesh):
    placed = (
        P(None, "wide", "narrow", None),
        P(None, None, "wide", "narrow", None),
        P(),
        P(None, "wide", "narrow"),
        P(None, "wide", "narrow"),
        P("wide", "narrow", None),
        P("wide", "narrow", None),
        P("wide", "narrow", None),
    )
    return jax.shard_map(
        body,
        mesh=mesh,
        in_specs=placed,
        out_specs=(P(None, "wide", "narrow", None), P("wide", "narrow", None, None)),
        check_vma=False,
    )
```
